32 devices in a mesh: dp: 8 (over z, x), seq: 4 (over y, core).
Axes of the slice: x: 2, y: 2, z: 4, core: 2. Of those that a mesh axis runs over, the one named last changes fastest.
Arguments:
- patches: bfloat16 [4, 8, 48, 1024], P(None, 'dp', None, 'seq'), may hold values from -6 to 6
- segments: int32 [4, 8, 1024], P(None, 'dp', 'seq'), may hold values from 0 to 4, as said below
- embed_in: float32 [48, 768], P(None, 'dp'), may hold values from -0.875 to 0.875
- pos_table: float32 [1024, 768], P(None, 'dp'), may hold values from -3 to 3
- attn_qkv: float32 [768, 2304], P('dp'), may hold values from -0.21875 to 0.21875
- attn_out: float32 [768, 768], P('dp'), may hold values from -0.875 to 0.875
- mlp_up: float32 [768, 3072], P('dp'), may hold values from -0.21875 to 0.21875
- mlp_down: float32 [3072, 768], P(None, 'dp'), may hold values from -0.109375 to 0.109375
- head_out: float32 [768, 96], P('dp'), may hold values from -0.109375 to 0.109375
- vectors: float32 [8, 768], P(None, 'dp'), may hold values from 0.5 to 1.5
- first_embed_in: float32 [48, 768], P(None, 'dp'), may hold values from -2.3841858e-06 to 2.3841858e-06
- first_pos_table: float32 [1024, 768], P(None, 'dp'), may hold values from -7.4505806e-08 to 7.4505806e-08
- first_attn_qkv: float32 [768, 2304], P('dp'), may hold values from -2.3841858e-06 to 2.3841858e-06
- first_attn_out: float32 [768, 768], P('dp'), may hold values from -2.3841858e-06 to 2.3841858e-06
- first_mlp_up: float32 [768, 3072], P('dp'), may hold values from -2.3841858e-06 to 2.3841858e-06
- first_mlp_down: float32 [3072, 768], P(None, 'dp'), may hold values from -2.3841858e-06 to 2.3841858e-06
- first_head_out: float32 [768, 96], P('dp'), may hold values from -2.3841858e-06 to 2.3841858e-06
- first_vectors: float32 [8, 768], P(None, 'dp'), may hold values from -9.536743e-06 to 9.536743e-06
- second_embed_in: float32 [48, 768], P(None, 'dp'), may hold values from 6.5906064e-13 to 2.6312307e-12
- second_pos_table: float32 [1024, 768], P(None, 'dp'), may hold values from 6.436139e-16 to 2.5695613e-15
- second_attn_qkv: float32 [768, 2304], P('dp'), may hold values from 6.5906064e-13 to 2.6312307e-12
- second_attn_out: float32 [768, 768], P('dp'), may hold values from 6.5906064e-13 to 2.6312307e-12
- second_mlp_up: float32 [768, 3072], P('dp'), may hold values from 6.5906064e-13 to 2.6312307e-12
- second_mlp_down: float32 [3072, 768], P(None, 'dp'), may hold values from 6.5906064e-13 to 2.6312307e-12
- second_head_out: float32 [768, 96], P('dp'), may hold values from 6.5906064e-13 to 2.6312307e-12
- second_vectors: float32 [8, 768], P(None, 'dp'), may hold values from 1.054497e-11 to 4.2099692e-11
Outputs:
- loss_bits: float32 [], replicated
- valid_dims: float32 [], replicated
- grad_norm: float32 [], replicated
- new_embed_in: float32 [48, 768], P(None, 'dp')
- new_pos_table: float32 [1024, 768], P(None, 'dp')
- new_attn_qkv: float32 [768, 2304], P('dp')
- new_attn_out: float32 [768, 768], P('dp')
- new_mlp_up: float32 [768, 3072], P('dp')
- new_mlp_down: float32 [3072, 768], P(None, 'dp')
- new_head_out: float32 [768, 96], P('dp')
- new_vectors: float32 [8, 768], P(None, 'dp')
- new_first_embed_in: float32 [48, 768], P(None, 'dp')
- new_first_pos_table: float32 [1024, 768], P(None, 'dp')
- new_first_attn_qkv: float32 [768, 2304], P('dp')
- new_first_attn_out: float32 [768, 768], P('dp')
- new_first_mlp_up: float32 [768, 3072], P('dp')
- new_first_mlp_down: float32 [3072, 768], P(None, 'dp')
- new_first_head_out: float32 [768, 96], P('dp')
- new_first_vectors: float32 [8, 768], P(None, 'dp')
- new_second_embed_in: float32 [48, 768], P(None, 'dp')
- new_second_pos_table: float32 [1024, 768], P(None, 'dp')
- new_second_attn_qkv: float32 [768, 2304], P('dp')
- new_second_attn_out: float32 [768, 768], P('dp')
- new_second_mlp_up: float32 [768, 3072], P('dp')
- new_second_mlp_down: float32 [3072, 768], P(None, 'dp')
- new_second_head_out: float32 [768, 96], P('dp')
- new_second_vectors: float32 [8, 768], P(None, 'dp')
The draws below stay inside these ranges and needn't reach their ends.
Inputs may be any that keep to these rules, and one draw needn't show every extreme that they name: `segments`: in each row slot ids never fall until the trailing padding of 0s (1 to L / 16 slots); images 1 to 3 end within the first L / 16 slots (some may be empty) and image 4 runs from there to the padding.
All inputs are finite; a program needn't handle non-finite values.
Results may differ from the reference program's by a relative error of at most 0.0024.
The reference program's roundings to bfloat16 on the way count: a program that leaves them out, or rounds other values in their place, can miss the bound.
Values may be sent and summed in bfloat16 or wider, within the bound.
A program may use at most 192 MiB of HBM per device.

```python
import math
import jax
import jax.numpy as jnp
from jax import lax

D = 768
HEADS = 12
FF = 3072
PATCH = 48
L = 1024
MICRO = 4
STEP = 10
OUT_DIM = 96
BATCH = 8
PARAMS = 7981056


def draw_segments(key, part):
    key = jax.random.fold_in(key, 11)
    key_cuts, key_pads = jax.random.split(key)
    cuts = jax.random.randint(key_cuts, (MICRO, BATCH, 3), 1, L // 16 + 1)
    cuts = jnp.sort(cuts, axis=-1)
    pads = jax.random.randint(key_pads, (MICRO, BATCH, 1), 1, L // 16 + 1)
    slot = jnp.arange(L)
    ids = 1 + jnp.sum((slot[:, None] >= cuts[:, :, None, :]).astype(jnp.int32), axis=-1)
    return jnp.where(slot[None, None, :] >= L - pads, 0, ids).astype(jnp.int32)


def block_levels(own_key, extent, shards, smallest, largest):
    def one(dim, shards_of):
        draws = jax.random.uniform(jax.random.fold_in(jax.random.fold_in(own_key, 6), dim), (shards_of,), jnp.float32, smallest / len(shards), largest / len(shards))
        return jnp.repeat(jnp.exp(draws), extent[dim] // shards_of).reshape((-1,) + (1,) * (len(extent) - dim - 1))

    factor_of = one(*shards[0])
    for cut in shards[1:]:
        factor_of = factor_of * one(*cut)
    return factor_of


def normal_values(key, extent, deviation, limit, cuts=(), dtype=jnp.bfloat16):
    drawn = deviation * jax.random.normal(key, extent, jnp.float32)
    if cuts:
        drawn = drawn * block_levels(key, extent, cuts, -0.22, 0.18)
    return jnp.clip(drawn, -limit, limit).astype(dtype)


def setup_inputs(seed: int = 0) -> dict:
    streams_of = jax.random.split(jax.random.key(seed), 27)
    patches = normal_values(streams_of[0], (MICRO, BATCH, PATCH, L), 1.0, 6.0, ((1, 8), (3, 4)))
    segments = draw_segments(jax.random.fold_in(streams_of[26], 71), 0)
    embed_in = normal_values(streams_of[2], (PATCH, D), PATCH ** -0.5, 0.875, ((1, 8),), jnp.float32)
    pos_table = normal_values(streams_of[3], (L, D), 0.5, 3.0, ((1, 8),), jnp.float32)
    attn_qkv = normal_values(streams_of[4], (D, 3 * D), D ** -0.5, 0.21875, ((0, 8),), jnp.float32)
    attn_out = normal_values(streams_of[5], (D, D), (D // 16) ** -0.5, 0.875, ((0, 8),), jnp.float32)
    mlp_up = normal_values(streams_of[6], (D, FF), D ** -0.5, 0.21875, ((0, 8),), jnp.float32)
    mlp_down = normal_values(streams_of[7], (FF, D), FF ** -0.5, 0.109375, ((1, 8),), jnp.float32)
    head_out = normal_values(streams_of[8], (D, OUT_DIM), (4 * D) ** -0.5, 0.109375, ((0, 8),), jnp.float32)
    vectors = jnp.clip(1.0 + 0.1 * jax.random.normal(streams_of[9], (8, D), jnp.float32), 0.5, 1.5)
    first_embed_in = normal_values(streams_of[10], (PATCH, D), (0.111 * 0.01 * PARAMS ** -0.5), 2.384185791015625e-06, ((1, 8),), jnp.float32)
    first_pos_table = normal_values(streams_of[11], (L, D), (0.111 * 0.01 * PARAMS ** -0.5 * L ** -0.5), 7.450580596923828e-08, ((1, 8),), jnp.float32)
    first_attn_qkv = normal_values(streams_of[12], (D, 3 * D), (0.111 * 0.01 * PARAMS ** -0.5), 2.384185791015625e-06, ((0, 8),), jnp.float32)
    first_attn_out = normal_values(streams_of[13], (D, D), (0.111 * 0.01 * PARAMS ** -0.5), 2.384185791015625e-06, ((0, 8),), jnp.float32)
    first_mlp_up = normal_values(streams_of[14], (D, FF), (0.111 * 0.01 * PARAMS ** -0.5), 2.384185791015625e-06, ((0, 8),), jnp.float32)
    first_mlp_down = normal_values(streams_of[15], (FF, D), (0.111 * 0.01 * PARAMS ** -0.5), 2.384185791015625e-06, ((1, 8),), jnp.float32)
    first_head_out = normal_values(streams_of[16], (D, OUT_DIM), (0.111 * 0.01 * PARAMS ** -0.5), 2.384185791015625e-06, ((0, 8),), jnp.float32)
    first_vectors = normal_values(streams_of[17], (8, D), (0.111 * 0.04 * PARAMS ** -0.5), 9.5367431640625e-06, ((1, 8),), jnp.float32)
    second_embed_in = jnp.clip(jnp.exp(math.log(2.631230736765966e-12) - 1.3843914 * jax.random.uniform(streams_of[18], (PATCH, D), jnp.float32) ** block_levels(streams_of[18], (PATCH, D), ((1, 8),), -0.2, 0.2)), 6.590606424321244e-13, 2.631230736765966e-12)
    second_pos_table = jnp.clip(jnp.exp(math.log(2.5695612663730136e-15) - 1.3843914 * jax.random.uniform(streams_of[19], (L, D), jnp.float32) ** block_levels(streams_of[19], (L, D), ((1, 8),), -0.2, 0.2)), 6.436139086251215e-16, 2.5695612663730136e-15)
    second_attn_qkv = jnp.clip(jnp.exp(math.log(2.631230736765966e-12) - 1.3843914 * jax.random.uniform(streams_of[20], (D, 3 * D), jnp.float32) ** block_levels(streams_of[20], (D, 3 * D), ((0, 8),), -0.2, 0.2)), 6.590606424321244e-13, 2.631230736765966e-12)
    second_attn_out = jnp.clip(jnp.exp(math.log(2.631230736765966e-12) - 1.3843914 * jax.random.uniform(streams_of[21], (D, D), jnp.float32) ** block_levels(streams_of[21], (D, D), ((0, 8),), -0.2, 0.2)), 6.590606424321244e-13, 2.631230736765966e-12)
    second_mlp_up = jnp.clip(jnp.exp(math.log(2.631230736765966e-12) - 1.3843914 * jax.random.uniform(streams_of[22], (D, FF), jnp.float32) ** block_levels(streams_of[22], (D, FF), ((0, 8),), -0.2, 0.2)), 6.590606424321244e-13, 2.631230736765966e-12)
    second_mlp_down = jnp.clip(jnp.exp(math.log(2.631230736765966e-12) - 1.3843914 * jax.random.uniform(streams_of[23], (FF, D), jnp.float32) ** block_levels(streams_of[23], (FF, D), ((1, 8),), -0.2, 0.2)), 6.590606424321244e-13, 2.631230736765966e-12)
    second_head_out = jnp.clip(jnp.exp(math.log(2.631230736765966e-12) - 1.3843914 * jax.random.uniform(streams_of[24], (D, OUT_DIM), jnp.float32) ** block_levels(streams_of[24], (D, OUT_DIM), ((0, 8),), -0.2, 0.2)), 6.590606424321244e-13, 2.631230736765966e-12)
    second_vectors = jnp.clip(jnp.exp(math.log(4.2099691788255456e-11) - 1.3843914 * jax.random.uniform(streams_of[25], (8, D), jnp.float32) ** block_levels(streams_of[25], (8, D), ((1, 8),), -0.2, 0.2)), 1.054497027891399e-11, 4.2099691788255456e-11)
    return dict(patches=patches, segments=segments, embed_in=embed_in, pos_table=pos_table, attn_qkv=attn_qkv, attn_out=attn_out, mlp_up=mlp_up, mlp_down=mlp_down, head_out=head_out, vectors=vectors, first_embed_in=first_embed_in, first_pos_table=first_pos_table, first_attn_qkv=first_attn_qkv, first_attn_out=first_attn_out, first_mlp_up=first_mlp_up, first_mlp_down=first_mlp_down, first_head_out=first_head_out, first_vectors=first_vectors, second_embed_in=second_embed_in, second_pos_table=second_pos_table, second_attn_qkv=second_attn_qkv, second_attn_out=second_attn_out, second_mlp_up=second_mlp_up, second_mlp_down=second_mlp_down, second_head_out=second_head_out, second_vectors=second_vectors)


HIGH = lax.Precision.HIGHEST
RATE = 0.02
VEC_RATE = 0.15
BETA_ONE = 0.9
BETA_TWO = 0.95
ADAM_EPS = 1e-08
DECAY = 0.1
CLIP_AT = 0.01
NORM_EPS = 1e-05

@jax.custom_vjp
def low(v):
    return lax.optimization_barrier(v.astype(jnp.bfloat16)).astype(jnp.float32)

@jax.custom_vjp
def low_back(v):
    return v

def low_keep(v):
    return (low(v), None)

def low_pass(kept, grad):
    return (grad,)

def back_keep(v):
    return (v, None)

def back_low(kept, grad):
    return (low(grad),)
low.defvjp(low_keep, low_pass)
low_back.defvjp(back_keep, back_low)

def matmul(left, right):
    return jnp.dot(left, right, precision=HIGH, preferred_element_type=jnp.float32)

def layer_norm(hidden, gain, shift):
    mean = lax.optimization_barrier(jnp.mean(hidden, -1, keepdims=True))
    centred = hidden - mean
    var = lax.optimization_barrier(jnp.mean(centred * centred, -1, keepdims=True))
    return centred * lax.rsqrt(var + NORM_EPS) * gain + shift

def row_terms(weights, patch, seg):
    embed, table, wqkv, wattn, wup, wdown, whead, vec = [low(w) for w in weights]
    length = seg.shape[0]
    width = embed.shape[1]
    slot = jnp.arange(length)
    same = seg[:, None] == seg[None, :]
    offset = lax.optimization_barrier(jnp.sum((same & (slot[None, :] < slot[:, None])).astype(jnp.int32), axis=1)).astype(jnp.int32)
    allowed = same & (slot[None, :] <= slot[:, None])
    h0 = low_back(matmul(patch, embed)) + (vec[6] - 1.0) + table[offset]
    normed = low(layer_norm(h0, vec[0], vec[1] - 1.0))
    qkv = low_back(low(matmul(normed, wqkv)))
    head_dim = width // HEADS
    query = qkv[:, :width].reshape(length, HEADS, head_dim)
    keys = qkv[:, width:2 * width].reshape(length, HEADS, head_dim)
    values = qkv[:, 2 * width:].reshape(length, HEADS, head_dim)
    scores = low_back(jnp.einsum('qhd,khd->hqk', query, keys, precision=HIGH) * head_dim ** (-0.5))
    scores = jnp.where(allowed[None], scores, -1e+30)
    probs = low(jax.nn.softmax(scores, axis=-1))
    attended = jnp.einsum('hqk,khd->qhd', probs, values, precision=HIGH).reshape(length, width)
    attended = low_back(low(attended))
    h1 = h0 + low_back(matmul(attended, wattn)) + (vec[7] - 1.0)
    mixed = low(layer_norm(h1, vec[2], vec[3] - 1.0))
    upper = low_back(matmul(mixed, wup))
    hidden = low(jax.nn.gelu(upper))
    h2 = h1 + low_back(matmul(hidden, wdown))
    final = low(layer_norm(h2, vec[4], vec[5] - 1.0))
    out = low_back(matmul(final, whead))
    shift = out[:, :PATCH]
    alpha = out[:, PATCH:]
    following = jnp.concatenate([patch[1:], jnp.zeros((1, PATCH), jnp.float32)], axis=0)
    seg_next = jnp.concatenate([seg[1:], jnp.zeros((1,), jnp.int32)], axis=0)
    pair = ((seg == seg_next) & (seg > 0)).astype(jnp.float32)[:, None]
    first = ((seg > 0) & (offset == 0)).astype(jnp.float32)[:, None]
    scaled = (following - shift) * jnp.exp(-alpha)
    return jnp.sum(pair * (0.5 * scaled * scaled + alpha)) + jnp.sum(first * 0.5 * patch * patch)

def adamw(weight, first, second, grad, rate, decay):
    new_first = BETA_ONE * first + (1.0 - BETA_ONE) * grad
    new_second = BETA_TWO * second + (1.0 - BETA_TWO) * grad * grad
    first_hat = new_first / (1.0 - BETA_ONE ** STEP)
    second_hat = new_second / (1.0 - BETA_TWO ** STEP)
    new_weight = weight - rate * (first_hat / (jnp.sqrt(second_hat) + ADAM_EPS) + decay * weight)
    return (new_weight, new_first, new_second)

def reference(patches, segments, embed_in, pos_table, attn_qkv, attn_out, mlp_up, mlp_down, head_out, vectors, first_embed_in, first_pos_table, first_attn_qkv, first_attn_out, first_mlp_up, first_mlp_down, first_head_out, first_vectors, second_embed_in, second_pos_table, second_attn_qkv, second_attn_out, second_mlp_up, second_mlp_down, second_head_out, second_vectors):
    masters = (embed_in, pos_table, attn_qkv, attn_out, mlp_up, mlp_down, head_out, vectors)
    firsts = (first_embed_in, first_pos_table, first_attn_qkv, first_attn_out, first_mlp_up, first_mlp_down, first_head_out, first_vectors)
    seconds = (second_embed_in, second_pos_table, second_attn_qkv, second_attn_out, second_mlp_up, second_mlp_down, second_head_out, second_vectors)
    length = segments.shape[-1]
    rows_x = jnp.swapaxes(patches, 2, 3).reshape(-1, length, PATCH).astype(jnp.float32)
    rows_seg = segments.reshape(-1, length)
    count = jnp.sum((segments > 0).astype(jnp.int32)).astype(jnp.float32) * PATCH
    row_fn = jax.checkpoint(row_terms)

    def total(weights):

        def one(acc, item):
            return (acc + row_fn(weights, item[0], item[1]), None)
        summed, _ = lax.scan(one, jnp.zeros((), jnp.float32), (rows_x, rows_seg))
        return summed
    loss_sum, pullback = jax.vjp(total, masters)
    grads = pullback(jnp.ones((), jnp.float32))[0]
    grads = [g / count for g in grads]
    norm = jnp.sqrt(sum((jnp.sum(g * g) for g in grads)))
    clip = jnp.minimum(1.0, CLIP_AT / (norm + 1e-06))
    results = [adamw(masters[i], firsts[i], seconds[i], grads[i] * clip, RATE if i < 7 else VEC_RATE, DECAY if i < 7 else 0.0) for i in range(8)]
    news = [r[0] for r in results]
    nfirst = [r[1] for r in results]
    nsecond = [r[2] for r in results]
    return (loss_sum / math.log(2.0), count, norm, news[0], news[1], news[2], news[3], news[4], news[5], news[6], news[7], nfirst[0], nfirst[1], nfirst[2], nfirst[3], nfirst[4], nfirst[5], nfirst[6], nfirst[7], nsecond[0], nsecond[1], nsecond[2], nsecond[3], nsecond[4], nsecond[5], nsecond[6], nsecond[7])
```

```python
import functools
import math

import jax
import jax.numpy as jnp
from jax import lax
from jax.experimental import pallas as pl
from jax.experimental.pallas import tpu as pltpu
from jax.sharding import PartitionSpec as P

HEADS = 12
PATCH = 48
STEP = 10
RATE = 0.02
VEC_RATE = 0.15
BETA_ONE = 0.9
BETA_TWO = 0.95
ADAM_EPS = 1e-08
DECAY = 0.1
CLIP_AT = 0.01
NORM_EPS = 1e-05

F32 = jnp.float32
BF16 = jnp.bfloat16
WIRE = jnp.bfloat16
NN = (((1,), (0,)), ((), ()))
NT = (((1,), (1,)), ((), ()))
TN = (((0,), (0,)), ((), ()))


def dot(left, right, dims=NN):
    return lax.dot_general(left, right, dims, preferred_element_type=F32)


def line(axis, size, count, stride):
    place = (lax.axis_index(axis) // stride) % count
    swaps = [
        (axis, [(source, source ^ (step * stride)) for source in range(size)])
        for step in range(1, count)
    ]
    return (count, place, swaps)


def lines():
    n_dp, n_seq = lax.axis_size("dp"), lax.axis_size("seq")
    n_x = 1 << ((n_dp.bit_length() - 1) // 2)
    return {
        "z": line("dp", n_dp, n_dp // n_x, n_x),
        "x": line("dp", n_dp, n_x, 1),
        "y": line("seq", n_seq, n_seq // 2, 2),
        "core": line("seq", n_seq, 2, 1),
    }


def gather_line(block, along):
    count, place, swaps = along
    others = [lax.ppermute(block, axis, swap) for axis, swap in swaps]
    if count == 2:
        first = place == 0
        return jnp.stack([jnp.where(first, block, others[0]), jnp.where(first, others[0], block)])
    whole = jnp.zeros((count,) + block.shape, block.dtype)
    for step, piece in enumerate([block] + others):
        whole = lax.dynamic_update_index_in_dim(whole, piece, place ^ step, 0)
    return whole


def scatter_line(blocks, along, dim, wire):
    count, place, swaps = along
    pick = lambda index: lax.dynamic_index_in_dim(blocks, index, dim, keepdims=False)
    arrived = [
        lax.ppermute(pick(place ^ (step + 1)).astype(wire), axis, swap)
        for step, (axis, swap) in enumerate(swaps)
    ]
    total = pick(place)
    for piece in arrived:
        total = total + piece.astype(F32)
    return total


def gather_rows(shard, ways, split_y):
    n_core, core, _ = ways["core"]
    n_y, y_at, _ = ways["y"]
    rows, columns = shard.shape
    if split_y:
        part = lax.dynamic_slice_in_dim(
            shard, (core * n_y + y_at) * (rows // (2 * n_y)), rows // (2 * n_y), 0
        )
    else:
        part = lax.dynamic_slice_in_dim(shard, core * (rows // 2), rows // 2, 0)
    part = gather_line(part, ways["z"])
    part = gather_line(part, ways["x"])
    if split_y:
        part = gather_line(part, ways["y"])
        part = gather_line(part, ways["core"])
        part = jnp.transpose(part, (3, 2, 0, 1, 4, 5))
    else:
        part = gather_line(part, ways["core"])
        part = jnp.transpose(part, (2, 1, 0, 3, 4))
    return part.reshape(-1, columns)


def scatter_rows(grad, ways, order, wire):
    n_z, n_x, n_y = ways["z"][0], ways["x"][0], ways["y"][0]
    columns = grad.shape[1]
    blocks = grad.reshape(n_z, n_x, 2, n_y, -1, columns)
    blocks = scatter_line(blocks, ways["core"], 2, wire)
    if order == "xy":
        blocks = scatter_line(blocks, ways["x"], 1, wire)
        blocks = scatter_line(blocks, ways["y"], 1, wire)
    else:
        blocks = scatter_line(blocks, ways["y"], 2, wire)
        blocks = scatter_line(blocks, ways["x"], 1, wire)
    return scatter_line(blocks, ways["z"], 0, wire)


def gather_parts(part, ways):
    part = gather_line(part, ways["y"])
    part = gather_line(part, ways["core"])
    return part.reshape(-1, part.shape[-1])


def visible(seg_key, seg_query, pos_query, keys, tile):
    pos_key = lax.broadcasted_iota(jnp.int32, (keys, tile), 0)
    return (seg_key == seg_query) & (pos_key <= pos_query)


def attend_kernel(tile, skip, hd, scale, q_ref, k_ref, v_ref, sq_ref, sk_ref, qp_ref, o_ref, lse_ref):
    length = k_ref.shape[0]
    for head in range(q_ref.shape[1] // hd):
        cols = slice(hd * head, hd * head + hd)
        for step in range(q_ref.shape[0] // tile):
            rows = slice(step * tile, (step + 1) * tile)
            keys = (step + 1) * tile if skip else length
            query = (q_ref[rows, cols].astype(F32) * scale).astype(BF16)
            scores = dot(k_ref[:keys, cols], query, NT)
            allowed = visible(sk_ref[:keys, :], sq_ref[:, rows], qp_ref[:, rows], keys, tile)
            scores = jnp.where(allowed, scores, -1e30)
            top = jnp.max(scores, 0, keepdims=True)
            weight = jnp.exp(scores - top)
            total = jnp.sum(weight, 0, keepdims=True)
            probs = (weight * (1.0 / total)).astype(BF16)
            o_ref[rows, cols] = dot(probs, v_ref[:keys, cols], TN).astype(BF16)
            lse_ref[0, head : head + 1, rows] = top + jnp.log(total)


def attend_back_kernel(
    tile, skip, hd, scale, q_ref, k_ref, v_ref, do_ref, lse_ref, sq_ref, sk_ref, qp_ref,
    dq_ref, dk_ref, dv_ref, dk_sum, dv_sum,
):
    length = k_ref.shape[0]
    dk_sum[...] = jnp.zeros_like(dk_sum)
    dv_sum[...] = jnp.zeros_like(dv_sum)
    for head in range(q_ref.shape[1] // hd):
        cols = slice(hd * head, hd * head + hd)
        for step in range(q_ref.shape[0] // tile):
            rows = slice(step * tile, (step + 1) * tile)
            keys = (step + 1) * tile if skip else length
            query = (q_ref[rows, cols].astype(F32) * scale).astype(BF16)
            key = k_ref[:keys, cols]
            dout = do_ref[rows, cols]
            scores = dot(key, query, NT)
            allowed = visible(sk_ref[:keys, :], sq_ref[:, rows], qp_ref[:, rows], keys, tile)
            scores = jnp.where(allowed, scores, -1e30)
            probs = jnp.exp(scores - lse_ref[0, head : head + 1, rows])
            dprobs = dot(v_ref[:keys, cols], dout, NT)
            delta = jnp.sum(dprobs * probs, 0, keepdims=True)
            dscores = (probs * (dprobs - delta)).astype(BF16)
            dv_sum[:keys, cols] += dot(probs.astype(BF16), dout)
            dk_sum[:keys, cols] += dot(dscores, query)
            dq_ref[rows, cols] = (dot(dscores, key, TN) * scale).astype(dq_ref.dtype)
    dk_ref[...] = dk_sum[...].astype(dk_ref.dtype)
    dv_ref[...] = dv_sum[...].astype(dv_ref.dtype)


def blocks_of(rows, width, offset):
    return pl.BlockSpec((rows, width), lambda pair: (0, pair + offset))


def fixed(shape):
    return pl.BlockSpec(shape, lambda pair: (0, 0))


def kernel_params():
    return pltpu.CompilerParams(vmem_limit_bytes=48 * 2**20)


def attend(qkv, keys, values, offsets, seg_q, seg_k, pos_q, width):
    count, length = qkv.shape[0], keys.shape[0]
    hd = width // HEADS
    lanes = 2 * hd
    pairs = HEADS // 2
    return pl.pallas_call(
        functools.partial(attend_kernel, min(256, count), count == length, hd, hd**-0.5),
        grid=(pairs,),
        in_specs=[
            blocks_of(count, lanes, 0),
            blocks_of(length, lanes, offsets[0]),
            blocks_of(length, lanes, offsets[1]),
            fixed((1, count)),
            fixed((length, 1)),
            fixed((1, count)),
        ],
        out_specs=[blocks_of(count, lanes, 0), pl.BlockSpec((1, 2, count), lambda pair: (pair, 0, 0))],
        out_shape=[
            jax.ShapeDtypeStruct((count, width), BF16),
            jax.ShapeDtypeStruct((pairs, 2, count), F32),
        ],
        cost_estimate=pl.CostEstimate(
            flops=25_000_000_000, bytes_accessed=8_000_000, transcendentals=8_000_000
        ),
        compiler_params=kernel_params(),
    )(qkv, keys, values, seg_q, seg_k, pos_q)


def attend_back(qkv, keys, values, offsets, dout, lse, seg_q, seg_k, pos_q, width, kv_type):
    count, length = qkv.shape[0], keys.shape[0]
    hd = width // HEADS
    lanes = 2 * hd
    pairs = HEADS // 2
    return pl.pallas_call(
        functools.partial(attend_back_kernel, min(256, count), count == length, hd, hd**-0.5),
        grid=(pairs,),
        in_specs=[
            blocks_of(count, lanes, 0),
            blocks_of(length, lanes, offsets[0]),
            blocks_of(length, lanes, offsets[1]),
            blocks_of(count, lanes, 0),
            pl.BlockSpec((1, 2, count), lambda pair: (pair, 0, 0)),
            fixed((1, count)),
            fixed((length, 1)),
            fixed((1, count)),
        ],
        out_specs=[
            blocks_of(count, lanes, 0),
            blocks_of(length, lanes, 0),
            blocks_of(length, lanes, 0),
        ],
        out_shape=[
            jax.ShapeDtypeStruct((count, width), BF16),
            jax.ShapeDtypeStruct((length, width), kv_type),
            jax.ShapeDtypeStruct((length, width), kv_type),
        ],
        scratch_shapes=[pltpu.VMEM((length, lanes), F32)] * 2,
        cost_estimate=pl.CostEstimate(
            flops=40_000_000_000, bytes_accessed=12_000_000, transcendentals=8_000_000
        ),
        compiler_params=kernel_params(),
    )(qkv, keys, values, dout, lse, seg_q, seg_k, pos_q)


def layer_norm(hidden, gain, shift):
    mean = jnp.mean(hidden, -1, keepdims=True)
    centred = hidden - mean
    var = jnp.mean(centred * centred, -1, keepdims=True)
    rstd = lax.rsqrt(var + NORM_EPS)
    unit = centred * rstd
    return (unit * gain + shift, unit, rstd)


def norm_back(grad, unit, rstd, gain):
    dunit = grad * gain
    dhid = rstd * (
        dunit
        - jnp.mean(dunit, -1, keepdims=True)
        - unit * jnp.mean(dunit * unit, -1, keepdims=True)
    )
    return (dhid, jnp.sum(grad * unit, 0), jnp.sum(grad, 0))


def adamw(weight, first, second, grad, rate, decay):
    new_first = BETA_ONE * first + (1.0 - BETA_ONE) * grad
    new_second = BETA_TWO * second + (1.0 - BETA_TWO) * grad * grad
    first_hat = new_first / (1.0 - BETA_ONE**STEP)
    second_hat = new_second / (1.0 - BETA_TWO**STEP)
    return (
        weight - rate * (first_hat / (jnp.sqrt(second_hat) + ADAM_EPS) + decay * weight),
        new_first,
        new_second,
    )


def body(*args):
    patches, segments = args[:2]
    masters, firsts, seconds = (args[2:10], args[10:18], args[18:26])
    embed_in, pos_table, attn_qkv, attn_out, mlp_up, mlp_down, head_out, vectors = masters
    ways = lines()
    n_seq = lax.axis_size("seq")
    seq_at = lax.axis_index("seq")
    micros, group = segments.shape[0], segments.shape[2]
    length = group * n_seq
    width = attn_qkv.shape[1] // 3

    share = max(1, n_seq // micros)
    count = length // share
    mine = seq_at // share
    patches = patches.reshape(micros, PATCH, group)
    segments = segments.reshape(micros, group)
    if share == 1:
        swaps = [
            ("seq", [(source, source ^ step) for source in range(n_seq)]) for step in range(1, n_seq)
        ]
        row = jnp.zeros((n_seq, PATCH, group), BF16)
        seg = jnp.zeros((n_seq, group), jnp.int32)
        for step in range(n_seq):
            piece = lax.dynamic_index_in_dim(patches, seq_at ^ step, 0, keepdims=False)
            ids = lax.dynamic_index_in_dim(segments, seq_at ^ step, 0, keepdims=False)
            if step:
                piece = lax.ppermute(piece, *swaps[step - 1])
                ids = lax.ppermute(ids, *swaps[step - 1])
            row = lax.dynamic_update_index_in_dim(row, piece, seq_at ^ step, 0)
            seg = lax.dynamic_update_index_in_dim(seg, ids, seq_at ^ step, 0)
        row = jnp.swapaxes(row, 0, 1).reshape(PATCH, length)
        seg = seg.reshape(length)
    else:
        row = lax.all_gather(patches, "seq", axis=2, tiled=True)
        seg = lax.all_gather(segments, "seq", axis=1, tiled=True)
        row = lax.dynamic_index_in_dim(row, mine, 0, keepdims=False)
        seg = lax.dynamic_index_in_dim(seg, mine, 0, keepdims=False)
    start = (seq_at % share) * count
    part = lambda value: lax.dynamic_slice_in_dim(value, start, count, 0)

    low = lambda value: value.astype(BF16)
    early = jnp.concatenate(
        [low(attn_qkv), low(pos_table).T, low(embed_in).T, low(vectors).T], axis=1
    )
    early = gather_rows(early, ways, False)
    w_qkv = early[:, : 3 * width]
    w_pos = early[:, 3 * width : 3 * width + length + PATCH]
    gains = early[:, 3 * width + length + PATCH :].astype(F32).T
    w_attn = gather_rows(jnp.concatenate([low(attn_out), low(head_out)], axis=1), ways, False)
    w_head = w_attn[:, width:]
    w_attn = w_attn[:, :width]
    w_up = gather_rows(low(mlp_up), ways, True)
    w_down = gather_rows(low(mlp_down).T, ways, True)

    at = jnp.arange(length)
    begins = jnp.zeros((length,), jnp.int32)
    for image in range(5):
        before = (seg > 0) & (seg < image) if image else seg > 0
        begins = jnp.where(seg == image, jnp.sum(before.astype(jnp.int32)), begins)
    offset = part(at - begins)
    own = part(seg)
    tokens = part(row.T)
    later = part(jnp.concatenate([row[:, 1:], jnp.zeros((PATCH, 1), BF16)], axis=1).T)
    seg_next = part(jnp.concatenate([seg[1:], jnp.zeros((1,), jnp.int32)]))
    pair = ((own == seg_next) & (own > 0)).astype(F32)[:, None]
    first = ((own > 0) & (offset == 0)).astype(F32)[:, None]
    valid = jnp.sum((own > 0).astype(jnp.int32)).astype(F32) * PATCH
    lookup = (offset[:, None] == jnp.arange(length)[None, :]).astype(BF16)
    inputs = jnp.concatenate([lookup, tokens], axis=1)
    seg_q, seg_k, pos_q = (own[None, :], seg[:, None], part(at)[None, :].astype(jnp.int32))

    h0 = dot(inputs, w_pos, NT) + (gains[6] - 1.0)
    normed, unit_one, rstd_one = layer_norm(h0, gains[0], gains[1] - 1.0)
    normed = low(normed)
    qkv = low(dot(normed, w_qkv))
    if share == 1:
        keys, values, offsets = (qkv, qkv, (HEADS // 2, HEADS))
    else:
        near = [list(range(g, g + share)) for g in range(0, n_seq, share)]
        keys = lax.all_gather(qkv[:, width:], "seq", axis=0, tiled=True, axis_index_groups=near)
        values, offsets = (keys, (0, HEADS // 2))
    attended, lse = attend(qkv, keys, values, offsets, seg_q, seg_k, pos_q, width)
    h1 = h0 + dot(attended, w_attn) + (gains[7] - 1.0)
    mixed, unit_two, rstd_two = layer_norm(h1, gains[2], gains[3] - 1.0)
    mixed = low(mixed)
    upper = dot(mixed, w_up)
    hidden = low(jax.nn.gelu(upper))
    h2 = h1 + dot(hidden, w_down, NT)
    final, unit_fin, rstd_fin = layer_norm(h2, gains[4], gains[5] - 1.0)
    final = low(final)
    out = dot(final, w_head)
    alpha = out[:, PATCH:]
    shrink = jnp.exp(-alpha)
    scaled = (later.astype(F32) - out[:, :PATCH]) * shrink
    plain = tokens.astype(F32)
    total = jnp.sum(pair * (0.5 * scaled * scaled + alpha)) + jnp.sum(first * 0.5 * plain * plain)

    dout = low(jnp.concatenate([-pair * scaled * shrink, pair * (1.0 - scaled * scaled)], axis=1))
    grad_head = dot(final, dout, TN)
    dh2, gain_fin, shift_fin = norm_back(dot(dout, w_head, NT), unit_fin, rstd_fin, gains[4])
    ddown = low(dh2)
    grad_down = dot(ddown, hidden, TN)
    _, gelu_back = jax.vjp(jax.nn.gelu, upper)
    dupper = low(gelu_back(dot(ddown, w_down))[0])
    grad_up = dot(mixed, dupper, TN)
    dnorm, gain_two, shift_two = norm_back(dot(dupper, w_up, NT), unit_two, rstd_two, gains[2])
    dh1 = dh2 + dnorm
    dattn = low(dh1)
    grad_attn = dot(attended, dattn, TN)
    dattended = low(dot(dattn, w_attn, NT))
    dquery, dkeys, dvalues = attend_back(
        qkv, keys, values, offsets, dattended, lse, seg_q, seg_k, pos_q, width,
        BF16 if share == 1 else F32,
    )
    if share > 1:
        dkeys, dvalues = (
            low(lax.psum_scatter(d, "seq", scatter_dimension=0, tiled=True, axis_index_groups=near))
            for d in (dkeys, dvalues)
        )
    dqkv = jnp.concatenate([dquery, dkeys, dvalues], axis=1)
    grad_qkv = dot(normed, dqkv, TN)
    dnorm, gain_one, shift_one = norm_back(dot(dqkv, w_qkv, NT), unit_one, rstd_one, gains[0])
    dh0 = dh1 + dnorm
    high = low(dh0)
    rest = low(dh0 - high.astype(F32))
    grad_pos = dot(high, inputs, TN)
    grad_pos = jnp.concatenate(
        [grad_pos[:, :length] + dot(rest, lookup, TN), grad_pos[:, length:]], axis=1
    )
    grad_vec = jnp.stack(
        [
            gain_one,
            shift_one,
            gain_two,
            shift_two,
            gain_fin,
            shift_fin,
            jnp.sum(dh0, 0),
            jnp.sum(dh1, 0),
        ],
        axis=1,
    )

    parts = [
        scatter_rows(grad_down, ways, "xy", WIRE),
        scatter_rows(grad_up, ways, "yx", WIRE),
        scatter_rows(grad_attn, ways, "xy", WIRE),
        scatter_rows(grad_qkv, ways, "yx", WIRE),
        scatter_rows(grad_pos[:, :length], ways, "xy", WIRE),
        scatter_rows(
            jnp.concatenate([grad_head, grad_pos[:, length:], grad_vec], axis=1), ways, "xy", F32
        ),
    ]
    squares = sum(jnp.sum(p * p) for p in parts)
    squares, total, valid = lax.psum((squares, total, valid), ("dp", "seq"))
    down, up, attn, wide, table, small = [gather_parts(p, ways) for p in parts]
    outs = head_out.shape[1]
    pieces = [
        small[:, outs : outs + PATCH].T,
        table.T,
        wide,
        attn,
        up,
        down.T,
        small[:, :outs],
        small[:, outs + PATCH :].T,
    ]
    norm = jnp.sqrt(squares) / valid
    clip = jnp.minimum(1.0, CLIP_AT / (norm + 1e-06))
    results = [
        adamw(
            masters[i],
            firsts[i],
            seconds[i],
            pieces[i] / valid * clip,
            RATE if i < 7 else VEC_RATE,
            DECAY if i < 7 else 0.0,
        )
        for i in range(8)
    ]
    return (
        total / math.log(2.0),
        valid,
        norm,
        *[r[0] for r in results],
        *[r[1] for r in results],
        *[r[2] for r in results],
    )


def solution(mesh):
    rows, columns = (P("dp", None), P(None, "dp"))
    weights = (columns, columns, rows, rows, rows, columns, rows, columns)
    in_specs = (P(None, "dp", None, "seq"), P(None, "dp", "seq")) + weights * 3
    out_specs = (P(), P(), P()) + weights * 3
    return jax.shard_map(body, mesh=mesh, in_specs=in_specs, out_specs=out_specs, check_vma=False)
```

```python
import functools
import math

import jax
import jax.numpy as jnp
from jax import lax
from jax.experimental import pallas as pl
from jax.experimental.pallas import tpu as pltpu
from jax.sharding import PartitionSpec as P

HEADS = 12
PATCH = 48
STEP = 10
RATE = 0.02
VEC_RATE = 0.15
BETA_ONE = 0.9
BETA_TWO = 0.95
ADAM_EPS = 1e-08
DECAY = 0.1
CLIP_AT = 0.01
NORM_EPS = 1e-05

F32 = jnp.float32
BF16 = jnp.bfloat16
WIRE = jnp.bfloat16
GATHER = [
    (1, 0, 1536, True),
    (1, 1536, 1536, True),
    (2, 0, 1536, True),
    (2, 1536, 1536, True),
    (3, 0, 768, True),
    (0, 0, 2304, False),
    (4, 0, 1024, False),
    (5, 0, 256, False),
]
REDUCE = [
    (5, 0, 256, "xy"),
    (0, 0, 1536, "yx"),
    (0, 1536, 1536, "xy"),
    (1, 0, 1536, "yx"),
    (1, 1536, 1536, "xy"),
    (2, 0, 768, "yx"),
    (3, 0, 1280, "xy"),
    (3, 1280, 1024, "yx"),
    (4, 0, 1024, "xy"),
]
NN = (((1,), (0,)), ((), ()))
NT = (((1,), (1,)), ((), ()))
TN = (((0,), (0,)), ((), ()))


def dot(left, right, dims=NN):
    return lax.dot_general(left, right, dims, preferred_element_type=F32)


def line(axis, size, count, stride):
    place = (lax.axis_index(axis) // stride) % count
    swaps = [
        (axis, [(source, source ^ (step * stride)) for source in range(size)])
        for step in range(1, count)
    ]
    return (count, place, swaps)


def lines():
    n_dp, n_seq = lax.axis_size("dp"), lax.axis_size("seq")
    n_x = 1 << ((n_dp.bit_length() - 1) // 2)
    return {
        "z": line("dp", n_dp, n_dp // n_x, n_x),
        "x": line("dp", n_dp, n_x, 1),
        "y": line("seq", n_seq, n_seq // 2, 2),
        "core": line("seq", n_seq, 2, 1),
    }


def gather_line(block, along):
    count, place, swaps = along
    others = [lax.ppermute(block, axis, swap) for axis, swap in swaps]
    if count == 2:
        first = place == 0
        return jnp.stack([jnp.where(first, block, others[0]), jnp.where(first, others[0], block)])
    whole = jnp.zeros((count,) + block.shape, block.dtype)
    for step, piece in enumerate([block] + others):
        whole = lax.dynamic_update_index_in_dim(whole, piece, place ^ step, 0)
    return whole


def scatter_line(blocks, along, dim, wire):
    count, place, swaps = along
    pick = lambda index: lax.dynamic_index_in_dim(blocks, index, dim, keepdims=False)
    arrived = [
        lax.ppermute(pick(place ^ (step + 1)).astype(wire), axis, swap)
        for step, (axis, swap) in enumerate(swaps)
    ]
    total = pick(place)
    for piece in arrived:
        total = total + piece.astype(F32)
    return total


def gather_rows(shard, ways, split_y):
    n_core, core, _ = ways["core"]
    n_y, y_at, _ = ways["y"]
    rows, columns = shard.shape
    if split_y:
        part = lax.dynamic_slice_in_dim(
            shard, (core * n_y + y_at) * (rows // (2 * n_y)), rows // (2 * n_y), 0
        )
    else:
        part = lax.dynamic_slice_in_dim(shard, core * (rows // 2), rows // 2, 0)
    part = gather_line(part, ways["z"])
    part = gather_line(part, ways["x"])
    if split_y:
        part = gather_line(part, ways["y"])
        part = gather_line(part, ways["core"])
        part = jnp.transpose(part, (3, 2, 0, 1, 4, 5))
    else:
        part = gather_line(part, ways["core"])
        part = jnp.transpose(part, (2, 1, 0, 3, 4))
    return part.reshape(-1, columns)


def scatter_rows(grad, ways, order, wire):
    n_z, n_x, n_y = ways["z"][0], ways["x"][0], ways["y"][0]
    columns = grad.shape[1]
    blocks = grad.reshape(n_z, n_x, 2, n_y, -1, columns)
    blocks = scatter_line(blocks, ways["core"], 2, wire)
    if order == "xy":
        blocks = scatter_line(blocks, ways["x"], 1, wire)
        blocks = scatter_line(blocks, ways["y"], 1, wire)
    else:
        blocks = scatter_line(blocks, ways["y"], 2, wire)
        blocks = scatter_line(blocks, ways["x"], 1, wire)
    return scatter_line(blocks, ways["z"], 0, wire)


def gather_parts(part, ways):
    part = gather_line(part, ways["y"])
    part = gather_line(part, ways["core"])
    return part.reshape(-1, part.shape[-1])


MESH=pl.DeviceIdType.MESH
X = 2
Z = 4
def here():
    d=lax.axis_index("dp"); s=lax.axis_index("seq")
    return d//X, d%X, s//2, s%2
def peer(kz,kx,ky,kc):
    z,x,y,c=here()
    return ((z^kz)*X+(x^kx), (y^ky)*2+(c^kc))
class Gather:
    def __init__(s, src, dst, sems, base, split, lo, width):
        s.src,s.dst,s.split,s.lo,s.width=src,dst,split,lo,width
        s.send,s.recv=sems; s.n=base
        s.live=[]; s.rows=src.shape[0]
        s.idx={}
    def region(s,ref,kz,kx,half,ky,local=False):
        z,x,y,c=here(); r=s.rows//2
        row=(c^half)*r
        if not local: row=row+((z^kz)*X+(x^kx))*s.rows
        row=pl.multiple_of(row,16)
        if ky is None: return ref.at[pl.ds(row,r),pl.ds(s.lo,s.width)]
        w=s.width//2
        return ref.at[pl.ds(row,r),pl.ds(pl.multiple_of(s.lo+(y^ky)*w,128),w)]
    def copy(s,key,kz,kx,ky,to,own=False):
        i=s.idx.setdefault(key,s.n)
        if i==s.n: s.n+=1
        col=ky if s.split else None
        return pltpu.make_async_remote_copy(s.region(s.src if own else s.dst,kz,kx,0,col,own),s.region(s.dst,kz,kx,0,col),s.send.at[i],s.recv.at[i],device_id=peer(*to),device_id_type=MESH)
    def start(s,*a,**k):
        c=s.copy(*a,**k); c.start(); s.live.append(c); return c
    def begin(s):
        for k in (1,2,3): s.start(("z",k),0,0,0,(k,0,0,0),own=True)
        s.start(("x",0),0,0,0,(0,1,0,0),own=True)
    def after_z(s,k):
        s.recvd(("z",k),k,0,0)
        s.start(("x",k),k,0,0,(0,1,0,0))
        if s.split: s.start(("y",k,0),k,0,0,(0,0,1,0))
        s.start(("c",k,0),k,0,0,(0,0,0,1))
    def after_x(s,k):
        s.recvd(("x",k),k,1,0)
        if s.split: s.start(("y",k,1),k,1,0,(0,0,1,0))
        s.start(("c",k,1),k,1,0,(0,0,0,1))
    def after_y(s,k,kx):
        s.recvd(("y",k,kx),k,kx,1)
        s.start(("d",k,kx),k,kx,1,(0,0,0,1))
    def recvd(s,key,kz,kx,ky):
        s.copy(key,kz,kx,ky,(0,0,0,1)).wait_recv()
    def stage_z(s):
        for k in (1,2,3): s.after_z(k)
    def stage_x(s):
        for k in range(4): s.after_x(k)
    def stage_y(s):
        if s.split:
            for kx in range(2):
                for k in range(4):
                    if k or kx: s.after_y(k,kx)
    def finish(s):
        for k in range(4):
            for kx in range(2):
                if (k or kx):
                    s.core_recv(("c",k,kx),k,kx,0)
                    if s.split: s.core_recv(("d",k,kx),k,kx,1)
        for c in s.live: c.wait_send()
    def core_recv(s,key,kz,kx,ky):
        i=s.idx[key]; col=ky if s.split else None
        r=s.region(s.dst,kz,kx,1,col)
        pltpu.make_async_remote_copy(r,r,s.send.at[i],s.recv.at[i],device_id=peer(0,0,0,1),device_id_type=MESH).wait_recv()

def greet(peers):
    bar=pltpu.get_barrier_semaphore()
    for p in peers: pl.semaphore_signal(bar,inc=1,device_id=peer(*p),device_id_type=MESH)
    pl.semaphore_wait(bar,len(peers))
PEERS=[(1,0,0,0),(2,0,0,0),(3,0,0,0),(0,1,0,0),(0,0,1,0),(0,0,0,1)]
def gather_kernel(chunks,n,ahead,*refs):
    src,dst=refs[:n],refs[n:2*n]; send,recv,loc=refs[2*n:]
    greet(PEERS)
    z,x,y,c=here()
    mine=[]
    for i in range(n):
        r=src[i].shape[0]
        m=pltpu.make_async_copy(src[i],dst[i].at[pl.ds(pl.multiple_of((z*X+x)*r,16),r),:],loc.at[i]); m.start(); mine.append(m)
    g=[]; base=0
    for (t,lo,w,sp) in chunks:
        g.append(Gather(src[t],dst[t],(send,recv),base,sp,lo,w)); base+=28 if sp else 14
    m=len(g)
    for i in range(min(ahead,m)): g[i].begin()
    for s in range(m+2):
        if s<m:
            g[s].stage_z()
            if s+ahead<m: g[s+ahead].begin()
        if 0<=s-1<m: g[s-1].stage_x()
        if 0<=s-2<m: g[s-2].stage_y()
    for a in g: a.finish()
    for a in mine: a.wait()
def gather(shards,chunks,ahead=2,cid=1):
    n=len(shards); dp=lax.axis_size("dp")
    tot=sum(28 if s[3] else 14 for s in chunks)
    anyspec=pl.BlockSpec(memory_space=pl.ANY)
    return pl.pallas_call(functools.partial(gather_kernel,chunks,n,ahead),
      out_shape=[jax.ShapeDtypeStruct((s.shape[0]*dp,s.shape[1]),s.dtype) for s in shards],
      in_specs=[pl.BlockSpec(memory_space=pltpu.VMEM)]*n,out_specs=[anyspec]*n,
      scratch_shapes=[pltpu.SemaphoreType.DMA((tot,)),pltpu.SemaphoreType.DMA((tot,)),pltpu.SemaphoreType.DMA((n,))],
      compiler_params=pltpu.CompilerParams(collective_id=cid,has_side_effects=True))(*shards)


PER=8
class Reduce:
    def __init__(s,g,out,bufs,sems,base,lo,w,order):
        s.g,s.out,s.lo,s.w,s.order=g,out,lo,w,order
        s.gc,s.r1,s.p2,s.r2,s.p3,s.r3,s.p4,s.r4=bufs
        s.send,s.recv,s.loc=sems; s.base=base; s.r=g.shape[3]
    def col(s,ky,lo=0):
        z,x,y,c=here(); h=s.w//2
        return pl.ds(pl.multiple_of(lo+(y^ky)*h,128),h)
    def remote(s,src,dst,i,to):
        return pltpu.make_async_remote_copy(src,dst,s.send.at[s.base+i],s.recv.at[s.base+i],device_id=peer(*to),device_id_type=MESH)
    def load(s):
        z,x,y,c=here()
        return pltpu.make_async_copy(s.g.at[:,:,c,:,pl.ds(s.lo,s.w)],s.gc,s.loc)
    def c1(s):
        z,x,y,c=here()
        return s.remote(s.g.at[:,:,1-c,:,pl.ds(s.lo,s.w)],s.r1,0,(0,0,0,1))
    def begin(s):
        s.load().start(); s.c1().start()
    def two(s,zz,xx,cols):
        return s.gc[zz,xx,:,cols].astype(F32)+s.r1[zz,xx,:,cols].astype(F32)
    def three(s,zz,xx,ky):
        z,x,y,c=here()
        if s.order=="xy": return s.two(zz,xx,s.col(ky))+s.r2[zz,:,s.col(ky)].astype(F32)
        return s.two(zz,xx,s.col(ky))+s.r2[zz,xx].astype(F32)
    def four(s,zz):
        z,x,y,c=here()
        return s.three(zz,x,0)+s.r3[zz].astype(F32)
    def c2(s): return s.remote(s.p2,s.r2,1,(0,1,0,0) if s.order=="xy" else (0,0,1,0))
    def c3(s): return s.remote(s.p3,s.r3,2,(0,0,1,0) if s.order=="xy" else (0,1,0,0))
    def c4(s,k): return s.remote(s.p4.at[k-1],s.r4.at[k-1],2+k,(k,0,0,0))
    def c5(s):
        z,x,y,c=here()
        ref=s.out.at[pl.ds(pl.multiple_of(c*s.r,8),s.r),s.col(0,s.lo)]
        return s.remote(ref,ref,6,(0,0,1,0))
    def c6(s):
        z,x,y,c=here()
        ref=s.out.at[pl.ds(pl.multiple_of(c*s.r,8),s.r),pl.ds(s.lo,s.w)]
        return s.remote(ref,ref,7,(0,0,0,1))
    def stage1(s):
        z,x,y,c=here()
        s.load().wait(); s.c1().wait_recv()
        @pl.loop(0,Z)
        def _(zz):
            if s.order=="xy":
                s.p2[zz]=s.two(zz,1-x,slice(None)).astype(s.p2.dtype)
            else:
                for xx in range(X): s.p2[zz,xx]=s.two(zz,xx,s.col(1)).astype(s.p2.dtype)
        s.c2().start()
    def stage2(s):
        z,x,y,c=here()
        s.c2().wait_recv()
        @pl.loop(0,Z)
        def _(zz):
            s.p3[zz]=(s.three(zz,x,1) if s.order=="xy" else s.three(zz,1-x,0)).astype(s.p3.dtype)
        s.c3().start()
    def stage3(s):
        z,x,y,c=here()
        s.c3().wait_recv()
        for k in (1,2,3):
            s.p4[k-1]=s.four(z^k).astype(s.p4.dtype)
            s.c4(k).start()
    def stage4(s):
        z,x,y,c=here()
        total=s.four(z)
        for k in (1,2,3):
            s.c4(k).wait_recv()
            total=total+s.r4[k-1].astype(F32)
        s.out[pl.ds(pl.multiple_of(c*s.r,8),s.r),s.col(0,s.lo)]=total
        s.c5().start()
        return total
    def stage5(s):
        s.c5().wait_recv()
        s.c6().start()
    def finish(s):
        s.c6().wait_recv()
        s.c1().wait_send(); s.c2().wait_send(); s.c3().wait_send()
        for k in (1,2,3): s.c4(k).wait_send()
        s.c5().wait_send(); s.c6().wait_send()

def shapes(r,w,order,dt):
    h=w//2
    two=(Z,r,w) if order=="xy" else (Z,X,r,h)
    return [((Z,X,r,w),dt)]*2+[(two,dt)]*2+[((Z,r,h),dt)]*2+[((3,r,h),dt)]*2

def totals(part,got,send,recv,base):
    d=lax.axis_index("dp"); q=lax.axis_index("seq")
    def hop(first,count,mine,peers):
        got[first+mine]=part[...]
        cs=[pltpu.make_async_remote_copy(part,got.at[first+mine],send.at[base+first+i],recv.at[base+first+i],device_id=p,device_id_type=MESH) for i,p in enumerate(peers)]
        for k in cs: k.start()
        for k in cs: k.wait()
        t=got[first]
        for i in range(1,count): t=t+got[first+i]
        part[...]=t
    hop(0,4,q,[peer(0,0,ky,kc) for ky,kc in ((0,1),(1,0),(1,1))])
    hop(4,8,d,[peer(kz,kx,0,0) for kz,kx in ((0,1),(1,0),(1,1),(2,0),(2,1),(3,0),(3,1))])

ALL=[(0,0,ky,kc) for ky,kc in ((0,1),(1,0),(1,1))]+[(kz,kx,0,0) for kz,kx in ((0,1),(1,0),(1,1),(2,0),(2,1),(3,0),(3,1))]
def fold(v):
    v=v*v
    t=jnp.zeros((8,128),F32)
    for i in range(v.shape[0]//8):
        for j in range(v.shape[1]//128):
            t=t+v[8*i:8*i+8,128*j:128*j+128]
    return t
def rs_kernel(chunks,n,*refs):
    g,part=refs[:n],refs[n]
    out,tot=refs[n+1:2*n+1],refs[2*n+1]
    k=2*n+2
    bufs=refs[k:k+8*len(chunks)]; send,recv,loc,got=refs[k+8*len(chunks):]
    greet(ALL)
    R=[Reduce(g[t],out[t],bufs[8*i:8*i+8],(send,recv,loc.at[i]),PER*i,lo,w,o) for i,(t,lo,w,o) in enumerate(chunks)]
    m=len(R)
    for a in R: a.begin()
    tot[...]=part[...]
    for s in range(m+4):
        if s<m: R[s].stage1()
        if 0<=s-1<m: R[s-1].stage2()
        if 0<=s-2<m: R[s-2].stage3()
        if 0<=s-3<m: tot[0]+=fold(R[s-3].stage4())
        if 0<=s-4<m: R[s-4].stage5()
    totals(tot,got,send,recv,PER*m)
    for a in R: a.finish()
def reduce_all(grads,part,chunks,cid=2):
    n=len(grads); dp=lax.axis_size("dp")
    r=grads[0].shape[0]//dp//2
    anyspec=pl.BlockSpec(memory_space=pl.ANY); vm=pl.BlockSpec(memory_space=pltpu.VMEM)
    bufs=[pltpu.VMEM(sh,dt) for (t,lo,w,o) in chunks for sh,dt in shapes(r,w,o,grads[t].dtype)]
    ns=PER*len(chunks)+12
    return pl.pallas_call(functools.partial(rs_kernel,chunks,n),
      out_shape=[jax.ShapeDtypeStruct((2*r,g.shape[1]),F32) for g in grads]+[jax.ShapeDtypeStruct((3,8,128),F32)],
      in_specs=[anyspec]*n+[vm],out_specs=[vm]*(n+1),
      scratch_shapes=bufs+[pltpu.SemaphoreType.DMA((ns,)),pltpu.SemaphoreType.DMA((ns,)),pltpu.SemaphoreType.DMA((len(chunks),)),pltpu.VMEM((12,3,8,128),F32)],
      compiler_params=pltpu.CompilerParams(collective_id=cid,has_side_effects=True,vmem_limit_bytes=60*2**20))(*[g.reshape(Z,X,2,r,-1) for g in grads],part)


def visible(seg_key, seg_query, pos_query, keys, tile):
    pos_key = lax.broadcasted_iota(jnp.int32, (keys, tile), 0)
    return (seg_key == seg_query) & (pos_key <= pos_query)


def attend_kernel(tile, skip, hd, scale, q_ref, k_ref, v_ref, sq_ref, sk_ref, qp_ref, o_ref, lse_ref):
    length = k_ref.shape[0]
    for head in range(q_ref.shape[1] // hd):
        cols = slice(hd * head, hd * head + hd)
        for step in range(q_ref.shape[0] // tile):
            rows = slice(step * tile, (step + 1) * tile)
            keys = (step + 1) * tile if skip else length
            query = (q_ref[rows, cols].astype(F32) * scale).astype(BF16)
            scores = dot(k_ref[:keys, cols], query, NT)
            allowed = visible(sk_ref[:keys, :], sq_ref[:, rows], qp_ref[:, rows], keys, tile)
            scores = jnp.where(allowed, scores, -1e30)
            top = jnp.max(scores, 0, keepdims=True)
            weight = jnp.exp(scores - top)
            total = jnp.sum(weight, 0, keepdims=True)
            probs = (weight * (1.0 / total)).astype(BF16)
            o_ref[rows, cols] = dot(probs, v_ref[:keys, cols], TN).astype(BF16)
            lse_ref[0, head : head + 1, rows] = top + jnp.log(total)


def attend_back_kernel(
    tile, skip, hd, scale, q_ref, k_ref, v_ref, do_ref, lse_ref, sq_ref, sk_ref, qp_ref,
    dq_ref, dk_ref, dv_ref, dk_sum, dv_sum,
):
    length = k_ref.shape[0]
    dk_sum[...] = jnp.zeros_like(dk_sum)
    dv_sum[...] = jnp.zeros_like(dv_sum)
    for head in range(q_ref.shape[1] // hd):
        cols = slice(hd * head, hd * head + hd)
        for step in range(q_ref.shape[0] // tile):
            rows = slice(step * tile, (step + 1) * tile)
            keys = (step + 1) * tile if skip else length
            query = (q_ref[rows, cols].astype(F32) * scale).astype(BF16)
            key = k_ref[:keys, cols]
            dout = do_ref[rows, cols]
            scores = dot(key, query, NT)
            allowed = visible(sk_ref[:keys, :], sq_ref[:, rows], qp_ref[:, rows], keys, tile)
            scores = jnp.where(allowed, scores, -1e30)
            probs = jnp.exp(scores - lse_ref[0, head : head + 1, rows])
            dprobs = dot(v_ref[:keys, cols], dout, NT)
            delta = jnp.sum(dprobs * probs, 0, keepdims=True)
            dscores = (probs * (dprobs - delta)).astype(BF16)
            dv_sum[:keys, cols] += dot(probs.astype(BF16), dout)
            dk_sum[:keys, cols] += dot(dscores, query)
            dq_ref[rows, cols] = (dot(dscores, key, TN) * scale).astype(dq_ref.dtype)
    dk_ref[...] = dk_sum[...].astype(dk_ref.dtype)
    dv_ref[...] = dv_sum[...].astype(dv_ref.dtype)


def blocks_of(rows, width, offset):
    return pl.BlockSpec((rows, width), lambda pair: (0, pair + offset))


def fixed(shape):
    return pl.BlockSpec(shape, lambda pair: (0, 0))


def kernel_params():
    return pltpu.CompilerParams(vmem_limit_bytes=48 * 2**20)


def attend(qkv, keys, values, offsets, seg_q, seg_k, pos_q, width):
    count, length = qkv.shape[0], keys.shape[0]
    hd = width // HEADS
    lanes = 2 * hd
    pairs = HEADS // 2
    return pl.pallas_call(
        functools.partial(attend_kernel, min(256, count), count == length, hd, hd**-0.5),
        grid=(pairs,),
        in_specs=[
            blocks_of(count, lanes, 0),
            blocks_of(length, lanes, offsets[0]),
            blocks_of(length, lanes, offsets[1]),
            fixed((1, count)),
            fixed((length, 1)),
            fixed((1, count)),
        ],
        out_specs=[blocks_of(count, lanes, 0), pl.BlockSpec((1, 2, count), lambda pair: (pair, 0, 0))],
        out_shape=[
            jax.ShapeDtypeStruct((count, width), BF16),
            jax.ShapeDtypeStruct((pairs, 2, count), F32),
        ],
        cost_estimate=pl.CostEstimate(
            flops=25_000_000_000, bytes_accessed=8_000_000, transcendentals=8_000_000
        ),
        compiler_params=kernel_params(),
    )(qkv, keys, values, seg_q, seg_k, pos_q)


def attend_back(qkv, keys, values, offsets, dout, lse, seg_q, seg_k, pos_q, width, kv_type):
    count, length = qkv.shape[0], keys.shape[0]
    hd = width // HEADS
    lanes = 2 * hd
    pairs = HEADS // 2
    return pl.pallas_call(
        functools.partial(attend_back_kernel, min(256, count), count == length, hd, hd**-0.5),
        grid=(pairs,),
        in_specs=[
            blocks_of(count, lanes, 0),
            blocks_of(length, lanes, offsets[0]),
            blocks_of(length, lanes, offsets[1]),
            blocks_of(count, lanes, 0),
            pl.BlockSpec((1, 2, count), lambda pair: (pair, 0, 0)),
            fixed((1, count)),
            fixed((length, 1)),
            fixed((1, count)),
        ],
        out_specs=[
            blocks_of(count, lanes, 0),
            blocks_of(length, lanes, 0),
            blocks_of(length, lanes, 0),
        ],
        out_shape=[
            jax.ShapeDtypeStruct((count, width), BF16),
            jax.ShapeDtypeStruct((length, width), kv_type),
            jax.ShapeDtypeStruct((length, width), kv_type),
        ],
        scratch_shapes=[pltpu.VMEM((length, lanes), F32)] * 2,
        cost_estimate=pl.CostEstimate(
            flops=40_000_000_000, bytes_accessed=12_000_000, transcendentals=8_000_000
        ),
        compiler_params=kernel_params(),
    )(qkv, keys, values, dout, lse, seg_q, seg_k, pos_q)


def layer_norm(hidden, gain, shift):
    mean = jnp.mean(hidden, -1, keepdims=True)
    centred = hidden - mean
    var = jnp.mean(centred * centred, -1, keepdims=True)
    rstd = lax.rsqrt(var + NORM_EPS)
    unit = centred * rstd
    return (unit * gain + shift, unit, rstd)


def norm_back(grad, unit, rstd, gain):
    dunit = grad * gain
    dhid = rstd * (
        dunit
        - jnp.mean(dunit, -1, keepdims=True)
        - unit * jnp.mean(dunit * unit, -1, keepdims=True)
    )
    return (dhid, jnp.sum(grad * unit, 0), jnp.sum(grad, 0))


def adamw(weight, first, second, grad, rate, decay):
    new_first = BETA_ONE * first + (1.0 - BETA_ONE) * grad
    new_second = BETA_TWO * second + (1.0 - BETA_TWO) * grad * grad
    first_hat = new_first / (1.0 - BETA_ONE**STEP)
    second_hat = new_second / (1.0 - BETA_TWO**STEP)
    return (
        weight - rate * (first_hat / (jnp.sqrt(second_hat) + ADAM_EPS) + decay * weight),
        new_first,
        new_second,
    )


def body(*args):
    patches, segments = args[:2]
    masters, firsts, seconds = (args[2:10], args[10:18], args[18:26])
    embed_in, pos_table, attn_qkv, attn_out, mlp_up, mlp_down, head_out, vectors = masters
    ways = lines()
    n_seq = lax.axis_size("seq")
    seq_at = lax.axis_index("seq")
    micros, group = segments.shape[0], segments.shape[2]
    length = group * n_seq
    width = attn_qkv.shape[1] // 3

    share = max(1, n_seq // micros)
    count = length // share
    mine = seq_at // share
    patches = patches.reshape(micros, PATCH, group)
    segments = segments.reshape(micros, group)
    if share == 1:
        swaps = [
            ("seq", [(source, source ^ step) for source in range(n_seq)]) for step in range(1, n_seq)
        ]
        row = jnp.zeros((n_seq, PATCH, group), BF16)
        seg = jnp.zeros((n_seq, group), jnp.int32)
        for step in range(n_seq):
            piece = lax.dynamic_index_in_dim(patches, seq_at ^ step, 0, keepdims=False)
            ids = lax.dynamic_index_in_dim(segments, seq_at ^ step, 0, keepdims=False)
            if step:
                piece = lax.ppermute(piece, *swaps[step - 1])
                ids = lax.ppermute(ids, *swaps[step - 1])
            row = lax.dynamic_update_index_in_dim(row, piece, seq_at ^ step, 0)
            seg = lax.dynamic_update_index_in_dim(seg, ids, seq_at ^ step, 0)
        row = jnp.swapaxes(row, 0, 1).reshape(PATCH, length)
        seg = seg.reshape(length)
    else:
        row = lax.all_gather(patches, "seq", axis=2, tiled=True)
        seg = lax.all_gather(segments, "seq", axis=1, tiled=True)
        row = lax.dynamic_index_in_dim(row, mine, 0, keepdims=False)
        seg = lax.dynamic_index_in_dim(seg, mine, 0, keepdims=False)
    start = (seq_at % share) * count
    part = lambda value: lax.dynamic_slice_in_dim(value, start, count, 0)

    low = lambda value: value.astype(BF16)
    outs = head_out.shape[1]
    pad = lambda value, columns: jnp.pad(value, ((0, 0), (0, columns - value.shape[1])))
    small = jnp.concatenate(
        [
            pad(low(head_out), 128),
            pad(jnp.concatenate([low(embed_in).T, low(vectors).T], axis=1), 128),
        ],
        axis=1,
    )
    shards = [low(attn_qkv), low(mlp_up), low(mlp_down).T, low(attn_out), low(pos_table).T, small]
    aligned = (lax.axis_size("dp"), n_seq) == (X * Z, 4) and width % (32 * X * Z) == 0
    if aligned:
        w_qkv, w_up, w_down, w_attn, w_pos, w_small = gather(shards, GATHER)
    else:
        w_qkv, w_up, w_down, w_attn, w_pos, w_small = [gather_rows(v, ways, False) for v in shards]
    w_head = w_small[:, :outs]
    w_pos = jnp.concatenate([w_pos, w_small[:, 128 : 128 + PATCH]], axis=1)
    gains = w_small[:, 128 + PATCH : 136 + PATCH].astype(F32).T

    at = jnp.arange(length)
    begins = jnp.zeros((length,), jnp.int32)
    for image in range(5):
        before = (seg > 0) & (seg < image) if image else seg > 0
        begins = jnp.where(seg == image, jnp.sum(before.astype(jnp.int32)), begins)
    offset = part(at - begins)
    own = part(seg)
    tokens = part(row.T)
    later = part(jnp.concatenate([row[:, 1:], jnp.zeros((PATCH, 1), BF16)], axis=1).T)
    seg_next = part(jnp.concatenate([seg[1:], jnp.zeros((1,), jnp.int32)]))
    pair = ((own == seg_next) & (own > 0)).astype(F32)[:, None]
    first = ((own > 0) & (offset == 0)).astype(F32)[:, None]
    valid = jnp.sum((own > 0).astype(jnp.int32)).astype(F32) * PATCH
    lookup = (offset[:, None] == jnp.arange(length)[None, :]).astype(BF16)
    inputs = jnp.concatenate([lookup, tokens], axis=1)
    seg_q, seg_k, pos_q = (own[None, :], seg[:, None], part(at)[None, :].astype(jnp.int32))

    h0 = dot(inputs, w_pos, NT) + (gains[6] - 1.0)
    normed, unit_one, rstd_one = layer_norm(h0, gains[0], gains[1] - 1.0)
    normed = low(normed)
    qkv = low(dot(normed, w_qkv))
    if share == 1:
        keys, values, offsets = (qkv, qkv, (HEADS // 2, HEADS))
    else:
        near = [list(range(g, g + share)) for g in range(0, n_seq, share)]
        keys = lax.all_gather(qkv[:, width:], "seq", axis=0, tiled=True, axis_index_groups=near)
        values, offsets = (keys, (0, HEADS // 2))
    attended, lse = attend(qkv, keys, values, offsets, seg_q, seg_k, pos_q, width)
    h1 = h0 + dot(attended, w_attn) + (gains[7] - 1.0)
    mixed, unit_two, rstd_two = layer_norm(h1, gains[2], gains[3] - 1.0)
    mixed = low(mixed)
    upper = dot(mixed, w_up)
    hidden = low(jax.nn.gelu(upper))
    h2 = h1 + dot(hidden, w_down, NT)
    final, unit_fin, rstd_fin = layer_norm(h2, gains[4], gains[5] - 1.0)
    final = low(final)
    out = dot(final, w_head)
    alpha = out[:, PATCH:]
    shrink = jnp.exp(-alpha)
    scaled = (later.astype(F32) - out[:, :PATCH]) * shrink
    plain = tokens.astype(F32)
    total = jnp.sum(pair * (0.5 * scaled * scaled + alpha)) + jnp.sum(first * 0.5 * plain * plain)

    dout = low(jnp.concatenate([-pair * scaled * shrink, pair * (1.0 - scaled * scaled)], axis=1))
    grad_head = dot(final, dout, TN)
    dh2, gain_fin, shift_fin = norm_back(dot(dout, w_head, NT), unit_fin, rstd_fin, gains[4])
    ddown = low(dh2)
    grad_down = dot(ddown, hidden, TN)
    _, gelu_back = jax.vjp(jax.nn.gelu, upper)
    dupper = low(gelu_back(dot(ddown, w_down))[0])
    grad_up = dot(mixed, dupper, TN)
    dnorm, gain_two, shift_two = norm_back(dot(dupper, w_up, NT), unit_two, rstd_two, gains[2])
    dh1 = dh2 + dnorm
    dattn = low(dh1)
    grad_attn = dot(attended, dattn, TN)
    dattended = low(dot(dattn, w_attn, NT))
    dquery, dkeys, dvalues = attend_back(
        qkv, keys, values, offsets, dattended, lse, seg_q, seg_k, pos_q, width,
        BF16 if share == 1 else F32,
    )
    if share > 1:
        dkeys, dvalues = (
            low(lax.psum_scatter(d, "seq", scatter_dimension=0, tiled=True, axis_index_groups=near))
            for d in (dkeys, dvalues)
        )
    dqkv = jnp.concatenate([dquery, dkeys, dvalues], axis=1)
    grad_qkv = dot(normed, dqkv, TN)
    dnorm, gain_one, shift_one = norm_back(dot(dqkv, w_qkv, NT), unit_one, rstd_one, gains[0])
    dh0 = dh1 + dnorm
    high = low(dh0)
    rest = low(dh0 - high.astype(F32))
    grad_pos = dot(high, inputs, TN)
    grad_pos = jnp.concatenate(
        [grad_pos[:, :length] + dot(rest, lookup, TN), grad_pos[:, length:]], axis=1
    )
    grad_vec = jnp.stack(
        [
            gain_one,
            shift_one,
            gain_two,
            shift_two,
            gain_fin,
            shift_fin,
            jnp.sum(dh0, 0),
            jnp.sum(dh1, 0),
        ],
        axis=1,
    )

    small = jnp.concatenate(
        [pad(grad_head, 128), pad(jnp.concatenate([grad_pos[:, length:], grad_vec], axis=1), 128)],
        axis=1,
    )
    grads = [low(grad_down), low(grad_up), low(grad_attn), low(grad_qkv), low(grad_pos[:, :length]), small]
    if aligned:
        part = jnp.zeros((3, 8, 128), F32).at[1, 0, 0].set(total).at[2, 0, 0].set(valid)
        *sums, part = reduce_all(grads, part, REDUCE)
        squares, total, valid = [jnp.sum(part[i]) for i in range(3)]
    else:
        parts = [
            scatter_rows(g.astype(F32), ways, order, F32 if g is small else BF16)
            for g, order in zip(grads, ("xy", "yx") * 3)
        ]
        squares = sum(jnp.sum(p * p) for p in parts)
        squares, total, valid = lax.psum((squares, total, valid), ("dp", "seq"))
        sums = [gather_parts(p, ways) for p in parts]
    down, up, attn, wide, table, small = sums
    pieces = [
        small[:, 128 : 128 + PATCH].T,
        table.T,
        wide,
        attn,
        up,
        down.T,
        small[:, :outs],
        small[:, 128 + PATCH : 136 + PATCH].T,
    ]
    norm = jnp.sqrt(squares) / valid
    clip = jnp.minimum(1.0, CLIP_AT / (norm + 1e-06))
    results = [
        adamw(
            masters[i],
            firsts[i],
            seconds[i],
            pieces[i] / valid * clip,
            RATE if i < 7 else VEC_RATE,
            DECAY if i < 7 else 0.0,
        )
        for i in range(8)
    ]
    return (
        total / math.log(2.0),
        valid,
        norm,
        *[r[0] for r in results],
        *[r[1] for r in results],
        *[r[2] for r in results],
    )


def solution(mesh):
    rows, columns = (P("dp", None), P(None, "dp"))
    weights = (columns, columns, rows, rows, rows, columns, rows, columns)
    in_specs = (P(None, "dp", None, "seq"), P(None, "dp", "seq")) + weights * 3
    out_specs = (P(), P(), P()) + weights * 3
    return jax.shard_map(body, mesh=mesh, in_specs=in_specs, out_specs=out_specs, check_vma=False)
```

```python
import functools
import math

import jax
import jax.numpy as jnp
from jax import lax
from jax.experimental import pallas as pl
from jax.experimental.pallas import tpu as pltpu
from jax.sharding import PartitionSpec as P

HEADS = 12
PATCH = 48
STEP = 10
RATE = 0.02
VEC_RATE = 0.15
BETA_ONE = 0.9
BETA_TWO = 0.95
ADAM_EPS = 1e-08
DECAY = 0.1
CLIP_AT = 0.01
NORM_EPS = 1e-05

F32 = jnp.float32
BF16 = jnp.bfloat16
WIRE = jnp.bfloat16
EARLY = [
    (0, 0, 1280, True),
    (0, 1280, 1024, True),
    (1, 0, 1024, False),
    (2, 0, 256, False),
]
LATE = [
    (0, 0, 1536, True),
    (0, 1536, 1536, True),
    (1, 0, 1536, True),
    (2, 0, 768, True),
    (1, 1536, 1536, False),
]
BEGIN = [
    (0, 0, 1536, "yx"),
    (0, 1536, 1536, "xy"),
    (1, 0, 1536, "yx"),
    (1, 1536, 1536, "xy"),
    (2, 0, 768, "yx"),
]
REDUCE = [
    (3, 0, 768, "xy"),
    (3, 768, 768, "yx"),
    (3, 1536, 768, "xy"),
    (4, 0, 1024, "yx"),
    (5, 0, 256, "xy"),
]
NN = (((1,), (0,)), ((), ()))
NT = (((1,), (1,)), ((), ()))
TN = (((0,), (0,)), ((), ()))


PAIR, FIRST, OFFSET, SLOT_ID = range(2 * PATCH, 2 * PATCH + 4)


def dot(left, right, dims=NN):
    return lax.dot_general(left, right, dims, preferred_element_type=F32)


def lookup_of(aux, length):
    slot = lax.broadcasted_iota(jnp.int32, (aux.shape[0], length), 1).astype(F32)
    return (slot == aux[:, OFFSET : OFFSET + 1]).astype(F32).astype(BF16)


def tokens_of(aux):
    lane = lax.broadcasted_iota(jnp.int32, aux.shape, 1)
    return jnp.where((lane >= PATCH) & (lane < 2 * PATCH), aux, 0.0).astype(BF16)


def gains_of(small):
    return small[...].astype(F32).T[:8]


def line(axis, size, count, stride):
    place = (lax.axis_index(axis) // stride) % count
    swaps = [
        (axis, [(source, source ^ (step * stride)) for source in range(size)])
        for step in range(1, count)
    ]
    return (count, place, swaps)


def lines():
    n_dp, n_seq = lax.axis_size("dp"), lax.axis_size("seq")
    n_x = 1 << ((n_dp.bit_length() - 1) // 2)
    return {
        "z": line("dp", n_dp, n_dp // n_x, n_x),
        "x": line("dp", n_dp, n_x, 1),
        "y": line("seq", n_seq, n_seq // 2, 2),
        "core": line("seq", n_seq, 2, 1),
    }


def gather_line(block, along):
    count, place, swaps = along
    others = [lax.ppermute(block, axis, swap) for axis, swap in swaps]
    if count == 2:
        first = place == 0
        return jnp.stack([jnp.where(first, block, others[0]), jnp.where(first, others[0], block)])
    whole = jnp.zeros((count,) + block.shape, block.dtype)
    for step, piece in enumerate([block] + others):
        whole = lax.dynamic_update_index_in_dim(whole, piece, place ^ step, 0)
    return whole


def scatter_line(blocks, along, dim, wire):
    count, place, swaps = along
    pick = lambda index: lax.dynamic_index_in_dim(blocks, index, dim, keepdims=False)
    arrived = [
        lax.ppermute(pick(place ^ (step + 1)).astype(wire), axis, swap)
        for step, (axis, swap) in enumerate(swaps)
    ]
    total = pick(place)
    for piece in arrived:
        total = total + piece.astype(F32)
    return total


def gather_rows(shard, ways, split_y):
    n_core, core, _ = ways["core"]
    n_y, y_at, _ = ways["y"]
    rows, columns = shard.shape
    if split_y:
        part = lax.dynamic_slice_in_dim(
            shard, (core * n_y + y_at) * (rows // (2 * n_y)), rows // (2 * n_y), 0
        )
    else:
        part = lax.dynamic_slice_in_dim(shard, core * (rows // 2), rows // 2, 0)
    part = gather_line(part, ways["z"])
    part = gather_line(part, ways["x"])
    if split_y:
        part = gather_line(part, ways["y"])
        part = gather_line(part, ways["core"])
        part = jnp.transpose(part, (3, 2, 0, 1, 4, 5))
    else:
        part = gather_line(part, ways["core"])
        part = jnp.transpose(part, (2, 1, 0, 3, 4))
    return part.reshape(-1, columns)


def scatter_rows(grad, ways, order, wire):
    n_z, n_x, n_y = ways["z"][0], ways["x"][0], ways["y"][0]
    columns = grad.shape[1]
    blocks = grad.reshape(n_z, n_x, 2, n_y, -1, columns)
    blocks = scatter_line(blocks, ways["core"], 2, wire)
    if order == "xy":
        blocks = scatter_line(blocks, ways["x"], 1, wire)
        blocks = scatter_line(blocks, ways["y"], 1, wire)
    else:
        blocks = scatter_line(blocks, ways["y"], 2, wire)
        blocks = scatter_line(blocks, ways["x"], 1, wire)
    return scatter_line(blocks, ways["z"], 0, wire)


def gather_parts(part, ways):
    part = gather_line(part, ways["y"])
    part = gather_line(part, ways["core"])
    return part.reshape(-1, part.shape[-1])


MESH=pl.DeviceIdType.MESH
X = 2
Z = 4
def here():
    d=lax.axis_index("dp"); s=lax.axis_index("seq")
    return d//X, d%X, s//2, s%2
def peer(kz,kx,ky,kc):
    z,x,y,c=here()
    return ((z^kz)*X+(x^kx), (y^ky)*2+(c^kc))
class Gather:
    def __init__(s, src, dst, sems, base, split, lo, width):
        s.src,s.dst,s.split,s.lo,s.width=src,dst,split,lo,width
        s.send,s.recv=sems; s.n=base
        s.live=[]; s.rows=src.shape[0]
        s.idx={}
    def region(s,ref,kz,kx,half,ky,local=False):
        z,x,y,c=here(); r=s.rows//2
        row=(c^half)*r
        if not local: row=row+((z^kz)*X+(x^kx))*s.rows
        row=pl.multiple_of(row,16)
        if ky is None: return ref.at[pl.ds(row,r),pl.ds(s.lo,s.width)]
        w=s.width//2
        return ref.at[pl.ds(row,r),pl.ds(pl.multiple_of(s.lo+(y^ky)*w,128),w)]
    def copy(s,key,kz,kx,ky,to,own=False):
        i=s.idx.setdefault(key,s.n)
        if i==s.n: s.n+=1
        col=ky if s.split else None
        return pltpu.make_async_remote_copy(s.region(s.src if own else s.dst,kz,kx,0,col,own),s.region(s.dst,kz,kx,0,col),s.send.at[i],s.recv.at[i],device_id=peer(*to),device_id_type=MESH)
    def start(s,*a,**k):
        s.copy(*a,**k).start(); s.live.append((a,k))
    def begin(s):
        for k in (1,2,3): s.start(("z",k),0,0,0,(k,0,0,0),own=True)
        s.start(("x",0),0,0,0,(0,1,0,0),own=True)
    def after_z(s,k):
        s.recvd(("z",k),k,0,0)
        s.start(("x",k),k,0,0,(0,1,0,0))
        if s.split: s.start(("y",k,0),k,0,0,(0,0,1,0))
        s.start(("c",k,0),k,0,0,(0,0,0,1))
    def after_x(s,k):
        s.recvd(("x",k),k,1,0)
        if s.split: s.start(("y",k,1),k,1,0,(0,0,1,0))
        s.start(("c",k,1),k,1,0,(0,0,0,1))
    def after_y(s,k,kx):
        s.recvd(("y",k,kx),k,kx,1)
        s.start(("d",k,kx),k,kx,1,(0,0,0,1))
    def recvd(s,key,kz,kx,ky):
        s.copy(key,kz,kx,ky,(0,0,0,1)).wait_recv()
    def stage_z(s):
        for k in (1,2,3): s.after_z(k)
    def stage_x(s):
        for k in range(4): s.after_x(k)
    def stage_y(s):
        if s.split:
            for kx in range(2):
                for k in range(4):
                    if k or kx: s.after_y(k,kx)
    def finish(s):
        for k in range(4):
            for kx in range(2):
                if (k or kx):
                    s.core_recv(("c",k,kx),k,kx,0)
                    if s.split: s.core_recv(("d",k,kx),k,kx,1)
        for a,k in s.live: s.copy(*a,**k).wait_send()
    def core_recv(s,key,kz,kx,ky):
        i=s.idx[key]; col=ky if s.split else None
        r=s.region(s.dst,kz,kx,1,col)
        pltpu.make_async_remote_copy(r,r,s.send.at[i],s.recv.at[i],device_id=peer(0,0,0,1),device_id_type=MESH).wait_recv()

def greet(peers):
    bar=pltpu.get_barrier_semaphore()
    for p in peers: pl.semaphore_signal(bar,inc=1,device_id=peer(*p),device_id_type=MESH)
    pl.semaphore_wait(bar,len(peers))
PEERS=[(1,0,0,0),(2,0,0,0),(3,0,0,0),(0,1,0,0),(0,0,1,0),(0,0,0,1)]
class Own:
    def __init__(s,*refs): s.refs=refs
    def copy(s):
        src,dst,sem=s.refs
        z,x,y,c=here(); r=src.shape[0]
        return pltpu.make_async_copy(src,dst.at[pl.ds(pl.multiple_of((z*X+x)*r,16),r),:],sem)
    def start(s): s.copy().start()
    def wait(s): s.copy().wait()
def open_chunks(chunks,src,dst,send,recv,loc):
    mine=[Own(src[i],dst[i],loc.at[i]) for i in range(len(src))]
    g=[]; base=0
    for (t,lo,w,sp) in chunks:
        g.append(Gather(src[t],dst[t],(send,recv),base,sp,lo,w)); base+=28 if sp else 14
    return mine,g
def about_slots(row,seg):
    ids=seg[...]; length=ids.shape[1]
    slot=lax.broadcasted_iota(jnp.int32,ids.shape,1)
    begins=jnp.zeros_like(ids)
    for image in range(5):
        before=(ids>0)&(ids<image) if image else ids>0
        begins=jnp.where(ids==image,jnp.sum(before.astype(F32),axis=1,keepdims=True).astype(jnp.int32),begins)
    offset=slot-begins
    after=jnp.where(slot==length-1,0,pltpu.roll(ids,length-1,1))
    pair=((ids==after)&(ids>0)).astype(F32)
    first=((ids>0)&(offset==0)).astype(F32)
    x=row[...].astype(F32)
    later=jnp.where(lax.broadcasted_iota(jnp.int32,x.shape,1)==length-1,0.0,pltpu.roll(x,length-1,1))
    line=lax.broadcasted_iota(jnp.int32,(128-2*PATCH,length),0)
    more=jnp.zeros(line.shape,F32)
    for i,v in enumerate((pair,first,offset.astype(F32),ids.astype(F32))): more=jnp.where(line==i,v,more)
    return jnp.concatenate([later,x,more],axis=0).T
def gather_kernel(chunks,n,ahead,*refs):
    src,(pieces,ids)=refs[:n],refs[n:n+2]
    dst,(aux,seg_row,count)=refs[n+2:2*n+2],refs[2*n+2:2*n+5]
    send,recv,loc,psend,precv,row,seg=refs[2*n+5:]
    greet(PEERS+[(0,0,1,1)])
    q=lax.axis_index("seq"); group=pieces.shape[2]
    mine,g=open_chunks(chunks,src,dst,send,recv,loc)
    m=len(g)
    swaps=[]
    at=pl.ds(pl.multiple_of(q*group,128),group)
    for k,to in ((1,(0,0,0,1)),(2,(0,0,1,0)),(3,(0,0,1,1))):
        for j,(a,b) in enumerate(((pieces.at[q^k],row.at[:,at]),(ids.at[q^k],seg.at[:,at]))):
            i=2*(k-1)+j
            swaps.append(pltpu.make_async_remote_copy(a,b,psend.at[i],precv.at[i],device_id=peer(*to),device_id_type=MESH))
            swaps[-1].start()
    for i in range(min(ahead,m)): g[i].begin()
    for a in mine: a.start()
    row[:,at]=pieces[q]; seg[:,at]=ids[q]
    for a in swaps: a.wait()
    aux[...]=about_slots(row,seg)
    seg_row[...]=seg[...].astype(F32)
    corner=(lax.broadcasted_iota(jnp.int32,count.shape,0)==0)&(lax.broadcasted_iota(jnp.int32,count.shape,1)==0)
    held=jnp.sum((seg[...]>0).astype(F32),axis=1,keepdims=True)
    count[...]=jnp.where(corner,held*PATCH,0.0)
    for s in range(m+2):
        if s<m:
            g[s].stage_z()
            if s+ahead<m: g[s+ahead].begin()
        if 0<=s-1<m: g[s-1].stage_x()
        if 0<=s-2<m: g[s-2].stage_y()
    for a in g: a.finish()
    for a in mine: a.wait()
def semaphores(chunks,n):
    tot=sum(28 if s[3] else 14 for s in chunks)
    return [pltpu.SemaphoreType.DMA((tot,)),pltpu.SemaphoreType.DMA((tot,)),pltpu.SemaphoreType.DMA((n,))]
def gather(shards,pieces,ids,chunks,ahead=2,cid=1):
    n=len(shards); dp,sq=lax.axis_size("dp"),lax.axis_size("seq")
    anyspec=pl.BlockSpec(memory_space=pl.ANY); vm=pl.BlockSpec(memory_space=pltpu.VMEM)
    group=pieces.shape[2]; length=group*sq
    return pl.pallas_call(functools.partial(gather_kernel,chunks,n,ahead),
      out_shape=[jax.ShapeDtypeStruct((s.shape[0]*dp,s.shape[1]),s.dtype) for s in shards]
      +[jax.ShapeDtypeStruct((length,128),F32),jax.ShapeDtypeStruct((1,length),F32),jax.ShapeDtypeStruct((8,128),F32)],
      in_specs=[vm]*(n+2),out_specs=[anyspec]*n+[vm]*3,
      scratch_shapes=semaphores(chunks,n)+[pltpu.SemaphoreType.DMA((6,)),pltpu.SemaphoreType.DMA((6,)),
        pltpu.VMEM((pieces.shape[1],length),pieces.dtype),pltpu.VMEM((1,length),ids.dtype)],
      compiler_params=pltpu.CompilerParams(collective_id=cid,has_side_effects=True,vmem_limit_bytes=32*2**20))(*shards,pieces,ids[:,None,:])
PER=8
class Reduce:
    def __init__(s,g,out,kept,bufs,sems,base,lo,w,order):
        s.g,s.out,s.kept,s.lo,s.w,s.order=g,out,kept,lo,w,order
        if g is None: s.p4,s.r4=bufs
        elif kept is None: s.r1,s.p2,s.r2,s.p3,s.r3,s.p4,s.r4=bufs
        else: s.gc,s.r1,s.p2,s.r2,s.p3,s.r3=bufs
        s.send,s.recv,s.loc=sems; s.base=base; s.r=(kept.shape[1] if g is None else g.shape[3])
    def col(s,ky,lo=0):
        z,x,y,c=here(); h=s.w//2
        return pl.ds(pl.multiple_of(lo+(y^ky)*h,128),h)
    def remote(s,src,dst,i,to):
        return pltpu.make_async_remote_copy(src,dst,s.send.at[s.base+i],s.recv.at[s.base+i],device_id=peer(*to),device_id_type=MESH)
    def load(s):
        z,x,y,c=here()
        return pltpu.make_async_copy(s.g.at[:,:,c,:,pl.ds(s.lo,s.w)],s.gc,s.loc)
    def c1(s):
        z,x,y,c=here()
        return s.remote(s.g.at[:,:,1-c,:,pl.ds(s.lo,s.w)],s.r1,0,(0,0,0,1))
    def begin(s):
        if s.kept is not None: s.load().start()
        s.c1().start()
    def two(s,zz,xx,ky=None):
        z,x,y,c=here()
        cols=slice(None) if ky is None else s.col(ky)
        if s.kept is not None: own=s.gc[zz,xx,:,cols]
        else: own=s.g[zz,xx,c,:,pl.ds(s.lo,s.w) if ky is None else s.col(ky,s.lo)]
        return own.astype(F32)+s.r1[zz,xx,:,cols].astype(F32)
    def three(s,zz,xx,ky):
        z,x,y,c=here()
        if s.order=="xy": return s.two(zz,xx,ky)+s.r2[zz,:,s.col(ky)].astype(F32)
        return s.two(zz,xx,ky)+s.r2[zz,xx].astype(F32)
    def half(s):
        return pl.ds(s.lo//2,s.w//2)
    def four(s,zz):
        z,x,y,c=here()
        if s.g is None: return s.kept[zz,:,s.half()]
        return s.three(zz,x,0)+s.r3[zz].astype(F32)
    def c2(s): return s.remote(s.p2,s.r2,1,(0,1,0,0) if s.order=="xy" else (0,0,1,0))
    def c3(s): return s.remote(s.p3,s.r3,2,(0,0,1,0) if s.order=="xy" else (0,1,0,0))
    def c4(s,k): return s.remote(s.p4.at[k-1],s.r4.at[k-1],2+k,(k,0,0,0))
    def c5(s):
        z,x,y,c=here()
        ref=s.out.at[pl.ds(pl.multiple_of(c*s.r,8),s.r),s.col(0,s.lo)]
        return s.remote(ref,ref,6,(0,0,1,0))
    def c6(s):
        z,x,y,c=here()
        ref=s.out.at[pl.ds(pl.multiple_of(c*s.r,8),s.r),pl.ds(s.lo,s.w)]
        return s.remote(ref,ref,7,(0,0,0,1))
    def stage1(s):
        z,x,y,c=here()
        if s.kept is not None: s.load().wait()
        s.c1().wait_recv()
        @pl.loop(0,Z)
        def _(zz):
            if s.order=="xy":
                s.p2[zz]=s.two(zz,1-x).astype(s.p2.dtype)
            else:
                for xx in range(X): s.p2[zz,xx]=s.two(zz,xx,1).astype(s.p2.dtype)
        s.c2().start()
    def stage2(s):
        z,x,y,c=here()
        s.c2().wait_recv()
        @pl.loop(0,Z)
        def _(zz):
            s.p3[zz]=(s.three(zz,x,1) if s.order=="xy" else s.three(zz,1-x,0)).astype(s.p3.dtype)
        s.c3().start()
    def keep(s):
        s.c3().wait_recv()
        z,x,y,c=here()
        @pl.loop(0,Z)
        def _(zz):
            s.kept[zz,:,s.half()]=s.three(zz,x,0)+s.r3[zz].astype(F32)
        s.c1().wait_send(); s.c2().wait_send(); s.c3().wait_send()
    def stage3(s):
        z,x,y,c=here()
        if s.g is not None: s.c3().wait_recv()
        for k in (1,2,3):
            s.p4[k-1]=s.four(z^k).astype(s.p4.dtype)
            s.c4(k).start()
    def stage4(s):
        z,x,y,c=here()
        total=s.four(z)
        for k in (1,2,3):
            s.c4(k).wait_recv()
            total=total+s.r4[k-1].astype(F32)
        s.out[pl.ds(pl.multiple_of(c*s.r,8),s.r),s.col(0,s.lo)]=total
        s.c5().start()
        return total
    def stage5(s):
        s.c5().wait_recv()
        s.c6().start()
    def finish(s):
        s.c6().wait_recv()
        if s.g is not None:
            s.c1().wait_send(); s.c2().wait_send(); s.c3().wait_send()
        for k in (1,2,3): s.c4(k).wait_send()
        s.c5().wait_send(); s.c6().wait_send()

def shapes(r,w,order,dt,first=True,last=True):
    h=w//2
    two=(Z,r,w) if order=="xy" else (Z,X,r,h)
    head=[((Z,X,r,w),dt)]+[(two,dt)]*2+[((Z,r,h),dt)]*2
    if not last: head=head[:1]+head
    return (head if first else [])+([((3,r,h),dt)]*2 if last else [])

def totals(part,got,send,recv,base):
    d=lax.axis_index("dp"); q=lax.axis_index("seq")
    def hop(first,count,mine,peers):
        got[first+mine]=part[...]
        cs=[pltpu.make_async_remote_copy(part,got.at[first+mine],send.at[base+first+i],recv.at[base+first+i],device_id=p,device_id_type=MESH) for i,p in enumerate(peers)]
        for k in cs: k.start()
        for k in cs: k.wait()
        t=got[first]
        for i in range(1,count): t=t+got[first+i]
        part[...]=t
    hop(0,4,q,[peer(0,0,ky,kc) for ky,kc in ((0,1),(1,0),(1,1))])
    hop(4,8,d,[peer(kz,kx,0,0) for kz,kx in ((0,1),(1,0),(1,1),(2,0),(2,1),(3,0),(3,1))])

ALL=[(0,0,ky,kc) for ky,kc in ((0,1),(1,0),(1,1))]+[(kz,kx,0,0) for kz,kx in ((0,1),(1,0),(1,1),(2,0),(2,1),(3,0),(3,1))]
def fold(v):
    v=v*v
    t=jnp.zeros((8,128),F32)
    for i in range(v.shape[0]//8):
        for j in range(v.shape[1]//128):
            t=t+v[8*i:8*i+8,128*j:128*j+128]
    return t


def hide(bias, tile, skip, sq_ref, sk, qp_ref):
    for step in range(bias.shape[1] // tile):
        rows = slice(step * tile, (step + 1) * tile)
        keys = (step + 1) * tile if skip else bias.shape[0]
        pos_key = lax.broadcasted_iota(jnp.int32, (keys, tile), 0)
        allowed = (sk[:keys, :] == sq_ref[:, rows]) & (pos_key <= qp_ref[:, rows])
        bias[:keys, rows] = jnp.where(allowed, 0.0, -1e30)


def head_forward(tile, skip, hd, scale, q_ref, k_ref, v_ref, bias, o_ref, lse_ref):
    length = k_ref.shape[0]
    for head in range(q_ref.shape[1] // hd):
        cols = slice(hd * head, hd * head + hd)
        for step in range(q_ref.shape[0] // tile):
            rows = slice(step * tile, (step + 1) * tile)
            keys = (step + 1) * tile if skip else length
            query = (q_ref[rows, cols].astype(F32) * scale).astype(BF16)
            scores = dot(k_ref[:keys, cols], query, NT) + bias[:keys, rows]
            top = jnp.max(scores, 0, keepdims=True)
            weight = jnp.exp(scores - top)
            total = jnp.sum(weight, 0, keepdims=True)
            probs = (weight * (1.0 / total)).astype(BF16)
            o_ref[rows, cols] = dot(probs, v_ref[:keys, cols], TN).astype(BF16)
            lse_ref[0, head : head + 1, rows] = top + jnp.log(total)


def attend_kernel(tile, skip, hd, scale, q_ref, k_ref, v_ref, sq_ref, sk_ref, qp_ref, o_ref, lse_ref, bias):
    @pl.when(pl.program_id(0) == 0)
    def _():
        hide(bias, tile, skip, sq_ref, sk_ref, qp_ref)

    head_forward(tile, skip, hd, scale, q_ref, k_ref, v_ref, bias, o_ref, lse_ref)


def front_kernel(
    tiles, lanes, shape, chunks, n, aux_ref, slots_ref, sq_ref, qp_ref, wp_ref, ws_ref, wq_ref, *refs,
):
    src, (h0_ref, normed_ref, qkv_ref, o_ref, lse_ref) = refs[:n], refs[n : n + 5]
    dst, (qkv, bias, gains_all) = refs[n + 5 : 2 * n + 5], refs[2 * n + 5 : 2 * n + 8]
    send, recv, loc = refs[2 * n + 8 :]
    step = pl.program_id(0)
    mine, g = open_chunks(chunks, src, dst, send, recv, loc)

    def when(index, *stages):
        @pl.when(step == index)
        def _():
            for stage in stages:
                stage()

    def begin():
        greet(PEERS)
        for a in g[:2]:
            a.begin()
        for a in mine:
            a.start()
        gains_all[...] = gains_of(ws_ref)

    when(0, begin)
    when(3, g[0].stage_z, g[2].begin)
    when(4, g[1].stage_z, g[3].begin, g[0].stage_x)
    when(6, g[2].stage_z, g[4].begin, g[1].stage_x)
    when(7, g[0].stage_y, g[3].stage_z)
    when(8, g[2].stage_x, g[1].stage_y)
    when(9, g[3].stage_x, g[4].stage_z)

    @pl.when(step < tiles)
    def _():
        tile, length = h0_ref.shape[0], wp_ref.shape[1]
        aux = aux_ref[...]
        gains = gains_all[...]
        h0 = dot(lookup_of(aux, length), wp_ref[...], NT) + dot(tokens_of(aux), ws_ref[...], NT)
        h0 = h0 + (gains[6:7] - 1.0)
        h0_ref[...] = h0
        unit, _ = norm_rows(h0)
        normed = (unit * gains[0:1] + (gains[1:2] - 1.0)).astype(BF16)
        normed_ref[...] = normed
        rows = pl.ds(pl.multiple_of(jnp.minimum(step, tiles - 1) * tile, tile), tile)
        value = dot(normed, wq_ref[...]).astype(BF16)
        qkv_ref[...] = value
        qkv[rows, :] = value

    @pl.when(step >= tiles)
    def _():
        pair = step - tiles
        width = qkv.shape[1] // 3

        @pl.when(pair == 0)
        def _():
            hide(bias, *shape[:2], sq_ref, slots_ref[:, SLOT_ID : SLOT_ID + 1], qp_ref)

        part = lambda i: qkv.at[:, pl.ds(pl.multiple_of(i * width + pair * lanes, lanes), lanes)]
        head_forward(*shape, part(0), part(1), part(2), bias, o_ref, lse_ref)

    def drain():
        g[2].stage_y()
        g[4].stage_x()
        g[3].stage_y()
        g[4].stage_y()
        for a in g:
            a.finish()
        for a in mine:
            a.wait()

    when(pl.num_programs(0) - 1, drain)


def front(aux, seg_q, pos_q, w_pos, w_small, w_qkv, shards, chunks):
    count, width, dp = aux.shape[0], w_pos.shape[0], lax.axis_size("dp")
    hd = width // HEADS
    lanes, pairs, tile = 2 * hd, HEADS // 2, 256
    tiles, n = count // tile, len(shards)
    once = lambda shape: pl.BlockSpec(shape, lambda i: (0, 0), pipeline_mode=pl.Buffered(1))
    row = lambda columns: pl.BlockSpec((tile, columns), lambda i: (jnp.minimum(i, tiles - 1), 0))
    late = lambda i: jnp.maximum(i - tiles, 0)
    return pl.pallas_call(
        functools.partial(front_kernel, tiles, lanes, (tile, True, hd, hd**-0.5), chunks, n),
        grid=(tiles + pairs,),
        in_specs=[
            row(128),
            once((count, 128)),
            once((1, count)),
            once((1, count)),
            once(w_pos.shape),
            pl.BlockSpec((width, 128), lambda i: (0, 1), pipeline_mode=pl.Buffered(1)),
            once(w_qkv.shape),
            *[once(v.shape) for v in shards],
        ],
        out_specs=[
            row(width),
            row(width),
            row(3 * width),
            pl.BlockSpec((count, lanes), lambda i: (0, late(i))),
            pl.BlockSpec((1, 2, count), lambda i: (late(i), 0, 0)),
        ]
        + [pl.BlockSpec(memory_space=pl.ANY)] * n,
        out_shape=[
            jax.ShapeDtypeStruct((count, width), F32),
            jax.ShapeDtypeStruct((count, width), BF16),
            jax.ShapeDtypeStruct((count, 3 * width), BF16),
            jax.ShapeDtypeStruct((count, width), BF16),
            jax.ShapeDtypeStruct((pairs, 2, count), F32),
        ]
        + [jax.ShapeDtypeStruct((v.shape[0] * dp, v.shape[1]), v.dtype) for v in shards],
        scratch_shapes=[
            pltpu.VMEM((count, 3 * width), BF16),
            pltpu.VMEM((count, count), F32),
            pltpu.VMEM((8, width), F32),
        ]
        + semaphores(chunks, n),
        compiler_params=pltpu.CompilerParams(
            collective_id=4, has_side_effects=True, vmem_limit_bytes=60 * 2**20
        ),
    )(aux, aux, seg_q, pos_q, w_pos, w_small, w_qkv, *shards)


def head_back(
    tile, skip, hd, scale, q_ref, k_ref, v_ref, do_ref, lse_ref, bias, dq_ref, dk_ref, dv_ref,
    dk_sum, dv_sum,
):
    length = k_ref.shape[0]
    dk_sum[...] = jnp.zeros_like(dk_sum)
    dv_sum[...] = jnp.zeros_like(dv_sum)
    for head in range(q_ref.shape[1] // hd):
        cols = slice(hd * head, hd * head + hd)
        for step in range(q_ref.shape[0] // tile):
            rows = slice(step * tile, (step + 1) * tile)
            keys = (step + 1) * tile if skip else length
            query = (q_ref[rows, cols].astype(F32) * scale).astype(BF16)
            key = k_ref[:keys, cols]
            dout = do_ref[rows, cols]
            scores = dot(key, query, NT) + bias[:keys, rows]
            probs = jnp.exp(scores - lse_ref[0, head : head + 1, rows])
            dprobs = dot(v_ref[:keys, cols], dout, NT)
            delta = jnp.sum(dprobs * probs, 0, keepdims=True)
            dscores = (probs * (dprobs - delta)).astype(BF16)
            dv_sum[:keys, cols] += dot(probs.astype(BF16), dout)
            dk_sum[:keys, cols] += dot(dscores, query)
            dq_ref[rows, cols] = (dot(dscores, key, TN) * scale).astype(dq_ref.dtype)
    dk_ref[...] = dk_sum[...].astype(dk_ref.dtype)
    dv_ref[...] = dv_sum[...].astype(dv_ref.dtype)


def attend_back_kernel(shape, chunks, n, *refs):
    ins, grads = refs[:8], refs[8 : 8 + n]
    outs, kept = refs[8 + n : 11 + n], refs[11 + n : 11 + 2 * n]
    sums, bias, rest = refs[11 + 2 * n : 13 + 2 * n], refs[13 + 2 * n], refs[14 + 2 * n :]
    sq_ref, sk_ref, qp_ref = ins[5:]

    @pl.when(pl.program_id(0) == 0)
    def _():
        hide(bias, *shape[:2], sq_ref, sk_ref, qp_ref)

    if chunks:
        send, recv, loc = rest[-3:]
        R = [
            Reduce(grads[t], None, kept[t], rest[6 * i : 6 * i + 6], (send, recv, loc.at[i]), PER * i, lo, w, o)
            for i, (t, lo, w, o) in enumerate(chunks)
        ]
        pair = pl.program_id(0)

        @pl.when(pair == 0)
        def _():
            greet(PEERS)
            for a in R:
                a.begin()

        @pl.when(pair == 1)
        def _():
            for a in R[:2]:
                a.stage1()

        @pl.when(pair == 2)
        def _():
            for a in R[2:]:
                a.stage1()

        @pl.when(pair == 4)
        def _():
            for a in R[:2]:
                a.stage2()

    head_back(*shape, *ins[:5], bias, *outs, *sums)
    if chunks:

        @pl.when(pair == pl.num_programs(0) - 1)
        def _():
            for a in R[2:]:
                a.stage2()
            for a in R:
                a.keep()


def blocks_of(rows, width, offset):
    return pl.BlockSpec((rows, width), lambda pair: (0, pair + offset))


def fixed(shape):
    return pl.BlockSpec(shape, lambda pair: (0, 0))


def kernel_params():
    return pltpu.CompilerParams(vmem_limit_bytes=48 * 2**20)


def attend(qkv, keys, values, offsets, seg_q, seg_k, pos_q, width):
    count, length = qkv.shape[0], keys.shape[0]
    hd = width // HEADS
    lanes = 2 * hd
    pairs = HEADS // 2
    return pl.pallas_call(
        functools.partial(attend_kernel, min(256, count), count == length, hd, hd**-0.5),
        grid=(pairs,),
        in_specs=[
            blocks_of(count, lanes, 0),
            blocks_of(length, lanes, offsets[0]),
            blocks_of(length, lanes, offsets[1]),
            fixed((1, count)),
            fixed((length, 1)),
            fixed((1, count)),
        ],
        out_specs=[blocks_of(count, lanes, 0), pl.BlockSpec((1, 2, count), lambda pair: (pair, 0, 0))],
        out_shape=[
            jax.ShapeDtypeStruct((count, width), BF16),
            jax.ShapeDtypeStruct((pairs, 2, count), F32),
        ],
        scratch_shapes=[pltpu.VMEM((length, count), F32)],
        cost_estimate=pl.CostEstimate(
            flops=25_000_000_000, bytes_accessed=8_000_000, transcendentals=8_000_000
        ),
        compiler_params=kernel_params(),
    )(qkv, keys, values, seg_q, seg_k, pos_q)


def attend_back(qkv, keys, values, offsets, dout, lse, seg_q, seg_k, pos_q, width, kv_type, grads, chunks):
    count, length = qkv.shape[0], keys.shape[0]
    hd = width // HEADS
    lanes = 2 * hd
    pairs = HEADS // 2
    rows, extra, blocks = (0, [], [])
    if chunks:
        rows = width // (2 * X * Z)
        blocks = [g.reshape(Z, X, 2, rows, -1) for g in grads]
        extra = [
            pltpu.VMEM(*b)
            for (t, lo, w, o) in chunks
            for b in shapes(rows, w, o, grads[t].dtype, last=False)
        ]
        count_of = len(chunks)
        extra += [
            pltpu.SemaphoreType.DMA((PER * count_of,)),
            pltpu.SemaphoreType.DMA((PER * count_of,)),
            pltpu.SemaphoreType.DMA((count_of,)),
        ]
    return pl.pallas_call(
        functools.partial(
            attend_back_kernel,
            (min(256, count), count == length, hd, hd**-0.5),
            chunks,
            len(grads),
        ),
        grid=(pairs,),
        in_specs=[
            blocks_of(count, lanes, 0),
            blocks_of(length, lanes, offsets[0]),
            blocks_of(length, lanes, offsets[1]),
            blocks_of(count, lanes, 0),
            pl.BlockSpec((1, 2, count), lambda pair: (pair, 0, 0)),
            fixed((1, count)),
            fixed((length, 1)),
            fixed((1, count)),
        ]
        + [pl.BlockSpec(memory_space=pl.ANY)] * len(grads),
        out_specs=[
            blocks_of(count, lanes, 0),
            blocks_of(length, lanes, 0),
            blocks_of(length, lanes, 0),
        ]
        + [pl.BlockSpec((Z, rows, g.shape[1] // 2), lambda pair: (0, 0, 0)) for g in grads],
        out_shape=[
            jax.ShapeDtypeStruct((count, width), BF16),
            jax.ShapeDtypeStruct((length, width), kv_type),
            jax.ShapeDtypeStruct((length, width), kv_type),
        ]
        + [jax.ShapeDtypeStruct((Z, rows, g.shape[1] // 2), F32) for g in grads],
        scratch_shapes=[pltpu.VMEM((length, lanes), F32)] * 2
        + [pltpu.VMEM((length, count), F32)]
        + extra,
        cost_estimate=pl.CostEstimate(
            flops=40_000_000_000, bytes_accessed=12_000_000, transcendentals=8_000_000
        ),
        compiler_params=pltpu.CompilerParams(
            vmem_limit_bytes=60 * 2**20,
            **(dict(collective_id=3, has_side_effects=True) if chunks else {}),
        ),
    )(qkv, keys, values, dout, lse, seg_q, seg_k, pos_q, *blocks)


def layer_norm(hidden, gain, shift):
    mean = jnp.mean(hidden, -1, keepdims=True)
    centred = hidden - mean
    var = jnp.mean(centred * centred, -1, keepdims=True)
    rstd = lax.rsqrt(var + NORM_EPS)
    unit = centred * rstd
    return (unit * gain + shift, unit, rstd)


def norm_back(grad, unit, rstd, gain):
    dunit = grad * gain
    dhid = rstd * (
        dunit
        - jnp.mean(dunit, -1, keepdims=True)
        - unit * jnp.mean(dunit * unit, -1, keepdims=True)
    )
    return (dhid, jnp.sum(grad * unit, 0), jnp.sum(grad, 0))


def adamw(weight, first, second, grad, rate, decay):
    new_first = BETA_ONE * first + (1.0 - BETA_ONE) * grad
    new_second = BETA_TWO * second + (1.0 - BETA_TWO) * grad * grad
    first_hat = new_first / (1.0 - BETA_ONE**STEP)
    second_hat = new_second / (1.0 - BETA_TWO**STEP)
    return (
        weight - rate * (first_hat / (jnp.sqrt(second_hat) + ADAM_EPS) + decay * weight),
        new_first,
        new_second,
    )


def norm_rows(hidden):
    mean = jnp.mean(hidden, -1, keepdims=True)
    centred = hidden - mean
    rstd = lax.rsqrt(jnp.mean(centred * centred, -1, keepdims=True) + NORM_EPS)
    return centred * rstd, rstd


def norm_rows_back(grad, unit, rstd, gain):
    dunit = grad * gain
    return rstd * (
        dunit
        - jnp.mean(dunit, -1, keepdims=True)
        - unit * jnp.mean(dunit * unit, -1, keepdims=True)
    )


def add_rows(ref, row, value):
    ref[row : row + 1, :] += jnp.sum(value, 0, keepdims=True)


GELU_A = math.sqrt(2.0 / math.pi)
GELU_B = 0.044715


def mlp_kernel(
    tiles, wide, o_ref, h0_ref, aux_ref, ws_ref, wa_ref, wu_ref, wd_ref, wh_ref,
    do_ref, dh1_ref, gdown_ref, gup_ref, gattn_ref, ghead_ref, sums_ref, loss_ref,
    m_all, hid_all, dd_all, du_all, o_all, dat_all, fin_all, dout_all, slope, gains_all,
):
    step = pl.program_id(0)
    tile, width = h0_ref.shape
    blocks = [slice(j, j + wide) for j in range(0, wu_ref.shape[1], wide)]
    rows = pl.ds(pl.multiple_of(jnp.minimum(step, tiles - 1) * tile, tile), tile)

    @pl.when(step == 0)
    def _():
        gains_all[...] = gains_of(ws_ref)
        sums_ref[...] = jnp.zeros_like(sums_ref)
        loss_ref[...] = jnp.zeros_like(loss_ref)

    @pl.when(step < tiles)
    def _():
        gains = gains_all[...]
        o = o_ref[...]
        o_all[rows, :] = o
        h1 = h0_ref[...] + dot(o, wa_ref[...]) + (gains[7:8] - 1.0)
        unit_two, rstd_two = norm_rows(h1)
        m = (unit_two * gains[2:3] + (gains[3:4] - 1.0)).astype(BF16)
        m_all[rows, :] = m
        h2 = h1
        for b in blocks:
            u = dot(m, wu_ref[:, b])
            square = u * u
            th = jnp.tanh(GELU_A * (u + GELU_B * (square * u)))
            hid = (0.5 * u * (1.0 + th)).astype(BF16)
            slope[:, b] = 0.5 * (1.0 + th) + (0.5 * u) * (1.0 - th * th) * (
                GELU_A * (1.0 + (3.0 * GELU_B) * square)
            )
            hid_all[rows, b] = hid
            h2 = h2 + dot(hid, wd_ref[:, b], NT)
        unit_fin, rstd_fin = norm_rows(h2)
        final = (unit_fin * gains[4:5] + (gains[5:6] - 1.0)).astype(BF16)
        fin_all[rows, :] = final
        out = dot(final, wh_ref[...])
        aux = aux_ref[...]
        lane = lax.broadcasted_iota(jnp.int32, out.shape, 1)
        used = lane < PATCH
        pair, first = aux[:, PAIR : PAIR + 1], aux[:, FIRST : FIRST + 1]
        alpha = jnp.where(used, pltpu.roll(out, 128 - PATCH, 1), 0.0)
        plain = jnp.where(used, pltpu.roll(aux, 128 - PATCH, 1), 0.0)
        shrink = jnp.exp(-alpha)
        scaled = jnp.where(used, aux - out, 0.0) * shrink
        term = pair * (0.5 * scaled * scaled + alpha) + first * (0.5 * plain * plain)
        loss_ref[...] += jnp.sum(term.reshape(tile // 8, 8, 128), 0)
        dmu = -pair * scaled * shrink
        dalpha = pltpu.roll(jnp.where(used, pair * (1.0 - scaled * scaled), 0.0), PATCH, 1)
        dout = jnp.where(used, dmu, dalpha).astype(BF16)
        dout_all[rows, :] = dout
        dfinal = dot(dout, wh_ref[...], NT)
        add_rows(sums_ref, 4, dfinal * unit_fin)
        add_rows(sums_ref, 5, dfinal)
        dh2 = norm_rows_back(dfinal, unit_fin, rstd_fin, gains[4:5])
        dd = dh2.astype(BF16)
        dd_all[rows, :] = dd
        dmixed = jnp.zeros((tile, width), F32)
        for b in blocks:
            du = (dot(dd, wd_ref[:, b]) * slope[:, b]).astype(BF16)
            du_all[rows, b] = du
            dmixed = dmixed + dot(du, wu_ref[:, b], NT)
        add_rows(sums_ref, 2, dmixed * unit_two)
        add_rows(sums_ref, 3, dmixed)
        dh1 = dh2 + norm_rows_back(dmixed, unit_two, rstd_two, gains[2:3])
        add_rows(sums_ref, 7, dh1)
        dh1_ref[...] = dh1
        dat = dh1.astype(BF16)
        dat_all[rows, :] = dat
        do_ref[...] = dot(dat, wa_ref[...], NT).astype(BF16)

    @pl.when(step >= tiles)
    def _():
        cols = pl.ds(pl.multiple_of((step - tiles) * wide, wide), wide)
        gdown_ref[...] = dot(dd_all[...], hid_all[:, cols], TN).astype(BF16)
        gup_ref[...] = dot(m_all[...], du_all[:, cols], TN).astype(BF16)

    @pl.when(step == tiles)
    def _():
        gattn_ref[...] = dot(o_all[...], dat_all[...], TN).astype(BF16)
        ghead_ref[...] = dot(fin_all[...], dout_all[...], TN)


def mlp(o, h0, aux, w_small, w_attn, w_up, w_down):
    count, width = h0.shape
    deep = w_up.shape[1]
    tile, wide = min(256, count), width
    tiles, parts = count // tile, deep // wide
    row = lambda columns: pl.BlockSpec((tile, columns), lambda i: (jnp.minimum(i, tiles - 1), 0))
    column = pl.BlockSpec((width, wide), lambda i: (0, jnp.maximum(i - tiles, 0)))
    once = lambda shape: pl.BlockSpec(shape, lambda i: (0, 0), pipeline_mode=pl.Buffered(1))
    keep = lambda columns: pltpu.VMEM((count, columns), BF16)
    return pl.pallas_call(
        functools.partial(mlp_kernel, tiles, wide),
        grid=(tiles + parts,),
        in_specs=[
            row(width),
            row(width),
            row(128),
            pl.BlockSpec((width, 128), lambda i: (0, 1), pipeline_mode=pl.Buffered(1)),
            once((width, width)),
            once((width, deep)),
            once((width, deep)),
            once((width, 128)),
        ],
        out_specs=[
            row(width),
            row(width),
            column,
            column,
            once((width, width)),
            once((width, 128)),
            once((8, width)),
            once((8, 128)),
        ],
        out_shape=[
            jax.ShapeDtypeStruct((count, width), BF16),
            jax.ShapeDtypeStruct((count, width), F32),
            jax.ShapeDtypeStruct((width, deep), BF16),
            jax.ShapeDtypeStruct((width, deep), BF16),
            jax.ShapeDtypeStruct((width, width), BF16),
            jax.ShapeDtypeStruct((width, 128), F32),
            jax.ShapeDtypeStruct((8, width), F32),
            jax.ShapeDtypeStruct((8, 128), F32),
        ],
        scratch_shapes=[
            keep(width), keep(deep), keep(width), keep(deep), keep(width), keep(width), keep(width),
            keep(128), pltpu.VMEM((tile, deep), F32), pltpu.VMEM((8, width), F32),
        ],
        cost_estimate=pl.CostEstimate(
            flops=36_000_000_000, bytes_accessed=40_000_000, transcendentals=4_000_000
        ),
        compiler_params=pltpu.CompilerParams(vmem_limit_bytes=60 * 2**20),
    )(o, h0, aux, w_small, w_attn, w_up, w_down, w_small)


def back_kernel(
    tiles, begun, chunks, counts, h0_ref, dh1_ref, aux_ref, slots_ref, normed_ref, dq_ref, dk_ref,
    dv_ref, wq_ref, ws_ref, ghead_ref, sums_ref, loss_ref, count_ref, *refs,
):
    held, final, result = refs[:3], refs[3:9], refs[9]
    send, recv, loc, got, gains_all, vec, high, rest, g_qkv, g_pos, g_small, tot, leave = refs[-19:-6]
    out = refs[-6:]
    step = pl.program_id(0)
    sources = (None, None, None, g_qkv, g_pos, g_small)
    R, at = [], 10
    for i, (t, lo, w, o) in enumerate(begun + chunks):
        old, c = i < len(begun), counts[i]
        sems = (send, recv, loc.at[i])
        kept = held[t] if old else None
        R.append(Reduce(sources[t], out[t], kept, refs[at : at + c], sems, PER * i, lo, w, o))
        at += c
    old, new = R[: len(begun)], R[len(begun) :]
    tile, width = h0_ref.shape
    place = lambda value: value.reshape(Z, X, 2, width // (2 * X * Z), value.shape[-1])

    def last(*group):
        for a in group:
            tot[0] += fold(a.stage4())

    def when(index, *stages):
        @pl.when(step == index)
        def _():
            for stage in stages:
                stage()

    def open_all():
        greet(ALL)
        for a in old:
            a.stage3()
        gains_all[...] = gains_of(ws_ref)
        vec[...] = sums_ref[...]
        tot[0] = jnp.zeros_like(tot[0])
        tot[1] = loss_ref[...]
        tot[2] = count_ref[...]

    when(0, open_all)
    for j, d_ref in enumerate((dq_ref, dk_ref, dv_ref)):

        @pl.when(step == j)
        def _():
            value = dot(normed_ref[...], d_ref[...], TN).astype(BF16)
            g_qkv[:, :, :, :, j * width : (j + 1) * width] = place(value)
            new[j].begin()

    when(3, new[0].stage1, new[1].stage1, lambda: last(*old[:2]))
    when(4, new[2].stage1, lambda: last(*old[2:4]), old[0].stage5, old[1].stage5)
    when(5, lambda: last(*old[4:]), old[2].stage5, old[3].stage5)
    when(6, new[0].stage2, new[1].stage2, old[4].stage5)

    @pl.when((step >= 3) & (step < 3 + tiles))
    def _():
        gains = gains_all[...]
        unit, rstd = norm_rows(h0_ref[...])
        rows = pl.ds(pl.multiple_of(jnp.clip(step - 3, 0, tiles - 1) * tile, tile), tile)
        dnormed = dot(dq_ref[rows, :], wq_ref[:, :width], NT)
        dnormed = dnormed + dot(dk_ref[rows, :], wq_ref[:, width : 2 * width], NT)
        dnormed = dnormed + dot(dv_ref[rows, :], wq_ref[:, 2 * width :], NT)
        add_rows(vec, 0, dnormed * unit)
        add_rows(vec, 1, dnormed)
        dh0 = dh1_ref[...] + norm_rows_back(dnormed, unit, rstd, gains[0:1])
        add_rows(vec, 6, dh0)
        top = dh0.astype(BF16)
        high[rows, :] = top
        rest[rows, :] = (dh0 - top.astype(F32)).astype(BF16)

    @pl.when(step == 3 + tiles)
    def _():
        new[2].stage2()
        slots = slots_ref[...]
        lookup = lookup_of(slots, g_pos.shape[-1])
        top = high[...]
        g_pos[...] = place((dot(top, lookup, TN) + dot(rest[...], lookup, TN)).astype(BF16))
        new[3].begin()
        line = jnp.concatenate([vec[...], jnp.zeros((120, width), F32)], axis=0)
        both = dot(top, tokens_of(slots), TN) + line.T
        g_small[...] = place(jnp.concatenate([ghead_ref[...], both], axis=1))
        new[4].begin()
        for a in new[:2]:
            a.stage3()
        new[4].stage1()
        new[3].stage1()
        new[2].stage3()
        last(*new[:2])
        new[4].stage2()
        new[3].stage2()
        last(new[2])
        for a in new[:3]:
            a.stage5()
        for a in old:
            a.finish()
        copies = [
            pltpu.make_async_copy(out[i], final[i], leave.at[i]) for i in range(len(out))
        ]
        for c in copies[:3]:
            c.start()
        new[4].stage3()
        new[3].stage3()
        last(new[4], new[3])
        new[4].stage5()
        new[3].stage5()
        totals(tot, got, send, recv, PER * len(R))
        result[...] = tot[...]
        for a in new:
            a.finish()
        for c in copies[3:]:
            c.start()
        for c in copies:
            c.wait()


def back(h0, dh1, aux, normed, dqkv, w_qkv, w_small, ghead, sums, loss, count_of, kept, begun, chunks):
    count, width = h0.shape
    length = count
    r = width // (2 * X * Z)
    tile = 256
    tiles = count // tile
    once = lambda shape: pl.BlockSpec(
        shape, lambda i: (0,) * len(shape), pipeline_mode=pl.Buffered(1)
    )
    row = lambda columns: pl.BlockSpec((tile, columns), lambda i: (jnp.clip(i - 3, 0, tiles - 1), 0))
    types = (BF16, BF16, BF16, BF16, BF16, F32)
    widths = [2 * k.shape[2] for k in kept] + [3 * width, length, 256]
    sets = [shapes(r, w, o, types[t], first=False) for (t, lo, w, o) in begun]
    sets += [shapes(r, w, o, types[t]) for (t, lo, w, o) in chunks]
    ns = PER * len(sets) + 12
    place = lambda columns, dt: pltpu.VMEM((Z, X, 2, r, columns), dt)
    outs = [jax.ShapeDtypeStruct((2 * r, w), F32) for w in widths]
    outs += [jax.ShapeDtypeStruct((3, 8, 128), F32)]
    return pl.pallas_call(
        functools.partial(back_kernel, tiles, begun, chunks, [len(g) for g in sets]),
        grid=(4 + tiles,),
        in_specs=[
            row(width),
            row(width),
            row(128),
            once((count, 128)),
            once((count, width)),
            once((count, width)),
            once((count, width)),
            once((count, width)),
            once(w_qkv.shape),
            pl.BlockSpec((width, 128), lambda i: (0, 1), pipeline_mode=pl.Buffered(1)),
            once((width, 128)),
            once((8, width)),
            once((8, 128)),
            once((8, 128)),
            *[once(k.shape) for k in kept],
        ],
        out_specs=[pl.BlockSpec(memory_space=pl.ANY)] * 6 + [once((3, 8, 128))],
        out_shape=outs,
        scratch_shapes=[pltpu.VMEM(*b) for group in sets for b in group]
        + [
            pltpu.SemaphoreType.DMA((ns,)),
            pltpu.SemaphoreType.DMA((ns,)),
            pltpu.SemaphoreType.DMA((len(sets),)),
            pltpu.VMEM((12, 3, 8, 128), F32),
            pltpu.VMEM((8, width), F32),
            pltpu.VMEM((8, width), F32),
            pltpu.VMEM((count, width), BF16),
            pltpu.VMEM((count, width), BF16),
            place(3 * width, BF16),
            place(length, BF16),
            place(256, F32),
            pltpu.VMEM((3, 8, 128), F32),
            pltpu.SemaphoreType.DMA((6,)),
            *[pltpu.VMEM(o.shape, F32) for o in outs[:6]],
        ],
        compiler_params=pltpu.CompilerParams(
            collective_id=2, has_side_effects=True, vmem_limit_bytes=60 * 2**20
        ),
    )(h0, dh1, aux, aux, normed, *dqkv, w_qkv, w_small, ghead, sums, loss, count_of, *kept)


def adam_kernel(totals_ref, down, up, attn, wide, table, small_rows, small, *refs):
    sums = [jnp.sum(totals_ref[i], axis=(0, 1), keepdims=True) for i in range(3)]
    squares, total, valid = sums
    norm = jnp.sqrt(squares) / valid
    clip = jnp.minimum(1.0, CLIP_AT / (norm + 1e-06))
    scale = clip / valid
    state, outs, scalars = refs[:24], refs[24:48], refs[48]
    row = lax.broadcasted_iota(jnp.int32, scalars.shape, 0)
    scalars[...] = jnp.where(row == 0, total / math.log(2.0), jnp.where(row == 1, valid, norm))

    def update(index, grad):
        rate, decay = (RATE, DECAY) if index < 7 else (VEC_RATE, 0.0)
        weight, first, second = [state[index + 8 * i][...] for i in range(3)]
        for i, value in enumerate(adamw(weight, first, second, grad * scale, rate, decay)):
            outs[index + 8 * i][...] = value

    @pl.when(pl.program_id(0) == 0)
    def _():
        both = small[:, 128:].T
        update(0, both[PATCH : 2 * PATCH, :])
        update(7, both[:8, :])

    update(1, table[...])
    update(2, wide[...])
    update(3, attn[...])
    update(4, up[...])
    update(5, down[...])
    update(6, small_rows[:, : state[6].shape[1]])


def adam(totals, sums, masters, firsts, seconds):
    down, up, attn, wide, table, small = sums
    cuts = 4
    whole = lambda a: pl.BlockSpec(a.shape, lambda i: (0,) * a.ndim)
    by_row = lambda a: pl.BlockSpec((a.shape[0] // cuts, a.shape[1]), lambda i: (i, 0))
    turn = lambda values: [v.T if i % 8 in (1, 5) else v for i, v in enumerate(values)]
    state = turn((*masters, *firsts, *seconds))
    specs = [whole(a) if i % 8 in (0, 7) else by_row(a) for i, a in enumerate(state)]
    outs = pl.pallas_call(
        adam_kernel,
        grid=(cuts,),
        in_specs=[
            whole(totals),
            by_row(down),
            by_row(up),
            by_row(attn),
            by_row(wide),
            by_row(table),
            by_row(small),
            whole(small),
            *specs,
        ],
        out_specs=[*specs, pl.BlockSpec((8, 128), lambda i: (0, 0))],
        out_shape=[jax.ShapeDtypeStruct(a.shape, F32) for a in state]
        + [jax.ShapeDtypeStruct((8, 128), F32)],
        compiler_params=pltpu.CompilerParams(vmem_limit_bytes=60 * 2**20),
    )(totals, down, up, attn, wide, table, small, small, *state)
    scalars = outs[24]
    return (scalars[0, 0], scalars[1, 0], scalars[2, 0], *turn(outs[:24]))


def body(*args):
    patches, segments = args[:2]
    masters, firsts, seconds = (args[2:10], args[10:18], args[18:26])
    embed_in, pos_table, attn_qkv, attn_out, mlp_up, mlp_down, head_out, vectors = masters
    ways = lines()
    n_seq = lax.axis_size("seq")
    seq_at = lax.axis_index("seq")
    micros, group = segments.shape[0], segments.shape[2]
    length = group * n_seq
    width = attn_qkv.shape[1] // 3

    share = max(1, n_seq // micros)
    count = length // share
    mine = seq_at // share
    patches = patches.reshape(micros, PATCH, group)
    segments = segments.reshape(micros, group)
    low = lambda value: value.astype(BF16)
    outs = head_out.shape[1]
    pad = lambda value, columns: jnp.pad(value, ((0, 0), (0, columns - value.shape[1])))
    small = jnp.concatenate(
        [pad(low(head_out), 128), pad(low(vectors).T, PATCH), pad(low(embed_in).T, 128 - PATCH)],
        axis=1,
    )
    early = [low(attn_qkv), low(pos_table).T, small]
    late = [low(mlp_up), low(mlp_down).T, low(attn_out)]
    aligned = (lax.axis_size("dp"), n_seq, micros) == (X * Z, 4, 4) and width % (32 * X * Z) == 0
    start = (seq_at % share) * count
    part = lambda value: lax.dynamic_slice_in_dim(value, start, count, 0)
    pos_q = (start + jnp.arange(count))[None, :].astype(jnp.int32)
    if aligned:
        w_qkv, w_pos, w_small, aux, seg_q, count_of = gather(early, patches, segments, EARLY)
        h0, normed, qkv, attended, lse, w_up, w_down, w_attn = front(
            aux, seg_q, pos_q, w_pos, w_small, w_qkv, late, LATE
        )
        dattended, dh1, grad_down, grad_up, grad_attn, grad_head, grad_sums, total = mlp(
            attended, h0, aux, w_small, w_attn, w_up, w_down
        )
        dq, dk, dv, *kept = attend_back(
            qkv, qkv, qkv, (HEADS // 2, HEADS), dattended, lse, seg_q,
            aux[:, SLOT_ID : SLOT_ID + 1], pos_q, width, BF16, [grad_down, grad_up, grad_attn], BEGIN,
        )
        *sums, part = back(
            h0, dh1, aux, normed, (dq, dk, dv), w_qkv, w_small, grad_head, grad_sums, total,
            count_of, kept, BEGIN, REDUCE,
        )
        return adam(part, sums, masters, firsts, seconds)

    row = lax.all_gather(patches, "seq", axis=2, tiled=True)
    seg = lax.all_gather(segments, "seq", axis=1, tiled=True)
    row = lax.dynamic_index_in_dim(row, mine, 0, keepdims=False)
    seg = lax.dynamic_index_in_dim(seg, mine, 0, keepdims=False)
    w_qkv, w_pos, w_small, w_up, w_down, w_attn = [
        gather_rows(v, ways, False) for v in early + late
    ]
    gains = w_small[:, 128:136].astype(F32).T

    at = jnp.arange(length)
    begins = jnp.zeros((length,), jnp.int32)
    for image in range(5):
        before = (seg > 0) & (seg < image) if image else seg > 0
        begins = jnp.where(seg == image, jnp.sum(before.astype(jnp.int32)), begins)
    offset = part(at - begins)
    own = part(seg)
    later = jnp.concatenate([row[:, 1:], jnp.zeros((PATCH, 1), BF16)], axis=1)
    seg_next = part(jnp.concatenate([seg[1:], jnp.zeros((1,), jnp.int32)]))
    pair = (own == seg_next) & (own > 0)
    first = (own > 0) & (offset == 0)
    more = jnp.stack([pair, first, offset, own], axis=1).astype(F32)
    aux = pad(jnp.concatenate([part(later.T).astype(F32), part(row.T).astype(F32), more], axis=1), 128)
    valid = jnp.sum((own > 0).astype(jnp.int32)).astype(F32) * PATCH
    seg_q, seg_k = own[None, :].astype(F32), seg[:, None].astype(F32)
    lookup, tokens = lookup_of(aux, length), tokens_of(aux)

    h0 = dot(lookup, w_pos, NT) + dot(tokens, w_small[:, 128:], NT) + (gains[6] - 1.0)
    normed, unit_one, rstd_one = layer_norm(h0, gains[0], gains[1] - 1.0)
    normed = low(normed)
    qkv = low(dot(normed, w_qkv))
    keys, values, offsets = (qkv, qkv, (HEADS // 2, HEADS))
    if share > 1:
        near = [list(range(g, g + share)) for g in range(0, n_seq, share)]
        keys = lax.all_gather(qkv[:, width:], "seq", axis=0, tiled=True, axis_index_groups=near)
        values, offsets = (keys, (0, HEADS // 2))
    attended, lse = attend(qkv, keys, values, offsets, seg_q, seg_k, pos_q, width)
    dattended, dh1, grad_down, grad_up, grad_attn, grad_head, grad_sums, total = mlp(
        attended, h0, aux, w_small, w_attn, w_up, w_down
    )
    dq, dk, dv = attend_back(
        qkv, keys, values, offsets, dattended, lse, seg_q, seg_k, pos_q, width,
        BF16 if share == 1 else F32, [], [],
    )
    if share > 1:
        dk, dv = (
            low(lax.psum_scatter(d, "seq", scatter_dimension=0, tiled=True, axis_index_groups=near))
            for d in (dk, dv)
        )
    dqkv = jnp.concatenate([dq, dk, dv], axis=1)
    grad_qkv = dot(normed, dqkv, TN)
    dnorm, gain_one, shift_one = norm_back(dot(dqkv, w_qkv, NT), unit_one, rstd_one, gains[0])
    dh0 = dh1 + dnorm
    high = low(dh0)
    grad_pos = dot(high, lookup, TN) + dot(low(dh0 - high.astype(F32)), lookup, TN)
    grad_vec = jnp.concatenate(
        [gain_one[None], shift_one[None], grad_sums[2:6], jnp.sum(dh0, 0)[None], grad_sums[7:]]
    )
    small = jnp.concatenate([grad_head, dot(high, tokens, TN) + pad(grad_vec.T, 128)], axis=1)
    grads = [grad_down, grad_up, grad_attn, grad_qkv, grad_pos, small]
    parts = [
        scatter_rows(g.astype(F32), ways, order, F32 if g is small else BF16)
        for g, order in zip(grads, ("xy", "yx") * 3)
    ]
    squares = sum(jnp.sum(p * p) for p in parts)
    squares, total, valid = lax.psum((squares, jnp.sum(total), valid), ("dp", "seq"))
    down, up, attn, wide, table, small = [gather_parts(p, ways) for p in parts]
    pieces = [
        small[:, 128 + PATCH : 128 + 2 * PATCH].T,
        table.T,
        wide,
        attn,
        up,
        down.T,
        small[:, :outs],
        small[:, 128:136].T,
    ]
    norm = jnp.sqrt(squares) / valid
    clip = jnp.minimum(1.0, CLIP_AT / (norm + 1e-06))
    results = [
        adamw(
            masters[i],
            firsts[i],
            seconds[i],
            pieces[i] / valid * clip,
            RATE if i < 7 else VEC_RATE,
            DECAY if i < 7 else 0.0,
        )
        for i in range(8)
    ]
    return (
        total / math.log(2.0),
        valid,
        norm,
        *[r[0] for r in results],
        *[r[1] for r in results],
        *[r[2] for r in results],
    )


def solution(mesh):
    rows, columns = (P("dp", None), P(None, "dp"))
    weights = (columns, columns, rows, rows, rows, columns, rows, columns)
    in_specs = (P(None, "dp", None, "seq"), P(None, "dp", "seq")) + weights * 3
    out_specs = (P(), P(), P()) + weights * 3
    return jax.shard_map(body, mesh=mesh, in_specs=in_specs, out_specs=out_specs, check_vma=False)
```

```python
import functools
import math

import jax
import jax.numpy as jnp
from jax import lax
from jax.experimental import pallas as pl
from jax.experimental.pallas import tpu as pltpu
from jax.sharding import PartitionSpec as P

HEADS = 12
PATCH = 48
STEP = 10
RATE = 0.02
VEC_RATE = 0.15
BETA_ONE = 0.9
BETA_TWO = 0.95
ADAM_EPS = 1e-08
DECAY = 0.1
CLIP_AT = 0.01
NORM_EPS = 1e-05

F32 = jnp.float32
BF16 = jnp.bfloat16
WIRE = jnp.bfloat16
EARLY = [
    (0, 0, 1280, True),
    (0, 1280, 1024, True),
    (1, 0, 1024, False),
    (2, 0, 256, False),
]
LATE = [
    (0, 0, 1536, True),
    (0, 1536, 1536, True),
    (1, 0, 1536, True),
    (2, 0, 768, True),
    (1, 1536, 1536, False),
]
DEEP = [
    (0, 0, 768, "xy"),
    (1, 0, 768, "yx"),
    (0, 768, 768, "xy"),
    (1, 768, 768, "yx"),
    (0, 1536, 768, "xy"),
    (1, 1536, 768, "yx"),
    (0, 2304, 768, "xy"),
    (1, 2304, 768, "xy"),
]
REST = [
    (0, 0, 768, "yx"),
    (1, 0, 768, "xy"),
    (1, 768, 768, "xy"),
    (1, 1536, 768, "yx"),
    (2, 0, 512, "yx"),
    (2, 512, 512, "xy"),
    (3, 0, 256, "xy"),
]
NN = (((1,), (0,)), ((), ()))
NT = (((1,), (1,)), ((), ()))
TN = (((0,), (0,)), ((), ()))


PAIR, FIRST, OFFSET, SLOT_ID = range(2 * PATCH, 2 * PATCH + 4)


def dot(left, right, dims=NN):
    return lax.dot_general(left, right, dims, preferred_element_type=F32)


def lookup_of(aux, length):
    slot = lax.broadcasted_iota(jnp.int32, (aux.shape[0], length), 1).astype(F32)
    return (slot == aux[:, OFFSET : OFFSET + 1]).astype(F32).astype(BF16)


def tokens_of(aux):
    lane = lax.broadcasted_iota(jnp.int32, aux.shape, 1)
    return jnp.where((lane >= PATCH) & (lane < 2 * PATCH), aux, 0.0).astype(BF16)


def gains_of(small):
    return small[...].astype(F32).T[:8]


def line(axis, size, count, stride):
    place = (lax.axis_index(axis) // stride) % count
    swaps = [
        (axis, [(source, source ^ (step * stride)) for source in range(size)])
        for step in range(1, count)
    ]
    return (count, place, swaps)


def lines():
    n_dp, n_seq = lax.axis_size("dp"), lax.axis_size("seq")
    n_x = 1 << ((n_dp.bit_length() - 1) // 2)
    return {
        "z": line("dp", n_dp, n_dp // n_x, n_x),
        "x": line("dp", n_dp, n_x, 1),
        "y": line("seq", n_seq, n_seq // 2, 2),
        "core": line("seq", n_seq, 2, 1),
    }


def gather_line(block, along):
    count, place, swaps = along
    others = [lax.ppermute(block, axis, swap) for axis, swap in swaps]
    if count == 2:
        first = place == 0
        return jnp.stack([jnp.where(first, block, others[0]), jnp.where(first, others[0], block)])
    whole = jnp.zeros((count,) + block.shape, block.dtype)
    for step, piece in enumerate([block] + others):
        whole = lax.dynamic_update_index_in_dim(whole, piece, place ^ step, 0)
    return whole


def scatter_line(blocks, along, dim, wire):
    count, place, swaps = along
    pick = lambda index: lax.dynamic_index_in_dim(blocks, index, dim, keepdims=False)
    arrived = [
        lax.ppermute(pick(place ^ (step + 1)).astype(wire), axis, swap)
        for step, (axis, swap) in enumerate(swaps)
    ]
    total = pick(place)
    for piece in arrived:
        total = total + piece.astype(F32)
    return total


def gather_rows(shard, ways, split_y):
    n_core, core, _ = ways["core"]
    n_y, y_at, _ = ways["y"]
    rows, columns = shard.shape
    if split_y:
        part = lax.dynamic_slice_in_dim(
            shard, (core * n_y + y_at) * (rows // (2 * n_y)), rows // (2 * n_y), 0
        )
    else:
        part = lax.dynamic_slice_in_dim(shard, core * (rows // 2), rows // 2, 0)
    part = gather_line(part, ways["z"])
    part = gather_line(part, ways["x"])
    if split_y:
        part = gather_line(part, ways["y"])
        part = gather_line(part, ways["core"])
        part = jnp.transpose(part, (3, 2, 0, 1, 4, 5))
    else:
        part = gather_line(part, ways["core"])
        part = jnp.transpose(part, (2, 1, 0, 3, 4))
    return part.reshape(-1, columns)


def scatter_rows(grad, ways, order, wire):
    n_z, n_x, n_y = ways["z"][0], ways["x"][0], ways["y"][0]
    columns = grad.shape[1]
    blocks = grad.reshape(n_z, n_x, 2, n_y, -1, columns)
    blocks = scatter_line(blocks, ways["core"], 2, wire)
    if order == "xy":
        blocks = scatter_line(blocks, ways["x"], 1, wire)
        blocks = scatter_line(blocks, ways["y"], 1, wire)
    else:
        blocks = scatter_line(blocks, ways["y"], 2, wire)
        blocks = scatter_line(blocks, ways["x"], 1, wire)
    return scatter_line(blocks, ways["z"], 0, wire)


def gather_parts(part, ways):
    part = gather_line(part, ways["y"])
    part = gather_line(part, ways["core"])
    return part.reshape(-1, part.shape[-1])


MESH=pl.DeviceIdType.MESH
X = 2
Z = 4
def here():
    d=lax.axis_index("dp"); s=lax.axis_index("seq")
    return d//X, d%X, s//2, s%2
def peer(kz,kx,ky,kc):
    z,x,y,c=here()
    return ((z^kz)*X+(x^kx), (y^ky)*2+(c^kc))
class Gather:
    def __init__(s, src, dst, sems, base, split, lo, width):
        s.src,s.dst,s.split,s.lo,s.width=src,dst,split,lo,width
        s.send,s.recv=sems; s.n=base
        s.live=[]; s.rows=src.shape[0]
        s.idx={}
    def region(s,ref,kz,kx,half,ky,local=False):
        z,x,y,c=here(); r=s.rows//2
        row=(c^half)*r
        if not local: row=row+((z^kz)*X+(x^kx))*s.rows
        row=pl.multiple_of(row,16)
        if ky is None: return ref.at[pl.ds(row,r),pl.ds(s.lo,s.width)]
        w=s.width//2
        return ref.at[pl.ds(row,r),pl.ds(pl.multiple_of(s.lo+(y^ky)*w,128),w)]
    def copy(s,key,kz,kx,ky,to,own=False):
        i=s.idx.setdefault(key,s.n)
        if i==s.n: s.n+=1
        col=ky if s.split else None
        return pltpu.make_async_remote_copy(s.region(s.src if own else s.dst,kz,kx,0,col,own),s.region(s.dst,kz,kx,0,col),s.send.at[i],s.recv.at[i],device_id=peer(*to),device_id_type=MESH)
    def start(s,*a,**k):
        s.copy(*a,**k).start(); s.live.append((a,k))
    def begin(s):
        for k in (1,2,3): s.start(("z",k),0,0,0,(k,0,0,0),own=True)
        s.start(("x",0),0,0,0,(0,1,0,0),own=True)
    def after_z(s,k):
        s.recvd(("z",k),k,0,0)
        s.start(("x",k),k,0,0,(0,1,0,0))
        if s.split: s.start(("y",k,0),k,0,0,(0,0,1,0))
        s.start(("c",k,0),k,0,0,(0,0,0,1))
    def after_x(s,k):
        s.recvd(("x",k),k,1,0)
        if s.split: s.start(("y",k,1),k,1,0,(0,0,1,0))
        s.start(("c",k,1),k,1,0,(0,0,0,1))
    def after_y(s,k,kx):
        s.recvd(("y",k,kx),k,kx,1)
        s.start(("d",k,kx),k,kx,1,(0,0,0,1))
    def recvd(s,key,kz,kx,ky):
        s.copy(key,kz,kx,ky,(0,0,0,1)).wait_recv()
    def stage_z(s):
        for k in (1,2,3): s.after_z(k)
    def stage_x(s):
        for k in range(4): s.after_x(k)
    def stage_y(s):
        if s.split:
            for kx in range(2):
                for k in range(4):
                    if k or kx: s.after_y(k,kx)
    def finish(s):
        for k in range(4):
            for kx in range(2):
                if (k or kx):
                    s.core_recv(("c",k,kx),k,kx,0)
                    if s.split: s.core_recv(("d",k,kx),k,kx,1)
        for a,k in s.live: s.copy(*a,**k).wait_send()
    def core_recv(s,key,kz,kx,ky):
        i=s.idx[key]; col=ky if s.split else None
        r=s.region(s.dst,kz,kx,1,col)
        pltpu.make_async_remote_copy(r,r,s.send.at[i],s.recv.at[i],device_id=peer(0,0,0,1),device_id_type=MESH).wait_recv()

def greet(peers):
    bar=pltpu.get_barrier_semaphore()
    for p in peers: pl.semaphore_signal(bar,inc=1,device_id=peer(*p),device_id_type=MESH)
    pl.semaphore_wait(bar,len(peers))
PEERS=[(1,0,0,0),(2,0,0,0),(3,0,0,0),(0,1,0,0),(0,0,1,0),(0,0,0,1)]
class Own:
    def __init__(s,*refs): s.refs=refs
    def copy(s):
        src,dst,sem=s.refs
        z,x,y,c=here(); r=src.shape[0]
        return pltpu.make_async_copy(src,dst.at[pl.ds(pl.multiple_of((z*X+x)*r,16),r),:],sem)
    def start(s): s.copy().start()
    def wait(s): s.copy().wait()
def open_chunks(chunks,src,dst,send,recv,loc):
    mine=[Own(src[i],dst[i],loc.at[i]) for i in range(len(src))]
    g=[]; base=0
    for (t,lo,w,sp) in chunks:
        g.append(Gather(src[t],dst[t],(send,recv),base,sp,lo,w)); base+=28 if sp else 14
    return mine,g
def about_slots(row,seg):
    ids=seg[...]; length=ids.shape[1]
    slot=lax.broadcasted_iota(jnp.int32,ids.shape,1)
    begins=jnp.zeros_like(ids)
    for image in range(5):
        before=(ids>0)&(ids<image) if image else ids>0
        begins=jnp.where(ids==image,jnp.sum(before.astype(F32),axis=1,keepdims=True).astype(jnp.int32),begins)
    offset=slot-begins
    after=jnp.where(slot==length-1,0,pltpu.roll(ids,length-1,1))
    pair=((ids==after)&(ids>0)).astype(F32)
    first=((ids>0)&(offset==0)).astype(F32)
    x=row[...].astype(F32)
    later=jnp.where(lax.broadcasted_iota(jnp.int32,x.shape,1)==length-1,0.0,pltpu.roll(x,length-1,1))
    line=lax.broadcasted_iota(jnp.int32,(128-2*PATCH,length),0)
    more=jnp.zeros(line.shape,F32)
    for i,v in enumerate((pair,first,offset.astype(F32),ids.astype(F32))): more=jnp.where(line==i,v,more)
    return jnp.concatenate([later,x,more],axis=0).T
def semaphores(chunks,n):
    tot=sum(28 if s[3] else 14 for s in chunks)
    return [pltpu.SemaphoreType.DMA((tot,)),pltpu.SemaphoreType.DMA((tot,)),pltpu.SemaphoreType.DMA((n,))]
PER=8
class Reduce:
    def __init__(s,g,out,bufs,sems,base,lo,w,order):
        s.g,s.out,s.lo,s.w,s.order=g,out,lo,w,order
        s.r1,s.p2,s.r2,s.p3,s.r3,s.p4,s.r4=bufs
        s.send,s.recv=sems; s.base=base; s.r=g.shape[3]
    def col(s,ky,lo=0):
        z,x,y,c=here(); h=s.w//2
        return pl.ds(pl.multiple_of(lo+(y^ky)*h,128),h)
    def remote(s,src,dst,i,to):
        return pltpu.make_async_remote_copy(src,dst,s.send.at[s.base+i],s.recv.at[s.base+i],device_id=peer(*to),device_id_type=MESH)
    def c1(s):
        z,x,y,c=here()
        return s.remote(s.g.at[:,:,1-c,:,pl.ds(s.lo,s.w)],s.r1,0,(0,0,0,1))
    def begin(s): s.c1().start()
    def two(s,zz,xx,ky=None):
        z,x,y,c=here()
        cols=slice(None) if ky is None else s.col(ky)
        own=s.g[zz,xx,c,:,pl.ds(s.lo,s.w) if ky is None else s.col(ky,s.lo)]
        return own.astype(F32)+s.r1[zz,xx,:,cols].astype(F32)
    def three(s,zz,xx,ky):
        if s.order=="xy": return s.two(zz,xx,ky)+s.r2[zz,:,s.col(ky)].astype(F32)
        return s.two(zz,xx,ky)+s.r2[zz,xx].astype(F32)
    def four(s,zz):
        z,x,y,c=here()
        return s.three(zz,x,0)+s.r3[zz].astype(F32)
    def c2(s): return s.remote(s.p2,s.r2,1,(0,1,0,0) if s.order=="xy" else (0,0,1,0))
    def c3(s): return s.remote(s.p3,s.r3,2,(0,0,1,0) if s.order=="xy" else (0,1,0,0))
    def c4(s,k): return s.remote(s.p4.at[k-1],s.r4.at[k-1],2+k,(k,0,0,0))
    def c5(s):
        z,x,y,c=here()
        ref=s.out.at[pl.ds(pl.multiple_of(c*s.r,8),s.r),s.col(0,s.lo)]
        return s.remote(ref,ref,6,(0,0,1,0))
    def c6(s):
        z,x,y,c=here()
        ref=s.out.at[pl.ds(pl.multiple_of(c*s.r,8),s.r),pl.ds(s.lo,s.w)]
        return s.remote(ref,ref,7,(0,0,0,1))
    def stage1(s):
        z,x,y,c=here()
        s.c1().wait_recv()
        @pl.loop(0,Z)
        def _(zz):
            if s.order=="xy":
                s.p2[zz]=s.two(zz,1-x).astype(s.p2.dtype)
            else:
                for xx in range(X): s.p2[zz,xx]=s.two(zz,xx,1).astype(s.p2.dtype)
        s.c2().start()
    def stage2(s):
        z,x,y,c=here()
        s.c2().wait_recv()
        @pl.loop(0,Z)
        def _(zz):
            s.p3[zz]=(s.three(zz,x,1) if s.order=="xy" else s.three(zz,1-x,0)).astype(s.p3.dtype)
        s.c3().start()
    def stage3(s):
        z,x,y,c=here()
        s.c3().wait_recv()
        for k in (1,2,3):
            s.p4[k-1]=s.four(z^k).astype(s.p4.dtype)
            s.c4(k).start()
    def stage4(s):
        z,x,y,c=here()
        total=s.four(z)
        for k in (1,2,3):
            s.c4(k).wait_recv()
            total=total+s.r4[k-1].astype(F32)
        s.out[pl.ds(pl.multiple_of(c*s.r,8),s.r),s.col(0,s.lo)]=total
        s.c5().start()
        return total
    def stage5(s):
        s.c5().wait_recv()
        s.c6().start()
    def finish(s):
        s.c6().wait_recv()
        s.c1().wait_send(); s.c2().wait_send(); s.c3().wait_send()
        for k in (1,2,3): s.c4(k).wait_send()
        s.c5().wait_send(); s.c6().wait_send()

def shapes(r,w,order,dt):
    h=w//2
    two=(Z,r,w) if order=="xy" else (Z,X,r,h)
    return [((Z,X,r,w),dt)]+[(two,dt)]*2+[((Z,r,h),dt)]*2+[((3,r,h),dt)]*2
def reducers(chunks,g,out,bufs,send,recv):
    return [Reduce(g[t],out[t],bufs[7*i:7*i+7],(send,recv),PER*i,lo,w,o) for i,(t,lo,w,o) in enumerate(chunks)]

def totals(part,got,send,recv,base):
    d=lax.axis_index("dp"); q=lax.axis_index("seq")
    def hop(first,count,mine,peers):
        got[first+mine]=part[...]
        cs=[pltpu.make_async_remote_copy(part,got.at[first+mine],send.at[base+first+i],recv.at[base+first+i],device_id=p,device_id_type=MESH) for i,p in enumerate(peers)]
        for k in cs: k.start()
        for k in cs: k.wait()
        t=got[first]
        for i in range(1,count): t=t+got[first+i]
        part[...]=t
    hop(0,4,q,[peer(0,0,ky,kc) for ky,kc in ((0,1),(1,0),(1,1))])
    hop(4,8,d,[peer(kz,kx,0,0) for kz,kx in ((0,1),(1,0),(1,1),(2,0),(2,1),(3,0),(3,1))])

ALL=[(0,0,ky,kc) for ky,kc in ((0,1),(1,0),(1,1))]+[(kz,kx,0,0) for kz,kx in ((0,1),(1,0),(1,1),(2,0),(2,1),(3,0),(3,1))]
def fold(v):
    v=v*v
    t=jnp.zeros((8,128),F32)
    for i in range(v.shape[0]//8):
        for j in range(v.shape[1]//128):
            t=t+v[8*i:8*i+8,128*j:128*j+128]
    return t


def hide(bias, tile, skip, sq_ref, sk, qp_ref):
    for step in range(bias.shape[1] // tile):
        rows = slice(step * tile, (step + 1) * tile)
        keys = (step + 1) * tile if skip else bias.shape[0]
        pos_key = lax.broadcasted_iota(jnp.int32, (keys, tile), 0)
        allowed = (sk[:keys, :] == sq_ref[:, rows]) & (pos_key <= qp_ref[:, rows])
        bias[:keys, rows] = jnp.where(allowed, 0.0, -1e30)


def head_forward(tile, skip, hd, scale, q_ref, k_ref, v_ref, bias, o_ref, lse_ref):
    length = k_ref.shape[0]
    for head in range(q_ref.shape[1] // hd):
        cols = slice(hd * head, hd * head + hd)
        for step in range(q_ref.shape[0] // tile):
            rows = slice(step * tile, (step + 1) * tile)
            keys = (step + 1) * tile if skip else length
            query = (q_ref[rows, cols].astype(F32) * scale).astype(BF16)
            scores = dot(k_ref[:keys, cols], query, NT) + bias[:keys, rows]
            top = jnp.max(scores, 0, keepdims=True)
            weight = jnp.exp(scores - top)
            total = jnp.sum(weight, 0, keepdims=True)
            probs = (weight * (1.0 / total)).astype(BF16)
            o_ref[rows, cols] = dot(probs, v_ref[:keys, cols], TN).astype(BF16)
            lse_ref[0, head : head + 1, rows] = top + jnp.log(total)


def attend_kernel(tile, skip, hd, scale, q_ref, k_ref, v_ref, sq_ref, sk_ref, qp_ref, o_ref, lse_ref, bias):
    @pl.when(pl.program_id(0) == 0)
    def _():
        hide(bias, tile, skip, sq_ref, sk_ref, qp_ref)

    head_forward(tile, skip, hd, scale, q_ref, k_ref, v_ref, bias, o_ref, lse_ref)


def front_kernel(tiles, lanes, shape, early, late, pieces, ids, qp_ref, *refs):
    src = refs[:6]
    aux, sq_ref, count, h0_ref, normed_ref, qkv_ref, o_ref, lse_ref = refs[6:14]
    wq_out, ws_out, *dst = refs[14:19]
    wq, wp, ws, qkv, bias, gains_all, row, seg = refs[19:27]
    send, recv, loc, late_send, late_recv, late_loc, psend, precv, leave = refs[27:]
    step = pl.program_id(0)
    mine, e = open_chunks(early, src[:3], (wq, wp, ws), send, recv, loc)
    mine_late, g = open_chunks(late, src[3:], dst, late_send, late_recv, late_loc)
    group = pieces.shape[2]

    def when(index, *stages):
        @pl.when(step == index)
        def _():
            for stage in stages:
                stage()

    def out(i):
        pair = ((wq, wq_out), (ws, ws_out))[i]
        return pltpu.make_async_copy(*pair, leave.at[i])

    def begin():
        greet(PEERS + [(0, 0, 1, 1)])
        q = lax.axis_index("seq")
        at = pl.ds(pl.multiple_of(q * group, 128), group)
        swaps = []
        for k, to in ((1, (0, 0, 0, 1)), (2, (0, 0, 1, 0)), (3, (0, 0, 1, 1))):
            for j, (a, b) in enumerate(
                ((pieces.at[q ^ k], row.at[:, at]), (ids.at[q ^ k], seg.at[:, at]))
            ):
                i = 2 * (k - 1) + j
                swaps.append(
                    pltpu.make_async_remote_copy(
                        a, b, psend.at[i], precv.at[i], device_id=peer(*to), device_id_type=MESH
                    )
                )
                swaps[-1].start()
        e[0].begin()
        e[1].begin()
        for a in mine + mine_late:
            a.start()
        row[:, at] = pieces[q]
        seg[:, at] = ids[q]
        for a in swaps:
            a.wait()
        aux[...] = about_slots(row, seg)
        sq_ref[...] = seg[...].astype(F32)
        down, across = [lax.broadcasted_iota(jnp.int32, count.shape, i) for i in range(2)]
        held = jnp.sum((seg[...] > 0).astype(F32), axis=1, keepdims=True)
        count[...] = jnp.where((down == 0) & (across == 0), held * PATCH, 0.0)
        e[0].stage_z()
        e[2].begin()
        e[3].begin()
        e[1].stage_z()
        g[0].begin()
        e[0].stage_x()
        e[2].stage_z()
        e[3].stage_z()
        g[1].begin()
        e[1].stage_x()
        e[0].stage_y()
        e[2].stage_x()
        e[3].stage_x()
        e[1].stage_y()
        for a in e:
            a.finish()
        for a in mine:
            a.wait()
        out(0).start()
        out(1).start()
        gains_all[...] = gains_of(ws.at[:, 128:])
        g[0].stage_z()
        g[2].begin()

    when(0, begin)
    when(2, g[1].stage_z, g[3].begin, g[0].stage_x)
    when(4, g[2].stage_z, g[4].begin, g[1].stage_x)
    when(5, g[0].stage_y, g[3].stage_z)
    when(6, g[2].stage_x)
    when(7, g[1].stage_y, g[3].stage_x)
    when(8, g[4].stage_z)
    when(9, g[2].stage_y)

    @pl.when(step < tiles)
    def _():
        tile, length = h0_ref.shape[0], wp.shape[1]
        rows = pl.ds(pl.multiple_of(jnp.minimum(step, tiles - 1) * tile, tile), tile)
        slots = aux[rows, :]
        gains = gains_all[...]
        h0 = dot(lookup_of(slots, length), wp[...], NT) + dot(tokens_of(slots), ws[:, 128:], NT)
        h0 = h0 + (gains[6:7] - 1.0)
        h0_ref[...] = h0
        unit, _ = norm_rows(h0)
        normed = (unit * gains[0:1] + (gains[1:2] - 1.0)).astype(BF16)
        normed_ref[...] = normed
        value = dot(normed, wq[...]).astype(BF16)
        qkv_ref[...] = value
        qkv[rows, :] = value

    @pl.when(step >= tiles)
    def _():
        pair = step - tiles
        width = qkv.shape[1] // 3

        @pl.when(pair == 0)
        def _():
            hide(bias, *shape[:2], sq_ref, aux[:, SLOT_ID : SLOT_ID + 1], qp_ref)

        part = lambda i: qkv.at[:, pl.ds(pl.multiple_of(i * width + pair * lanes, lanes), lanes)]
        head_forward(*shape, part(0), part(1), part(2), bias, o_ref, lse_ref)

    def drain():
        g[4].stage_x()
        g[3].stage_y()
        g[4].stage_y()
        for a in g:
            a.finish()
        for a in mine_late:
            a.wait()
        out(0).wait()
        out(1).wait()

    when(pl.num_programs(0) - 1, drain)


def front(pieces, ids, pos_q, early_shards, late_shards, early, late):
    count, dp = pos_q.shape[1], lax.axis_size("dp")
    shards = [*early_shards, *late_shards]
    full = [jax.ShapeDtypeStruct((v.shape[0] * dp, v.shape[1]), v.dtype) for v in shards]
    width = full[0].shape[0]
    hd = width // HEADS
    lanes, pairs, tile = 2 * hd, HEADS // 2, 256
    tiles = count // tile
    once = lambda shape: pl.BlockSpec(
        shape, lambda i: (0,) * len(shape), pipeline_mode=pl.Buffered(1)
    )
    row = lambda columns: pl.BlockSpec((tile, columns), lambda i: (jnp.minimum(i, tiles - 1), 0))
    after = lambda i: jnp.maximum(i - tiles, 0)
    anywhere = pl.BlockSpec(memory_space=pl.ANY)
    ids = ids[:, None, :]
    landing = [pltpu.VMEM(v.shape, v.dtype) for v in full[:3]]
    return pl.pallas_call(
        functools.partial(front_kernel, tiles, lanes, (tile, True, hd, hd**-0.5), early, late),
        grid=(tiles + pairs,),
        in_specs=[once(pieces.shape), once(ids.shape), once((1, count))]
        + [once(v.shape) for v in shards],
        out_specs=[
            once((count, 128)),
            once((1, count)),
            once((8, 128)),
            row(width),
            row(width),
            row(3 * width),
            pl.BlockSpec((count, lanes), lambda i: (0, after(i))),
            pl.BlockSpec((1, 2, count), lambda i: (after(i), 0, 0)),
        ]
        + [anywhere] * 5,
        out_shape=[
            jax.ShapeDtypeStruct((count, 128), F32),
            jax.ShapeDtypeStruct((1, count), F32),
            jax.ShapeDtypeStruct((8, 128), F32),
            jax.ShapeDtypeStruct((count, width), F32),
            jax.ShapeDtypeStruct((count, width), BF16),
            jax.ShapeDtypeStruct((count, 3 * width), BF16),
            jax.ShapeDtypeStruct((count, width), BF16),
            jax.ShapeDtypeStruct((pairs, 2, count), F32),
            full[0],
            full[2],
            *full[3:],
        ],
        scratch_shapes=landing
        + [
            pltpu.VMEM((count, 3 * width), BF16),
            pltpu.VMEM((count, count), F32),
            pltpu.VMEM((8, width), F32),
            pltpu.VMEM((pieces.shape[1], count), pieces.dtype),
            pltpu.VMEM((1, count), ids.dtype),
        ]
        + semaphores(early, 3)
        + semaphores(late, 3)
        + [pltpu.SemaphoreType.DMA((6,)), pltpu.SemaphoreType.DMA((6,)), pltpu.SemaphoreType.DMA((2,))],
        compiler_params=pltpu.CompilerParams(
            collective_id=4, has_side_effects=True, vmem_limit_bytes=60 * 2**20
        ),
    )(pieces, ids, pos_q, *shards)


def head_back(
    tile, skip, hd, scale, q_ref, k_ref, v_ref, do_ref, lse_ref, bias, dq_ref, dk_ref, dv_ref,
    dk_sum, dv_sum, before=lambda head: None,
):
    length = k_ref.shape[0]
    dk_sum[...] = jnp.zeros_like(dk_sum)
    dv_sum[...] = jnp.zeros_like(dv_sum)
    for head in range(q_ref.shape[1] // hd):
        cols = slice(hd * head, hd * head + hd)
        before(head)
        for step in range(q_ref.shape[0] // tile):
            rows = slice(step * tile, (step + 1) * tile)
            keys = (step + 1) * tile if skip else length
            query = (q_ref[rows, cols].astype(F32) * scale).astype(BF16)
            key = k_ref[:keys, cols]
            dout = do_ref[rows, cols]
            scores = dot(key, query, NT) + bias[:keys, rows]
            probs = jnp.exp(scores - lse_ref[0, head : head + 1, rows])
            dprobs = dot(v_ref[:keys, cols], dout, NT)
            delta = jnp.sum(dprobs * probs, 0, keepdims=True)
            dscores = (probs * (dprobs - delta)).astype(BF16)
            dv_sum[:keys, cols] += dot(probs.astype(BF16), dout)
            dk_sum[:keys, cols] += dot(dscores, query)
            dq_ref[rows, cols] = (dot(dscores, key, TN) * scale).astype(dq_ref.dtype)
    dk_ref[...] = dk_sum[...].astype(dk_ref.dtype)
    dv_ref[...] = dv_sum[...].astype(dv_ref.dtype)


def attend_back_kernel(
    tile, skip, hd, scale, q_ref, k_ref, v_ref, do_ref, lse_ref, sq_ref, sk_ref, qp_ref,
    dq_ref, dk_ref, dv_ref, dk_sum, dv_sum, bias,
):
    @pl.when(pl.program_id(0) == 0)
    def _():
        hide(bias, tile, skip, sq_ref, sk_ref, qp_ref)

    head_back(
        tile, skip, hd, scale, q_ref, k_ref, v_ref, do_ref, lse_ref, bias, dq_ref, dk_ref, dv_ref,
        dk_sum, dv_sum,
    )


def attend_back_deep_kernel(
    parts, shape, chunks, m_ref, dd_ref, hid_ref, du_ref, q_ref, k_ref, v_ref, do_ref, lse_ref,
    sq_ref, sk_ref, qp_ref, dq_ref, dk_ref, dv_ref, squares, down_ref, up_ref, dk_sum, dv_sum, bias,
    g_down, g_up, down, up, send, recv, leave, *bufs,
):
    step = pl.program_id(0)
    width, wide = m_ref.shape[1], hid_ref.shape[1]
    R = reducers(chunks, (g_down, g_up), (down, up), bufs, send, recv)
    pairs = [R[2 * j : 2 * j + 2] for j in range(parts)]
    every = lambda name, j: lambda: [getattr(a, name)() for a in pairs[j]]

    def last(j):
        def run():
            for a in pairs[j]:
                squares[...] += fold(a.stage4())

        return run

    def when(index, *stages):
        @pl.when(step == index)
        def _():
            for stage in stages:
                stage()

    def first():
        greet(PEERS)
        squares[...] = jnp.zeros_like(squares)

    when(0, first)
    place = lambda value: value.astype(BF16).reshape(Z, X, 2, width // (2 * X * Z), wide)
    for j in range(parts):

        @pl.when(step == j)
        def _():
            cols = slice(j * wide, (j + 1) * wide)
            g_down[:, :, :, :, cols] = place(dot(dd_ref[...], hid_ref[...], TN))
            pairs[j][0].begin()
            g_up[:, :, :, :, cols] = place(dot(m_ref[...], du_ref[...], TN))
            pairs[j][1].begin()
            if j == 1:
                every("stage1", 0)()
            if j == 3:
                every("stage1", 1)()

    when(parts, lambda: hide(bias, *shape[:2], sq_ref, sk_ref, qp_ref))
    moves = {
        1: [every("stage2", 0)],
        3: [every("stage1", 2), every("stage3", 0)],
        4: [every("stage2", 1)],
        6: [every("stage1", 3), last(0), every("stage3", 1)],
        7: [every("stage2", 2)],
        9: [last(1), every("stage5", 0)],
        10: [every("stage2", 3), every("stage3", 2)],
        11: [every("stage5", 1)],
    }

    def before(head):
        for half, stages in moves.items():
            if half % 2 == head:
                when(parts + half // 2, *stages)

    @pl.when(step >= parts)
    def _():
        head_back(
            *shape, q_ref, k_ref, v_ref, do_ref, lse_ref, bias, dq_ref, dk_ref, dv_ref, dk_sum,
            dv_sum, before,
        )

    def drain():
        last(2)()
        every("stage3", 3)()
        every("stage5", 2)()
        last(3)()
        every("stage5", 3)()
        for a in R:
            a.finish()
        copies = [
            pltpu.make_async_copy(down, down_ref, leave.at[0]),
            pltpu.make_async_copy(up, up_ref, leave.at[1]),
        ]
        for c in copies:
            c.start()
        for c in copies:
            c.wait()

    when(9, drain)


def blocks_of(rows, width, offset):
    return pl.BlockSpec((rows, width), lambda pair: (0, pair + offset))


def fixed(shape):
    return pl.BlockSpec(shape, lambda pair: (0, 0))


def kernel_params():
    return pltpu.CompilerParams(vmem_limit_bytes=48 * 2**20)


def attend(qkv, keys, values, offsets, seg_q, seg_k, pos_q, width):
    count, length = qkv.shape[0], keys.shape[0]
    hd = width // HEADS
    lanes = 2 * hd
    pairs = HEADS // 2
    return pl.pallas_call(
        functools.partial(attend_kernel, min(256, count), count == length, hd, hd**-0.5),
        grid=(pairs,),
        in_specs=[
            blocks_of(count, lanes, 0),
            blocks_of(length, lanes, offsets[0]),
            blocks_of(length, lanes, offsets[1]),
            fixed((1, count)),
            fixed((length, 1)),
            fixed((1, count)),
        ],
        out_specs=[blocks_of(count, lanes, 0), pl.BlockSpec((1, 2, count), lambda pair: (pair, 0, 0))],
        out_shape=[
            jax.ShapeDtypeStruct((count, width), BF16),
            jax.ShapeDtypeStruct((pairs, 2, count), F32),
        ],
        scratch_shapes=[pltpu.VMEM((length, count), F32)],
        cost_estimate=pl.CostEstimate(
            flops=25_000_000_000, bytes_accessed=8_000_000, transcendentals=8_000_000
        ),
        compiler_params=kernel_params(),
    )(qkv, keys, values, seg_q, seg_k, pos_q)


def attend_back(qkv, keys, values, offsets, dout, lse, seg_q, seg_k, pos_q, width, kv_type):
    count, length = qkv.shape[0], keys.shape[0]
    hd = width // HEADS
    lanes = 2 * hd
    pairs = HEADS // 2
    return pl.pallas_call(
        functools.partial(attend_back_kernel, min(256, count), count == length, hd, hd**-0.5),
        grid=(pairs,),
        in_specs=[
            blocks_of(count, lanes, 0),
            blocks_of(length, lanes, offsets[0]),
            blocks_of(length, lanes, offsets[1]),
            blocks_of(count, lanes, 0),
            pl.BlockSpec((1, 2, count), lambda pair: (pair, 0, 0)),
            fixed((1, count)),
            fixed((length, 1)),
            fixed((1, count)),
        ],
        out_specs=[
            blocks_of(count, lanes, 0),
            blocks_of(length, lanes, 0),
            blocks_of(length, lanes, 0),
        ],
        out_shape=[
            jax.ShapeDtypeStruct((count, width), BF16),
            jax.ShapeDtypeStruct((length, width), kv_type),
            jax.ShapeDtypeStruct((length, width), kv_type),
        ],
        scratch_shapes=[pltpu.VMEM((length, lanes), F32)] * 2 + [pltpu.VMEM((length, count), F32)],
        compiler_params=kernel_params(),
    )(qkv, keys, values, dout, lse, seg_q, seg_k, pos_q)


def attend_back_deep(qkv, dout, lse, seg_q, seg_k, pos_q, mixed, ddown, hidden, dupper, chunks):
    count, width = mixed.shape
    hd = width // HEADS
    lanes, pairs, parts = 2 * hd, HEADS // 2, hidden.shape[1] // width
    r = width // (2 * X * Z)
    pair = lambda offset: pl.BlockSpec(
        (count, lanes), lambda i: (0, offset + jnp.maximum(i - parts, 0))
    )
    column = pl.BlockSpec((count, width), lambda i: (0, jnp.minimum(i, parts - 1)))
    once = lambda shape: pl.BlockSpec(shape, lambda i: (0, 0), pipeline_mode=pl.Buffered(1))
    heads = jax.ShapeDtypeStruct((count, width), BF16)
    total = jax.ShapeDtypeStruct((2 * r, hidden.shape[1]), F32)
    ns = PER * len(chunks)
    return pl.pallas_call(
        functools.partial(attend_back_deep_kernel, parts, (256, True, hd, hd**-0.5), chunks),
        grid=(parts + pairs,),
        in_specs=[
            once((count, width)),
            once((count, width)),
            column,
            column,
            pair(0),
            pair(pairs),
            pair(2 * pairs),
            pair(0),
            pl.BlockSpec((1, 2, count), lambda i: (jnp.maximum(i - parts, 0), 0, 0)),
            once((1, count)),
            once((count, 1)),
            once((1, count)),
        ],
        out_specs=[pair(0), pair(0), pair(0), once((8, 128))]
        + [pl.BlockSpec(memory_space=pl.ANY)] * 2,
        out_shape=[heads, heads, heads, jax.ShapeDtypeStruct((8, 128), F32), total, total],
        scratch_shapes=[
            pltpu.VMEM((count, lanes), F32),
            pltpu.VMEM((count, lanes), F32),
            pltpu.VMEM((count, count), F32),
            pltpu.VMEM((Z, X, 2, r, hidden.shape[1]), BF16),
            pltpu.VMEM((Z, X, 2, r, hidden.shape[1]), BF16),
            pltpu.VMEM(total.shape, F32),
            pltpu.VMEM(total.shape, F32),
            pltpu.SemaphoreType.DMA((ns,)),
            pltpu.SemaphoreType.DMA((ns,)),
            pltpu.SemaphoreType.DMA((2,)),
        ]
        + [pltpu.VMEM(*b) for (t, lo, w, o) in chunks for b in shapes(r, w, o, BF16)],
        compiler_params=pltpu.CompilerParams(
            collective_id=3, has_side_effects=True, vmem_limit_bytes=60 * 2**20
        ),
    )(mixed, ddown, hidden, dupper, qkv, qkv, qkv, dout, lse, seg_q, seg_k, pos_q)


def layer_norm(hidden, gain, shift):
    mean = jnp.mean(hidden, -1, keepdims=True)
    centred = hidden - mean
    var = jnp.mean(centred * centred, -1, keepdims=True)
    rstd = lax.rsqrt(var + NORM_EPS)
    unit = centred * rstd
    return (unit * gain + shift, unit, rstd)


def norm_back(grad, unit, rstd, gain):
    dunit = grad * gain
    dhid = rstd * (
        dunit
        - jnp.mean(dunit, -1, keepdims=True)
        - unit * jnp.mean(dunit * unit, -1, keepdims=True)
    )
    return (dhid, jnp.sum(grad * unit, 0), jnp.sum(grad, 0))


def adamw(weight, first, second, grad, rate, decay):
    new_first = BETA_ONE * first + (1.0 - BETA_ONE) * grad
    new_second = BETA_TWO * second + (1.0 - BETA_TWO) * grad * grad
    first_hat = new_first / (1.0 - BETA_ONE**STEP)
    second_hat = new_second / (1.0 - BETA_TWO**STEP)
    return (
        weight - rate * (first_hat / (jnp.sqrt(second_hat) + ADAM_EPS) + decay * weight),
        new_first,
        new_second,
    )


def norm_rows(hidden):
    mean = jnp.mean(hidden, -1, keepdims=True)
    centred = hidden - mean
    rstd = lax.rsqrt(jnp.mean(centred * centred, -1, keepdims=True) + NORM_EPS)
    return centred * rstd, rstd


def norm_rows_back(grad, unit, rstd, gain):
    dunit = grad * gain
    return rstd * (
        dunit
        - jnp.mean(dunit, -1, keepdims=True)
        - unit * jnp.mean(dunit * unit, -1, keepdims=True)
    )


def add_rows(ref, row, value):
    ref[row : row + 1, :] += jnp.sum(value, 0, keepdims=True)


GELU_A = math.sqrt(2.0 / math.pi)
GELU_B = 0.044715


def mlp_kernel(
    wide, o_ref, h0_ref, aux_ref, ws_ref, wa_ref, wu_ref, wd_ref, wh_ref,
    do_ref, dh1_ref, dat_ref, m_ref, hid_ref, dd_ref, du_ref, ghead_ref, sums_ref, loss_ref,
    slope, gains_all,
):
    step = pl.program_id(0)
    tile, width = h0_ref.shape
    blocks = [slice(j, j + wide) for j in range(0, wu_ref.shape[1], wide)]

    @pl.when(step == 0)
    def _():
        gains_all[...] = gains_of(ws_ref)
        sums_ref[...] = jnp.zeros_like(sums_ref)
        loss_ref[...] = jnp.zeros_like(loss_ref)
        ghead_ref[...] = jnp.zeros_like(ghead_ref)

    gains = gains_all[...]
    o = o_ref[...]
    h1 = h0_ref[...] + dot(o, wa_ref[...]) + (gains[7:8] - 1.0)
    unit_two, rstd_two = norm_rows(h1)
    m = (unit_two * gains[2:3] + (gains[3:4] - 1.0)).astype(BF16)
    m_ref[...] = m
    h2 = h1
    for b in blocks:
        u = dot(m, wu_ref[:, b])
        square = u * u
        th = jnp.tanh(GELU_A * (u + GELU_B * (square * u)))
        hid = (0.5 * u * (1.0 + th)).astype(BF16)
        slope[:, b] = 0.5 * (1.0 + th) + (0.5 * u) * (1.0 - th * th) * (
            GELU_A * (1.0 + (3.0 * GELU_B) * square)
        )
        hid_ref[:, b] = hid
        h2 = h2 + dot(hid, wd_ref[:, b], NT)
    unit_fin, rstd_fin = norm_rows(h2)
    final = (unit_fin * gains[4:5] + (gains[5:6] - 1.0)).astype(BF16)
    out = dot(final, wh_ref[...])
    aux = aux_ref[...]
    lane = lax.broadcasted_iota(jnp.int32, out.shape, 1)
    used = lane < PATCH
    pair, first = aux[:, PAIR : PAIR + 1], aux[:, FIRST : FIRST + 1]
    alpha = jnp.where(used, pltpu.roll(out, 128 - PATCH, 1), 0.0)
    plain = jnp.where(used, pltpu.roll(aux, 128 - PATCH, 1), 0.0)
    shrink = jnp.exp(-alpha)
    scaled = jnp.where(used, aux - out, 0.0) * shrink
    term = pair * (0.5 * scaled * scaled + alpha) + first * (0.5 * plain * plain)
    loss_ref[...] += jnp.sum(term.reshape(tile // 8, 8, 128), 0)
    dmu = -pair * scaled * shrink
    dalpha = pltpu.roll(jnp.where(used, pair * (1.0 - scaled * scaled), 0.0), PATCH, 1)
    dout = jnp.where(used, dmu, dalpha).astype(BF16)
    ghead_ref[...] += dot(final, dout, TN)
    dfinal = dot(dout, wh_ref[...], NT)
    add_rows(sums_ref, 4, dfinal * unit_fin)
    add_rows(sums_ref, 5, dfinal)
    dh2 = norm_rows_back(dfinal, unit_fin, rstd_fin, gains[4:5])
    dd = dh2.astype(BF16)
    dd_ref[...] = dd
    dmixed = jnp.zeros((tile, width), F32)
    for b in blocks:
        du = (dot(dd, wd_ref[:, b]) * slope[:, b]).astype(BF16)
        du_ref[:, b] = du
        dmixed = dmixed + dot(du, wu_ref[:, b], NT)
    add_rows(sums_ref, 2, dmixed * unit_two)
    add_rows(sums_ref, 3, dmixed)
    dh1 = dh2 + norm_rows_back(dmixed, unit_two, rstd_two, gains[2:3])
    add_rows(sums_ref, 7, dh1)
    dh1_ref[...] = dh1
    dat = dh1.astype(BF16)
    dat_ref[...] = dat
    do_ref[...] = dot(dat, wa_ref[...], NT).astype(BF16)


def mlp(o, h0, aux, w_small, w_attn, w_up, w_down):
    count, width = h0.shape
    deep = w_up.shape[1]
    tile = min(256, count)
    row = lambda columns: pl.BlockSpec((tile, columns), lambda i: (i, 0))
    once = lambda shape: pl.BlockSpec(shape, lambda i: (0, 0), pipeline_mode=pl.Buffered(1))
    tall = lambda columns, dt: jax.ShapeDtypeStruct((count, columns), dt)
    return pl.pallas_call(
        functools.partial(mlp_kernel, width),
        grid=(count // tile,),
        in_specs=[
            row(width),
            row(width),
            row(128),
            pl.BlockSpec((width, 128), lambda i: (0, 1), pipeline_mode=pl.Buffered(1)),
            once((width, width)),
            once((width, deep)),
            once((width, deep)),
            once((width, 128)),
        ],
        out_specs=[
            row(width),
            row(width),
            row(width),
            row(width),
            row(deep),
            row(width),
            row(deep),
            once((width, 128)),
            once((8, width)),
            once((8, 128)),
        ],
        out_shape=[
            tall(width, BF16),
            tall(width, F32),
            tall(width, BF16),
            tall(width, BF16),
            tall(deep, BF16),
            tall(width, BF16),
            tall(deep, BF16),
            jax.ShapeDtypeStruct((width, 128), F32),
            jax.ShapeDtypeStruct((8, width), F32),
            jax.ShapeDtypeStruct((8, 128), F32),
        ],
        scratch_shapes=[pltpu.VMEM((tile, deep), F32), pltpu.VMEM((8, width), F32)],
        compiler_params=pltpu.CompilerParams(vmem_limit_bytes=60 * 2**20),
    )(o, h0, aux, w_small, w_attn, w_up, w_down, w_small)


def back_kernel(
    tiles, chunks, h0_ref, dh1_ref, aux_ref, slots_ref, o_far, dat_far, normed_far, dq_far, dk_far,
    dv_far, wq_far, ws_ref, ghead_ref, sums_ref, squares_ref, loss_ref, count_ref, *refs,
):
    final, result, out, g = refs[:4], refs[4], refs[5:9], refs[9:13]
    tot, got, gains_all, vec, high, rest, send, recv, leave, enter = refs[13:23]
    near = refs[23:30]
    o_ref, dat_ref, normed_ref, dq_ref, dk_ref, dv_ref, wq_ref = near
    step = pl.program_id(0)
    R = reducers(chunks, g, out, refs[30:], send, recv)
    far = (o_far, dat_far, normed_far, dq_far, dk_far, dv_far, wq_far)
    bring = lambda i: pltpu.make_async_copy(far[i], near[i], enter.at[i])
    tile, width = h0_ref.shape
    place = lambda value: value.reshape(Z, X, 2, width // (2 * X * Z), value.shape[-1])

    def last(*group):
        for a in group:
            tot[0] += fold(a.stage4())

    def when(index, *stages):
        @pl.when(step == index)
        def _():
            for stage in stages:
                stage()

    def first():
        for i in range(len(far)):
            bring(i).start()
        greet(ALL)
        gains_all[...] = gains_of(ws_ref)
        vec[...] = sums_ref[...]
        tot[0] = squares_ref[...]
        tot[1] = loss_ref[...]
        tot[2] = count_ref[...]

    when(0, first)
    for j, d_ref in enumerate((dat_ref, dq_ref, dk_ref, dv_ref)):

        @pl.when(step == j)
        def _():
            for i in ((0, 1), (2, 3), (4,), (5,))[j]:
                bring(i).wait()
            if j:
                value = dot(normed_ref[...], d_ref[...], TN).astype(BF16)
                g[1][:, :, :, :, (j - 1) * width : j * width] = place(value)
            else:
                g[0][...] = place(dot(o_ref[...], d_ref[...], TN).astype(BF16))
            R[j].begin()
            if j:
                R[j - 1].stage1()

    when(4, R[3].stage1, bring(6).wait)
    when(6, R[0].stage2)
    when(8, R[1].stage2)

    @pl.when((step >= 4) & (step < 4 + tiles))
    def _():
        gains = gains_all[...]
        unit, rstd = norm_rows(h0_ref[...])
        rows = pl.ds(pl.multiple_of(jnp.clip(step - 4, 0, tiles - 1) * tile, tile), tile)
        dnormed = dot(dq_ref[rows, :], wq_ref[:, :width], NT)
        dnormed = dnormed + dot(dk_ref[rows, :], wq_ref[:, width : 2 * width], NT)
        dnormed = dnormed + dot(dv_ref[rows, :], wq_ref[:, 2 * width :], NT)
        add_rows(vec, 0, dnormed * unit)
        add_rows(vec, 1, dnormed)
        dh0 = dh1_ref[...] + norm_rows_back(dnormed, unit, rstd, gains[0:1])
        add_rows(vec, 6, dh0)
        top = dh0.astype(BF16)
        high[rows, :] = top
        rest[rows, :] = (dh0 - top.astype(F32)).astype(BF16)

    @pl.when(step == 4 + tiles)
    def _():
        slots = slots_ref[...]
        lookup = lookup_of(slots, g[2].shape[-1])
        top, low = high[...], rest[...]
        half = lookup.shape[1] // 2
        for j in range(2):
            cols = slice(j * half, (j + 1) * half)
            value = dot(top, lookup[:, cols], TN) + dot(low, lookup[:, cols], TN)
            g[2][:, :, :, :, cols] = place(value.astype(BF16))
            R[4 + j].begin()
        line = jnp.concatenate([vec[...], jnp.zeros((120, width), F32)], axis=0)
        both = dot(top, tokens_of(slots), TN) + line.T
        g[3][...] = place(jnp.concatenate([ghead_ref[...], both], axis=1))
        R[6].begin()
        for a in R[4:]:
            a.stage1()
        R[0].stage3()
        R[2].stage2()
        R[3].stage2()
        R[1].stage3()
        last(R[0], R[1])
        for a in R[4:]:
            a.stage2()
        R[2].stage3()
        R[3].stage3()
        R[0].stage5()
        R[1].stage5()
        for a in R[4:]:
            a.stage3()
        last(R[2], R[3])
        last(*R[4:])
        totals(tot, got, send, recv, PER * len(R))
        result[...] = tot[...]
        for a in R[2:]:
            a.stage5()
        for a in R:
            a.finish()
        copies = [pltpu.make_async_copy(out[i], final[i], leave.at[i]) for i in range(4)]
        for c in copies:
            c.start()
        for c in copies:
            c.wait()


def back(h0, dh1, aux, normed, o, dat, dqkv, w_qkv, w_small, ghead, sums, squares, loss, held, chunks):
    count, width = h0.shape
    length = count
    r = width // (2 * X * Z)
    tile = 256
    tiles = count // tile
    once = lambda shape: pl.BlockSpec(
        shape, lambda i: (0,) * len(shape), pipeline_mode=pl.Buffered(1)
    )
    row = lambda columns: pl.BlockSpec((tile, columns), lambda i: (jnp.clip(i - 4, 0, tiles - 1), 0))
    types = (BF16, BF16, BF16, F32)
    widths = (width, 3 * width, length, 256)
    ns = PER * len(chunks) + 12
    outs = [jax.ShapeDtypeStruct((2 * r, w), F32) for w in widths]
    totals_of = jax.ShapeDtypeStruct((3, 8, 128), F32)
    far = (o, dat, normed, *dqkv, w_qkv)
    return pl.pallas_call(
        functools.partial(back_kernel, tiles, chunks),
        grid=(5 + tiles,),
        in_specs=[
            row(width),
            row(width),
            row(128),
            once((count, 128)),
            *[pl.BlockSpec(memory_space=pl.ANY)] * len(far),
            pl.BlockSpec((width, 128), lambda i: (0, 1), pipeline_mode=pl.Buffered(1)),
            once((width, 128)),
            once((8, width)),
            *[once((8, 128))] * 3,
        ],
        out_specs=[pl.BlockSpec(memory_space=pl.ANY)] * 4 + [once((3, 8, 128))],
        out_shape=[*outs, totals_of],
        scratch_shapes=[pltpu.VMEM(o.shape, F32) for o in outs]
        + [pltpu.VMEM((Z, X, 2, r, w), t) for w, t in zip(widths, types)]
        + [
            pltpu.VMEM((3, 8, 128), F32),
            pltpu.VMEM((12, 3, 8, 128), F32),
            pltpu.VMEM((8, width), F32),
            pltpu.VMEM((8, width), F32),
            pltpu.VMEM((count, width), BF16),
            pltpu.VMEM((count, width), BF16),
            pltpu.SemaphoreType.DMA((ns,)),
            pltpu.SemaphoreType.DMA((ns,)),
            pltpu.SemaphoreType.DMA((4,)),
            pltpu.SemaphoreType.DMA((len(far),)),
            *[pltpu.VMEM(v.shape, v.dtype) for v in far],
        ]
        + [pltpu.VMEM(*b) for (t, lo, w, o) in chunks for b in shapes(r, w, o, types[t])],
        compiler_params=pltpu.CompilerParams(
            collective_id=2, has_side_effects=True, vmem_limit_bytes=60 * 2**20
        ),
    )(h0, dh1, aux, aux, *far, w_small, ghead, sums, squares, loss, held)


def adam_kernel(totals_ref, down, up, attn, wide, table, small_rows, small, *refs):
    sums = [jnp.sum(totals_ref[i], axis=(0, 1), keepdims=True) for i in range(3)]
    squares, total, valid = sums
    norm = jnp.sqrt(squares) / valid
    clip = jnp.minimum(1.0, CLIP_AT / (norm + 1e-06))
    scale = clip / valid
    state, outs, scalars = refs[:24], refs[24:48], refs[48]
    row = lax.broadcasted_iota(jnp.int32, scalars.shape, 0)
    scalars[...] = jnp.where(row == 0, total / math.log(2.0), jnp.where(row == 1, valid, norm))

    def update(index, grad):
        rate, decay = (RATE, DECAY) if index < 7 else (VEC_RATE, 0.0)
        weight, first, second = [state[index + 8 * i][...] for i in range(3)]
        for i, value in enumerate(adamw(weight, first, second, grad * scale, rate, decay)):
            outs[index + 8 * i][...] = value

    @pl.when(pl.program_id(0) == 0)
    def _():
        both = small[:, 128:].T
        update(0, both[PATCH : 2 * PATCH, :])
        update(7, both[:8, :])

    update(1, table[...])
    update(2, wide[...])
    update(3, attn[...])
    update(4, up[...])
    update(5, down[...])
    update(6, small_rows[:, : state[6].shape[1]])


def adam(totals, sums, masters, firsts, seconds):
    down, up, attn, wide, table, small = sums
    cuts = 4
    whole = lambda a: pl.BlockSpec(a.shape, lambda i: (0,) * a.ndim)
    by_row = lambda a: pl.BlockSpec((a.shape[0] // cuts, a.shape[1]), lambda i: (i, 0))
    turn = lambda values: [v.T if i % 8 in (1, 5) else v for i, v in enumerate(values)]
    state = turn((*masters, *firsts, *seconds))
    specs = [whole(a) if i % 8 in (0, 7) else by_row(a) for i, a in enumerate(state)]
    outs = pl.pallas_call(
        adam_kernel,
        grid=(cuts,),
        in_specs=[
            whole(totals),
            by_row(down),
            by_row(up),
            by_row(attn),
            by_row(wide),
            by_row(table),
            by_row(small),
            whole(small),
            *specs,
        ],
        out_specs=[*specs, pl.BlockSpec((8, 128), lambda i: (0, 0))],
        out_shape=[jax.ShapeDtypeStruct(a.shape, F32) for a in state]
        + [jax.ShapeDtypeStruct((8, 128), F32)],
        compiler_params=pltpu.CompilerParams(vmem_limit_bytes=60 * 2**20),
    )(totals, down, up, attn, wide, table, small, small, *state)
    scalars = outs[24]
    return (scalars[0, 0], scalars[1, 0], scalars[2, 0], *turn(outs[:24]))


def body(*args):
    patches, segments = args[:2]
    masters, firsts, seconds = (args[2:10], args[10:18], args[18:26])
    embed_in, pos_table, attn_qkv, attn_out, mlp_up, mlp_down, head_out, vectors = masters
    ways = lines()
    n_seq = lax.axis_size("seq")
    seq_at = lax.axis_index("seq")
    micros, group = segments.shape[0], segments.shape[2]
    length = group * n_seq
    width = attn_qkv.shape[1] // 3

    share = max(1, n_seq // micros)
    count = length // share
    mine = seq_at // share
    patches = patches.reshape(micros, PATCH, group)
    segments = segments.reshape(micros, group)
    low = lambda value: value.astype(BF16)
    outs = head_out.shape[1]
    pad = lambda value, columns: jnp.pad(value, ((0, 0), (0, columns - value.shape[1])))
    small = jnp.concatenate(
        [pad(low(head_out), 128), pad(low(vectors).T, PATCH), pad(low(embed_in).T, 128 - PATCH)],
        axis=1,
    )
    early = [low(attn_qkv), low(pos_table).T, small]
    late = [low(mlp_up), low(mlp_down).T, low(attn_out)]
    aligned = (lax.axis_size("dp"), n_seq, micros) == (X * Z, 4, 4) and width % (32 * X * Z) == 0
    start = (seq_at % share) * count
    part = lambda value: lax.dynamic_slice_in_dim(value, start, count, 0)
    pos_q = (start + jnp.arange(count))[None, :].astype(jnp.int32)
    if aligned:
        aux, seg_q, count_of, h0, normed, qkv, attended, lse, w_qkv, w_small, w_up, w_down, w_attn = front(
            patches, segments, pos_q, early, late, EARLY, LATE
        )
        dattended, dh1, dat, mixed, hidden, ddown, dupper, grad_head, grad_sums, total = mlp(
            attended, h0, aux, w_small, w_attn, w_up, w_down
        )
        dq, dk, dv, squares, down, up = attend_back_deep(
            qkv, dattended, lse, seg_q, aux[:, SLOT_ID : SLOT_ID + 1], pos_q, mixed, ddown, hidden,
            dupper, DEEP,
        )
        attn, wide, table, small, part = back(
            h0, dh1, aux, normed, attended, dat, (dq, dk, dv), w_qkv, w_small, grad_head, grad_sums,
            squares, total, count_of, REST,
        )
        sums = (down, up, attn, wide, table, small)
        return adam(part, sums, masters, firsts, seconds)

    row = lax.all_gather(patches, "seq", axis=2, tiled=True)
    seg = lax.all_gather(segments, "seq", axis=1, tiled=True)
    row = lax.dynamic_index_in_dim(row, mine, 0, keepdims=False)
    seg = lax.dynamic_index_in_dim(seg, mine, 0, keepdims=False)
    w_qkv, w_pos, w_small, w_up, w_down, w_attn = [
        gather_rows(v, ways, False) for v in early + late
    ]
    gains = w_small[:, 128:136].astype(F32).T

    at = jnp.arange(length)
    begins = jnp.zeros((length,), jnp.int32)
    for image in range(5):
        before = (seg > 0) & (seg < image) if image else seg > 0
        begins = jnp.where(seg == image, jnp.sum(before.astype(jnp.int32)), begins)
    offset = part(at - begins)
    own = part(seg)
    later = jnp.concatenate([row[:, 1:], jnp.zeros((PATCH, 1), BF16)], axis=1)
    seg_next = part(jnp.concatenate([seg[1:], jnp.zeros((1,), jnp.int32)]))
    pair = (own == seg_next) & (own > 0)
    first = (own > 0) & (offset == 0)
    more = jnp.stack([pair, first, offset, own], axis=1).astype(F32)
    aux = pad(jnp.concatenate([part(later.T).astype(F32), part(row.T).astype(F32), more], axis=1), 128)
    valid = jnp.sum((own > 0).astype(jnp.int32)).astype(F32) * PATCH
    seg_q, seg_k = own[None, :].astype(F32), seg[:, None].astype(F32)
    lookup, tokens = lookup_of(aux, length), tokens_of(aux)

    h0 = dot(lookup, w_pos, NT) + dot(tokens, w_small[:, 128:], NT) + (gains[6] - 1.0)
    normed, unit_one, rstd_one = layer_norm(h0, gains[0], gains[1] - 1.0)
    normed = low(normed)
    qkv = low(dot(normed, w_qkv))
    keys, values, offsets = (qkv, qkv, (HEADS // 2, HEADS))
    if share > 1:
        near = [list(range(g, g + share)) for g in range(0, n_seq, share)]
        keys = lax.all_gather(qkv[:, width:], "seq", axis=0, tiled=True, axis_index_groups=near)
        values, offsets = (keys, (0, HEADS // 2))
    attended, lse = attend(qkv, keys, values, offsets, seg_q, seg_k, pos_q, width)
    dattended, dh1, dat, mixed, hidden, ddown, dupper, grad_head, grad_sums, total = mlp(
        attended, h0, aux, w_small, w_attn, w_up, w_down
    )
    grad_down, grad_up = dot(ddown, hidden, TN), dot(mixed, dupper, TN)
    grad_attn = dot(attended, dat, TN)
    dq, dk, dv = attend_back(
        qkv, keys, values, offsets, dattended, lse, seg_q, seg_k, pos_q, width,
        BF16 if share == 1 else F32,
    )
    if share > 1:
        dk, dv = (
            low(lax.psum_scatter(d, "seq", scatter_dimension=0, tiled=True, axis_index_groups=near))
            for d in (dk, dv)
        )
    dqkv = jnp.concatenate([dq, dk, dv], axis=1)
    grad_qkv = dot(normed, dqkv, TN)
    dnorm, gain_one, shift_one = norm_back(dot(dqkv, w_qkv, NT), unit_one, rstd_one, gains[0])
    dh0 = dh1 + dnorm
    high = low(dh0)
    grad_pos = dot(high, lookup, TN) + dot(low(dh0 - high.astype(F32)), lookup, TN)
    grad_vec = jnp.concatenate(
        [gain_one[None], shift_one[None], grad_sums[2:6], jnp.sum(dh0, 0)[None], grad_sums[7:]]
    )
    small = jnp.concatenate([grad_head, dot(high, tokens, TN) + pad(grad_vec.T, 128)], axis=1)
    grads = [grad_down, grad_up, grad_attn, grad_qkv, grad_pos, small]
    parts = [
        scatter_rows(g.astype(F32), ways, order, F32 if g is small else BF16)
        for g, order in zip(grads, ("xy", "yx") * 3)
    ]
    squares = sum(jnp.sum(p * p) for p in parts)
    squares, total, valid = lax.psum((squares, jnp.sum(total), valid), ("dp", "seq"))
    down, up, attn, wide, table, small = [gather_parts(p, ways) for p in parts]
    pieces = [
        small[:, 128 + PATCH : 128 + 2 * PATCH].T,
        table.T,
        wide,
        attn,
        up,
        down.T,
        small[:, :outs],
        small[:, 128:136].T,
    ]
    norm = jnp.sqrt(squares) / valid
    clip = jnp.minimum(1.0, CLIP_AT / (norm + 1e-06))
    results = [
        adamw(
            masters[i],
            firsts[i],
            seconds[i],
            pieces[i] / valid * clip,
            RATE if i < 7 else VEC_RATE,
            DECAY if i < 7 else 0.0,
        )
        for i in range(8)
    ]
    return (
        total / math.log(2.0),
        valid,
        norm,
        *[r[0] for r in results],
        *[r[1] for r in results],
        *[r[2] for r in results],
    )


def solution(mesh):
    rows, columns = (P("dp", None), P(None, "dp"))
    weights = (columns, columns, rows, rows, rows, columns, rows, columns)
    in_specs = (P(None, "dp", None, "seq"), P(None, "dp", "seq")) + weights * 3
    out_specs = (P(), P(), P()) + weights * 3
    return jax.shard_map(body, mesh=mesh, in_specs=in_specs, out_specs=out_specs, check_vma=False)
```

```python
import functools
import math

import jax
import jax.numpy as jnp
from jax import lax
from jax.experimental import pallas as pl
from jax.experimental.pallas import tpu as pltpu
from jax.sharding import PartitionSpec as P

HEADS = 12
PATCH = 48
STEP = 10
RATE = 0.02
VEC_RATE = 0.15
BETA_ONE = 0.9
BETA_TWO = 0.95
ADAM_EPS = 1e-08
DECAY = 0.1
CLIP_AT = 0.01
NORM_EPS = 1e-05

F32 = jnp.float32
BF16 = jnp.bfloat16
WIRE = jnp.bfloat16
EARLY = [
    (0, 0, 1280, True),
    (0, 1280, 1024, True),
    (1, 0, 1024, False),
    (2, 0, 256, False),
]
LATE = [
    (0, 0, 1536, True),
    (0, 1536, 1536, True),
    (1, 0, 1536, True),
    (2, 0, 768, True),
    (1, 1536, 1536, False),
]
DEEP = [
    (0, 0, 768, "xy"),
    (1, 0, 768, "yx"),
    (0, 768, 768, "xy"),
    (1, 768, 768, "yx"),
    (0, 1536, 768, "xy"),
    (1, 1536, 768, "yx"),
    (0, 2304, 768, "xy"),
    (1, 2304, 768, "yx"),
]
REST = [
    (0, 0, 768, "yx"),
    (1, 0, 768, "xy"),
    (1, 768, 768, "xy"),
    (1, 1536, 768, "yx"),
    (2, 0, 512, "yx"),
    (2, 512, 512, "xy"),
    (3, 0, 256, "xy"),
]
NN = (((1,), (0,)), ((), ()))
NT = (((1,), (1,)), ((), ()))
TN = (((0,), (0,)), ((), ()))


PAIR, FIRST, OFFSET, SLOT_ID = range(2 * PATCH, 2 * PATCH + 4)


def dot(left, right, dims=NN):
    return lax.dot_general(left, right, dims, preferred_element_type=F32)


def lookup_of(aux, length):
    slot = lax.broadcasted_iota(jnp.int32, (aux.shape[0], length), 1).astype(F32)
    return (slot == aux[:, OFFSET : OFFSET + 1]).astype(F32).astype(BF16)


def tokens_of(aux):
    lane = lax.broadcasted_iota(jnp.int32, aux.shape, 1)
    return jnp.where((lane >= PATCH) & (lane < 2 * PATCH), aux, 0.0).astype(BF16)


def gains_of(small):
    return small[...].astype(F32).T[:8]


def line(axis, size, count, stride):
    place = (lax.axis_index(axis) // stride) % count
    swaps = [
        (axis, [(source, source ^ (step * stride)) for source in range(size)])
        for step in range(1, count)
    ]
    return (count, place, swaps)


def lines():
    n_dp, n_seq = lax.axis_size("dp"), lax.axis_size("seq")
    n_x = 1 << ((n_dp.bit_length() - 1) // 2)
    return {
        "z": line("dp", n_dp, n_dp // n_x, n_x),
        "x": line("dp", n_dp, n_x, 1),
        "y": line("seq", n_seq, n_seq // 2, 2),
        "core": line("seq", n_seq, 2, 1),
    }


def gather_line(block, along):
    count, place, swaps = along
    others = [lax.ppermute(block, axis, swap) for axis, swap in swaps]
    if count == 2:
        first = place == 0
        return jnp.stack([jnp.where(first, block, others[0]), jnp.where(first, others[0], block)])
    whole = jnp.zeros((count,) + block.shape, block.dtype)
    for step, piece in enumerate([block] + others):
        whole = lax.dynamic_update_index_in_dim(whole, piece, place ^ step, 0)
    return whole


def scatter_line(blocks, along, dim, wire):
    count, place, swaps = along
    pick = lambda index: lax.dynamic_index_in_dim(blocks, index, dim, keepdims=False)
    arrived = [
        lax.ppermute(pick(place ^ (step + 1)).astype(wire), axis, swap)
        for step, (axis, swap) in enumerate(swaps)
    ]
    total = pick(place)
    for piece in arrived:
        total = total + piece.astype(F32)
    return total


def gather_rows(shard, ways, split_y):
    n_core, core, _ = ways["core"]
    n_y, y_at, _ = ways["y"]
    rows, columns = shard.shape
    if split_y:
        part = lax.dynamic_slice_in_dim(
            shard, (core * n_y + y_at) * (rows // (2 * n_y)), rows // (2 * n_y), 0
        )
    else:
        part = lax.dynamic_slice_in_dim(shard, core * (rows // 2), rows // 2, 0)
    part = gather_line(part, ways["z"])
    part = gather_line(part, ways["x"])
    if split_y:
        part = gather_line(part, ways["y"])
        part = gather_line(part, ways["core"])
        part = jnp.transpose(part, (3, 2, 0, 1, 4, 5))
    else:
        part = gather_line(part, ways["core"])
        part = jnp.transpose(part, (2, 1, 0, 3, 4))
    return part.reshape(-1, columns)


def scatter_rows(grad, ways, order, wire):
    n_z, n_x, n_y = ways["z"][0], ways["x"][0], ways["y"][0]
    columns = grad.shape[1]
    blocks = grad.reshape(n_z, n_x, 2, n_y, -1, columns)
    blocks = scatter_line(blocks, ways["core"], 2, wire)
    if order == "xy":
        blocks = scatter_line(blocks, ways["x"], 1, wire)
        blocks = scatter_line(blocks, ways["y"], 1, wire)
    else:
        blocks = scatter_line(blocks, ways["y"], 2, wire)
        blocks = scatter_line(blocks, ways["x"], 1, wire)
    return scatter_line(blocks, ways["z"], 0, wire)


def gather_parts(part, ways):
    part = gather_line(part, ways["y"])
    part = gather_line(part, ways["core"])
    return part.reshape(-1, part.shape[-1])


MESH=pl.DeviceIdType.MESH
X = 2
Z = 4
def here():
    d=lax.axis_index("dp"); s=lax.axis_index("seq")
    return d//X, d%X, s//2, s%2
def peer(kz,kx,ky,kc):
    z,x,y,c=here()
    return ((z^kz)*X+(x^kx), (y^ky)*2+(c^kc))
class Gather:
    def __init__(s, src, dst, sems, base, split, lo, width):
        s.src,s.dst,s.split,s.lo,s.width=src,dst,split,lo,width
        s.send,s.recv=sems; s.n=base
        s.live=[]; s.rows=src.shape[0]
        s.idx={}
    def region(s,ref,kz,kx,half,ky,local=False):
        z,x,y,c=here(); r=s.rows//2
        row=(c^half)*r
        if not local: row=row+((z^kz)*X+(x^kx))*s.rows
        row=pl.multiple_of(row,16)
        if ky is None: return ref.at[pl.ds(row,r),pl.ds(s.lo,s.width)]
        w=s.width//2
        return ref.at[pl.ds(row,r),pl.ds(pl.multiple_of(s.lo+(y^ky)*w,128),w)]
    def copy(s,key,kz,kx,ky,to,own=False):
        i=s.idx.setdefault(key,s.n)
        if i==s.n: s.n+=1
        col=ky if s.split else None
        return pltpu.make_async_remote_copy(s.region(s.src if own else s.dst,kz,kx,0,col,own),s.region(s.dst,kz,kx,0,col),s.send.at[i],s.recv.at[i],device_id=peer(*to),device_id_type=MESH)
    def start(s,*a,**k):
        s.copy(*a,**k).start(); s.live.append((a,k))
    def begin(s):
        for k in (1,2,3): s.start(("z",k),0,0,0,(k,0,0,0),own=True)
        s.start(("x",0),0,0,0,(0,1,0,0),own=True)
    def after_z(s,k):
        s.recvd(("z",k),k,0,0)
        s.start(("x",k),k,0,0,(0,1,0,0))
        if s.split: s.start(("y",k,0),k,0,0,(0,0,1,0))
        s.start(("c",k,0),k,0,0,(0,0,0,1))
    def after_x(s,k):
        s.recvd(("x",k),k,1,0)
        if s.split: s.start(("y",k,1),k,1,0,(0,0,1,0))
        s.start(("c",k,1),k,1,0,(0,0,0,1))
    def after_y(s,k,kx):
        s.recvd(("y",k,kx),k,kx,1)
        s.start(("d",k,kx),k,kx,1,(0,0,0,1))
    def recvd(s,key,kz,kx,ky):
        s.copy(key,kz,kx,ky,(0,0,0,1)).wait_recv()
    def stage_z(s):
        for k in (1,2,3): s.after_z(k)
    def stage_x(s):
        for k in range(4): s.after_x(k)
    def stage_y(s):
        if s.split:
            for kx in range(2):
                for k in range(4):
                    if k or kx: s.after_y(k,kx)
    def finish(s):
        for k in range(4):
            for kx in range(2):
                if (k or kx):
                    s.core_recv(("c",k,kx),k,kx,0)
                    if s.split: s.core_recv(("d",k,kx),k,kx,1)
        for a,k in s.live: s.copy(*a,**k).wait_send()
    def core_recv(s,key,kz,kx,ky):
        i=s.idx[key]; col=ky if s.split else None
        r=s.region(s.dst,kz,kx,1,col)
        pltpu.make_async_remote_copy(r,r,s.send.at[i],s.recv.at[i],device_id=peer(0,0,0,1),device_id_type=MESH).wait_recv()

def greet(peers):
    bar=pltpu.get_barrier_semaphore()
    for p in peers: pl.semaphore_signal(bar,inc=1,device_id=peer(*p),device_id_type=MESH)
    pl.semaphore_wait(bar,len(peers))
PEERS=[(1,0,0,0),(2,0,0,0),(3,0,0,0),(0,1,0,0),(0,0,1,0),(0,0,0,1)]
class Own:
    def __init__(s,*refs): s.refs=refs
    def copy(s):
        src,dst,sem=s.refs
        z,x,y,c=here(); r=src.shape[0]
        return pltpu.make_async_copy(src,dst.at[pl.ds(pl.multiple_of((z*X+x)*r,16),r),:],sem)
    def start(s): s.copy().start()
    def wait(s): s.copy().wait()
def open_chunks(chunks,src,dst,send,recv,loc):
    mine=[Own(src[i],dst[i],loc.at[i]) for i in range(len(src))]
    g=[]; base=0
    for (t,lo,w,sp) in chunks:
        g.append(Gather(src[t],dst[t],(send,recv),base,sp,lo,w)); base+=28 if sp else 14
    return mine,g
def about_slots(row,seg):
    ids=seg[...]; length=ids.shape[1]
    slot=lax.broadcasted_iota(jnp.int32,ids.shape,1)
    begins=jnp.zeros_like(ids)
    for image in range(5):
        before=(ids>0)&(ids<image) if image else ids>0
        begins=jnp.where(ids==image,jnp.sum(before.astype(F32),axis=1,keepdims=True).astype(jnp.int32),begins)
    offset=slot-begins
    after=jnp.where(slot==length-1,0,pltpu.roll(ids,length-1,1))
    pair=((ids==after)&(ids>0)).astype(F32)
    first=((ids>0)&(offset==0)).astype(F32)
    x=row[...].astype(F32)
    later=jnp.where(lax.broadcasted_iota(jnp.int32,x.shape,1)==length-1,0.0,pltpu.roll(x,length-1,1))
    line=lax.broadcasted_iota(jnp.int32,(128-2*PATCH,length),0)
    more=jnp.zeros(line.shape,F32)
    for i,v in enumerate((pair,first,offset.astype(F32),ids.astype(F32))): more=jnp.where(line==i,v,more)
    return jnp.concatenate([later,x,more],axis=0).T
def semaphores(chunks,n):
    tot=sum(28 if s[3] else 14 for s in chunks)
    return [pltpu.SemaphoreType.DMA((tot,)),pltpu.SemaphoreType.DMA((tot,)),pltpu.SemaphoreType.DMA((n,))]
PER=8
class Reduce:
    def __init__(s,g,out,bufs,sems,base,lo,w,order):
        s.g,s.out,s.lo,s.w,s.order=g,out,lo,w,order
        s.r1,s.p2,s.r2,s.p3,s.r3,s.p4,s.r4=bufs
        s.send,s.recv=sems; s.base=base; s.r=g.shape[3]
    def col(s,ky,lo=0):
        z,x,y,c=here(); h=s.w//2
        return pl.ds(pl.multiple_of(lo+(y^ky)*h,128),h)
    def remote(s,src,dst,i,to):
        return pltpu.make_async_remote_copy(src,dst,s.send.at[s.base+i],s.recv.at[s.base+i],device_id=peer(*to),device_id_type=MESH)
    def c1(s):
        z,x,y,c=here()
        return s.remote(s.g.at[:,:,1-c,:,pl.ds(s.lo,s.w)],s.r1,0,(0,0,0,1))
    def begin(s): s.c1().start()
    def two(s,zz,xx,ky=None):
        z,x,y,c=here()
        cols=slice(None) if ky is None else s.col(ky)
        own=s.g[zz,xx,c,:,pl.ds(s.lo,s.w) if ky is None else s.col(ky,s.lo)]
        return own.astype(F32)+s.r1[zz,xx,:,cols].astype(F32)
    def three(s,zz,xx,ky):
        if s.order=="xy": return s.two(zz,xx,ky)+s.r2[zz,:,s.col(ky)].astype(F32)
        return s.two(zz,xx,ky)+s.r2[zz,xx].astype(F32)
    def four(s,zz):
        z,x,y,c=here()
        return s.three(zz,x,0)+s.r3[zz].astype(F32)
    def c2(s): return s.remote(s.p2,s.r2,1,(0,1,0,0) if s.order=="xy" else (0,0,1,0))
    def c3(s): return s.remote(s.p3,s.r3,2,(0,0,1,0) if s.order=="xy" else (0,1,0,0))
    def c4(s,k): return s.remote(s.p4.at[k-1],s.r4.at[k-1],2+k,(k,0,0,0))
    def c5(s):
        z,x,y,c=here()
        ref=s.out.at[pl.ds(pl.multiple_of(c*s.r,8),s.r),s.col(0,s.lo)]
        return s.remote(ref,ref,6,(0,0,1,0))
    def c6(s):
        z,x,y,c=here()
        ref=s.out.at[pl.ds(pl.multiple_of(c*s.r,8),s.r),pl.ds(s.lo,s.w)]
        return s.remote(ref,ref,7,(0,0,0,1))
    def stage1(s):
        z,x,y,c=here()
        s.c1().wait_recv()
        @pl.loop(0,Z)
        def _(zz):
            if s.order=="xy":
                s.p2[zz]=s.two(zz,1-x).astype(s.p2.dtype)
            else:
                for xx in range(X): s.p2[zz,xx]=s.two(zz,xx,1).astype(s.p2.dtype)
        s.c2().start()
    def stage2(s):
        z,x,y,c=here()
        s.c2().wait_recv()
        @pl.loop(0,Z)
        def _(zz):
            s.p3[zz]=(s.three(zz,x,1) if s.order=="xy" else s.three(zz,1-x,0)).astype(s.p3.dtype)
        s.c3().start()
    def stage3(s):
        z,x,y,c=here()
        s.c3().wait_recv()
        for k in (1,2,3):
            s.p4[k-1]=s.four(z^k).astype(s.p4.dtype)
            s.c4(k).start()
    def stage4(s):
        z,x,y,c=here()
        total=s.four(z)
        for k in (1,2,3):
            s.c4(k).wait_recv()
            total=total+s.r4[k-1].astype(F32)
        s.out[pl.ds(pl.multiple_of(c*s.r,8),s.r),s.col(0,s.lo)]=total
        s.c5().start()
        return total
    def stage5(s):
        s.c5().wait_recv()
        s.c6().start()
    def finish(s):
        s.c6().wait_recv()
        s.c1().wait_send(); s.c2().wait_send(); s.c3().wait_send()
        for k in (1,2,3): s.c4(k).wait_send()
        s.c5().wait_send(); s.c6().wait_send()

def shapes(r,w,order,dt):
    h=w//2
    two=(Z,r,w) if order=="xy" else (Z,X,r,h)
    return [((Z,X,r,w),dt)]+[(two,dt)]*2+[((Z,r,h),dt)]*2+[((3,r,h),dt)]*2
def reducers(chunks,g,out,bufs,send,recv):
    return [Reduce(g[t],out[t],bufs[7*i:7*i+7],(send,recv),PER*i,lo,w,o) for i,(t,lo,w,o) in enumerate(chunks)]

def totals(part,got,send,recv,base):
    d=lax.axis_index("dp"); q=lax.axis_index("seq")
    def hop(first,count,mine,peers):
        got[first+mine]=part[...]
        cs=[pltpu.make_async_remote_copy(part,got.at[first+mine],send.at[base+first+i],recv.at[base+first+i],device_id=p,device_id_type=MESH) for i,p in enumerate(peers)]
        for k in cs: k.start()
        for k in cs: k.wait()
        t=got[first]
        for i in range(1,count): t=t+got[first+i]
        part[...]=t
    hop(0,4,q,[peer(0,0,ky,kc) for ky,kc in ((0,1),(1,0),(1,1))])
    hop(4,8,d,[peer(kz,kx,0,0) for kz,kx in ((0,1),(1,0),(1,1),(2,0),(2,1),(3,0),(3,1))])

ALL=[(0,0,ky,kc) for ky,kc in ((0,1),(1,0),(1,1))]+[(kz,kx,0,0) for kz,kx in ((0,1),(1,0),(1,1),(2,0),(2,1),(3,0),(3,1))]
def fold(v):
    v=v*v
    t=jnp.zeros((8,128),F32)
    for i in range(v.shape[0]//8):
        for j in range(v.shape[1]//128):
            t=t+v[8*i:8*i+8,128*j:128*j+128]
    return t


def hide(bias, tile, skip, sq_ref, sk, qp_ref):
    for step in range(bias.shape[1] // tile):
        rows = slice(step * tile, (step + 1) * tile)
        keys = (step + 1) * tile if skip else bias.shape[0]
        pos_key = lax.broadcasted_iota(jnp.int32, (keys, tile), 0)
        if qp_ref is None:
            pos = lax.broadcasted_iota(jnp.int32, (1, tile), 1) + step * tile
        else:
            pos = qp_ref[:, rows]
        allowed = (sk[:keys, :] == sq_ref[:, rows]) & (pos_key <= pos)
        bias[:keys, rows] = jnp.where(allowed, 0.0, -1e30)


def head_forward(tile, skip, hd, scale, q_ref, k_ref, v_ref, bias, o_ref, lse_ref):
    length = k_ref.shape[0]
    for head in range(q_ref.shape[1] // hd):
        cols = slice(hd * head, hd * head + hd)
        for step in range(q_ref.shape[0] // tile):
            rows = slice(step * tile, (step + 1) * tile)
            keys = (step + 1) * tile if skip else length
            query = (q_ref[rows, cols].astype(F32) * scale).astype(BF16)
            scores = dot(k_ref[:keys, cols], query, NT) + bias[:keys, rows]
            top = jnp.max(scores, 0, keepdims=True)
            weight = jnp.exp(scores - top)
            total = jnp.sum(weight, 0, keepdims=True)
            probs = (weight * (1.0 / total)).astype(BF16)
            o_ref[rows, cols] = dot(probs, v_ref[:keys, cols], TN).astype(BF16)
            lse_ref[0, head : head + 1, rows] = top + jnp.log(total)


def attend_kernel(tile, skip, hd, scale, q_ref, k_ref, v_ref, sq_ref, sk_ref, qp_ref, o_ref, lse_ref, bias):
    @pl.when(pl.program_id(0) == 0)
    def _():
        hide(bias, tile, skip, sq_ref, sk_ref, qp_ref)

    head_forward(tile, skip, hd, scale, q_ref, k_ref, v_ref, bias, o_ref, lse_ref)


def front_kernel(tiles, lanes, shape, early, late, pieces, ids, *refs):
    wide, src = refs[:6], refs[-6:]
    aux, sq_ref, count, h0_ref, normed_ref, qkv_ref, o_ref, lse_ref = refs[6:14]
    wq_out, ws_out, *dst = refs[14:19]
    wq, wp, ws, qkv, bias, gains_all, row, seg = refs[19:27]
    send, recv, loc, late_send, late_recv, late_loc, psend, precv, leave = refs[27:-6]
    step = pl.program_id(0)
    mine, e = open_chunks(early, src[:3], (wq, wp, ws), send, recv, loc)
    mine_late, g = open_chunks(late, src[3:], dst, late_send, late_recv, late_loc)
    group = pieces.shape[2]

    def when(index, *stages):
        @pl.when(step == index)
        def _():
            for stage in stages:
                stage()

    def out(i):
        pair = ((wq, wq_out), (ws, ws_out))[i]
        return pltpu.make_async_copy(*pair, leave.at[i])

    def begin():
        greet(PEERS + [(0, 0, 1, 1)])
        q = lax.axis_index("seq")
        at = pl.ds(pl.multiple_of(q * group, 128), group)
        swaps = []
        for k, to in ((1, (0, 0, 0, 1)), (2, (0, 0, 1, 0)), (3, (0, 0, 1, 1))):
            for j, (a, b) in enumerate(
                ((pieces.at[q ^ k], row.at[:, at]), (ids.at[q ^ k], seg.at[:, at]))
            ):
                i = 2 * (k - 1) + j
                swaps.append(
                    pltpu.make_async_remote_copy(
                        a, b, psend.at[i], precv.at[i], device_id=peer(*to), device_id_type=MESH
                    )
                )
                swaps[-1].start()

        def narrow(*which):
            for i in which:
                src[i][...] = wide[i][...].astype(BF16)

        narrow(0)
        e[0].begin()
        e[1].begin()
        narrow(1, 2)
        for a in mine:
            a.start()
        narrow(3, 4, 5)
        for a in mine_late:
            a.start()
        row[:, at] = pieces[q]
        seg[:, at] = ids[q]
        for a in swaps:
            a.wait()
        aux[...] = about_slots(row, seg)
        sq_ref[...] = seg[...].astype(F32)
        down, across = [lax.broadcasted_iota(jnp.int32, count.shape, i) for i in range(2)]
        held = jnp.sum((seg[...] > 0).astype(F32), axis=1, keepdims=True)
        count[...] = jnp.where((down == 0) & (across == 0), held * PATCH, 0.0)
        e[0].stage_z()
        e[2].begin()
        e[3].begin()
        e[1].stage_z()
        g[0].begin()
        e[0].stage_x()
        e[2].stage_z()
        e[3].stage_z()
        g[1].begin()
        e[1].stage_x()
        e[0].stage_y()
        e[2].stage_x()
        e[3].stage_x()
        e[1].stage_y()
        for a in e:
            a.finish()
        for a in mine:
            a.wait()
        out(0).start()
        out(1).start()
        gains_all[...] = gains_of(ws.at[:, 128:])
        g[0].stage_z()
        g[2].begin()

    when(0, begin)
    when(2, g[1].stage_z, g[3].begin, g[0].stage_x)
    when(4, g[2].stage_z, g[4].begin, g[1].stage_x)
    when(5, g[0].stage_y, g[3].stage_z)
    when(6, g[2].stage_x)
    when(7, g[1].stage_y, g[3].stage_x)
    when(8, g[4].stage_z)
    when(9, g[2].stage_y)

    @pl.when(step < tiles)
    def _():
        tile, length = h0_ref.shape[0], wp.shape[1]
        rows = pl.ds(pl.multiple_of(jnp.minimum(step, tiles - 1) * tile, tile), tile)
        slots = aux[rows, :]
        gains = gains_all[...]
        h0 = dot(lookup_of(slots, length), wp[...], NT) + dot(tokens_of(slots), ws[:, 128:], NT)
        h0 = h0 + (gains[6:7] - 1.0)
        h0_ref[...] = h0
        unit, _ = norm_rows(h0)
        normed = (unit * gains[0:1] + (gains[1:2] - 1.0)).astype(BF16)
        normed_ref[...] = normed
        value = dot(normed, wq[...]).astype(BF16)
        qkv_ref[...] = value
        qkv[rows, :] = value

    @pl.when(step >= tiles)
    def _():
        pair = step - tiles
        width = qkv.shape[1] // 3

        @pl.when(pair == 0)
        def _():
            hide(bias, *shape[:2], sq_ref, aux[:, SLOT_ID : SLOT_ID + 1], None)

        part = lambda i: qkv.at[:, pl.ds(pl.multiple_of(i * width + pair * lanes, lanes), lanes)]
        head_forward(*shape, part(0), part(1), part(2), bias, o_ref, lse_ref)

    def drain():
        g[4].stage_x()
        g[3].stage_y()
        g[4].stage_y()
        for a in g:
            a.finish()
        for a in mine_late:
            a.wait()
        out(0).wait()
        out(1).wait()

    when(pl.num_programs(0) - 1, drain)


def front(pieces, ids, early_shards, late_shards, early, late):
    count, dp = pieces.shape[2] * lax.axis_size("seq"), lax.axis_size("dp")
    shards = [*early_shards, *late_shards]
    full = [jax.ShapeDtypeStruct((v.shape[0] * dp, v.shape[1]), BF16) for v in shards]
    width = full[0].shape[0]
    hd = width // HEADS
    lanes, pairs, tile = 2 * hd, HEADS // 2, 256
    tiles = count // tile
    once = lambda shape: pl.BlockSpec(
        shape, lambda i: (0,) * len(shape), pipeline_mode=pl.Buffered(1)
    )
    row = lambda columns: pl.BlockSpec((tile, columns), lambda i: (jnp.minimum(i, tiles - 1), 0))
    after = lambda i: jnp.maximum(i - tiles, 0)
    anywhere = pl.BlockSpec(memory_space=pl.ANY)
    ids = ids[:, None, :]
    landing = [pltpu.VMEM(v.shape, v.dtype) for v in full[:3]]
    return pl.pallas_call(
        functools.partial(front_kernel, tiles, lanes, (tile, True, hd, hd**-0.5), early, late),
        grid=(tiles + pairs,),
        in_specs=[once(pieces.shape), once(ids.shape)]
        + [once(v.shape) for v in shards],
        out_specs=[
            once((count, 128)),
            once((1, count)),
            once((8, 128)),
            row(width),
            row(width),
            row(3 * width),
            pl.BlockSpec((count, lanes), lambda i: (0, after(i))),
            pl.BlockSpec((1, 2, count), lambda i: (after(i), 0, 0)),
        ]
        + [anywhere] * 5,
        out_shape=[
            jax.ShapeDtypeStruct((count, 128), F32),
            jax.ShapeDtypeStruct((1, count), F32),
            jax.ShapeDtypeStruct((8, 128), F32),
            jax.ShapeDtypeStruct((count, width), F32),
            jax.ShapeDtypeStruct((count, width), BF16),
            jax.ShapeDtypeStruct((count, 3 * width), BF16),
            jax.ShapeDtypeStruct((count, width), BF16),
            jax.ShapeDtypeStruct((pairs, 2, count), F32),
            full[0],
            full[2],
            *full[3:],
        ],
        scratch_shapes=landing
        + [
            pltpu.VMEM((count, 3 * width), BF16),
            pltpu.VMEM((count, count), F32),
            pltpu.VMEM((8, width), F32),
            pltpu.VMEM((pieces.shape[1], count), pieces.dtype),
            pltpu.VMEM((1, count), ids.dtype),
        ]
        + semaphores(early, 3)
        + semaphores(late, 3)
        + [pltpu.SemaphoreType.DMA((6,)), pltpu.SemaphoreType.DMA((6,)), pltpu.SemaphoreType.DMA((2,))]
        + [pltpu.VMEM(v.shape, BF16) for v in shards],
        compiler_params=pltpu.CompilerParams(
            collective_id=4, has_side_effects=True, vmem_limit_bytes=60 * 2**20
        ),
    )(pieces, ids, *shards)


def head_back(
    tile, skip, hd, scale, q_ref, k_ref, v_ref, do_ref, lse_ref, bias, dq_ref, dk_ref, dv_ref,
    dk_sum, dv_sum, before=lambda head: None,
):
    length = k_ref.shape[0]
    dk_sum[...] = jnp.zeros_like(dk_sum)
    dv_sum[...] = jnp.zeros_like(dv_sum)
    for head in range(q_ref.shape[1] // hd):
        cols = slice(hd * head, hd * head + hd)
        before(head)
        for step in range(q_ref.shape[0] // tile):
            rows = slice(step * tile, (step + 1) * tile)
            keys = (step + 1) * tile if skip else length
            query = (q_ref[rows, cols].astype(F32) * scale).astype(BF16)
            key = k_ref[:keys, cols]
            dout = do_ref[rows, cols]
            scores = dot(key, query, NT) + bias[:keys, rows]
            probs = jnp.exp(scores - lse_ref[0, head : head + 1, rows])
            dprobs = dot(v_ref[:keys, cols], dout, NT)
            delta = jnp.sum(dprobs * probs, 0, keepdims=True)
            dscores = (probs * (dprobs - delta)).astype(BF16)
            dv_sum[:keys, cols] += dot(probs.astype(BF16), dout)
            dk_sum[:keys, cols] += dot(dscores, query)
            dq_ref[rows, cols] = (dot(dscores, key, TN) * scale).astype(dq_ref.dtype)
    dk_ref[...] = dk_sum[...].astype(dk_ref.dtype)
    dv_ref[...] = dv_sum[...].astype(dv_ref.dtype)


def attend_back_kernel(
    tile, skip, hd, scale, q_ref, k_ref, v_ref, do_ref, lse_ref, sq_ref, sk_ref, qp_ref,
    dq_ref, dk_ref, dv_ref, dk_sum, dv_sum, bias,
):
    @pl.when(pl.program_id(0) == 0)
    def _():
        hide(bias, tile, skip, sq_ref, sk_ref, qp_ref)

    head_back(
        tile, skip, hd, scale, q_ref, k_ref, v_ref, do_ref, lse_ref, bias, dq_ref, dk_ref, dv_ref,
        dk_sum, dv_sum,
    )


def attend_back_deep_kernel(
    parts, shape, chunks, m_ref, dd_ref, hid_ref, du_ref, q_ref, k_ref, v_ref, do_ref, lse_ref,
    sq_ref, aux_ref, dq_ref, dk_ref, dv_ref, squares, down_ref, up_ref, dk_sum, dv_sum, bias,
    g_down, g_up, down, up, send, recv, leave, *bufs,
):
    step = pl.program_id(0)
    width, wide = m_ref.shape[1], hid_ref.shape[1]
    R = reducers(chunks, (g_down, g_up), (down, up), bufs, send, recv)
    pairs = [R[2 * j : 2 * j + 2] for j in range(parts)]
    every = lambda name, j: lambda: [getattr(a, name)() for a in pairs[j]]

    def last(j):
        def run():
            for a in pairs[j]:
                squares[...] += fold(a.stage4())

        return run

    def when(index, *stages):
        @pl.when(step == index)
        def _():
            for stage in stages:
                stage()

    def first():
        greet(PEERS)
        squares[...] = jnp.zeros_like(squares)

    when(0, first)
    place = lambda value: value.astype(BF16).reshape(Z, X, 2, width // (2 * X * Z), wide)
    for j in range(parts):

        @pl.when(step == j)
        def _():
            cols = slice(j * wide, (j + 1) * wide)
            g_down[:, :, :, :, cols] = place(dot(dd_ref[...], hid_ref[...], TN))
            pairs[j][0].begin()
            g_up[:, :, :, :, cols] = place(dot(m_ref[...], du_ref[...], TN))
            pairs[j][1].begin()
            if j == 1:
                every("stage1", 0)()
            if j == 3:
                every("stage1", 1)()

    when(parts, lambda: hide(bias, *shape[:2], sq_ref, aux_ref[:, SLOT_ID : SLOT_ID + 1], None))
    moves = {
        1: [every("stage2", 0)],
        2: [every("stage1", 2)],
        4: [every("stage2", 1), every("stage3", 0)],
        5: [every("stage1", 3)],
        7: [every("stage2", 2), every("stage3", 1), last(0)],
        9: [every("stage2", 3)],
        10: [every("stage3", 2), last(1), every("stage5", 0)],
        11: [every("stage3", 3)],
    }

    def before(head):
        for half, stages in moves.items():
            if half % 2 == head:
                when(parts + half // 2, *stages)

    @pl.when(step >= parts)
    def _():
        head_back(
            *shape, q_ref, k_ref, v_ref, do_ref, lse_ref, bias, dq_ref, dk_ref, dv_ref, dk_sum,
            dv_sum, before,
        )

    def drain():
        last(2)()
        every("stage5", 1)()
        last(3)()
        every("stage5", 2)()
        every("stage5", 3)()
        for a in R:
            a.finish()
        copies = [
            pltpu.make_async_copy(down, down_ref, leave.at[0]),
            pltpu.make_async_copy(up, up_ref, leave.at[1]),
        ]
        for c in copies:
            c.start()
        for c in copies:
            c.wait()

    when(9, drain)


def blocks_of(rows, width, offset):
    return pl.BlockSpec((rows, width), lambda pair: (0, pair + offset))


def fixed(shape):
    return pl.BlockSpec(shape, lambda pair: (0, 0))


def kernel_params():
    return pltpu.CompilerParams(vmem_limit_bytes=48 * 2**20)


def attend(qkv, keys, values, offsets, seg_q, seg_k, pos_q, width):
    count, length = qkv.shape[0], keys.shape[0]
    hd = width // HEADS
    lanes = 2 * hd
    pairs = HEADS // 2
    return pl.pallas_call(
        functools.partial(attend_kernel, min(256, count), count == length, hd, hd**-0.5),
        grid=(pairs,),
        in_specs=[
            blocks_of(count, lanes, 0),
            blocks_of(length, lanes, offsets[0]),
            blocks_of(length, lanes, offsets[1]),
            fixed((1, count)),
            fixed((length, 1)),
            fixed((1, count)),
        ],
        out_specs=[blocks_of(count, lanes, 0), pl.BlockSpec((1, 2, count), lambda pair: (pair, 0, 0))],
        out_shape=[
            jax.ShapeDtypeStruct((count, width), BF16),
            jax.ShapeDtypeStruct((pairs, 2, count), F32),
        ],
        scratch_shapes=[pltpu.VMEM((length, count), F32)],
        cost_estimate=pl.CostEstimate(
            flops=25_000_000_000, bytes_accessed=8_000_000, transcendentals=8_000_000
        ),
        compiler_params=kernel_params(),
    )(qkv, keys, values, seg_q, seg_k, pos_q)


def attend_back(qkv, keys, values, offsets, dout, lse, seg_q, seg_k, pos_q, width, kv_type):
    count, length = qkv.shape[0], keys.shape[0]
    hd = width // HEADS
    lanes = 2 * hd
    pairs = HEADS // 2
    return pl.pallas_call(
        functools.partial(attend_back_kernel, min(256, count), count == length, hd, hd**-0.5),
        grid=(pairs,),
        in_specs=[
            blocks_of(count, lanes, 0),
            blocks_of(length, lanes, offsets[0]),
            blocks_of(length, lanes, offsets[1]),
            blocks_of(count, lanes, 0),
            pl.BlockSpec((1, 2, count), lambda pair: (pair, 0, 0)),
            fixed((1, count)),
            fixed((length, 1)),
            fixed((1, count)),
        ],
        out_specs=[
            blocks_of(count, lanes, 0),
            blocks_of(length, lanes, 0),
            blocks_of(length, lanes, 0),
        ],
        out_shape=[
            jax.ShapeDtypeStruct((count, width), BF16),
            jax.ShapeDtypeStruct((length, width), kv_type),
            jax.ShapeDtypeStruct((length, width), kv_type),
        ],
        scratch_shapes=[pltpu.VMEM((length, lanes), F32)] * 2 + [pltpu.VMEM((length, count), F32)],
        compiler_params=kernel_params(),
    )(qkv, keys, values, dout, lse, seg_q, seg_k, pos_q)


def attend_back_deep(qkv, dout, lse, seg_q, aux, mixed, ddown, hidden, dupper, chunks):
    count, width = mixed.shape
    hd = width // HEADS
    lanes, pairs, parts = 2 * hd, HEADS // 2, hidden.shape[1] // width
    r = width // (2 * X * Z)
    pair = lambda offset: pl.BlockSpec(
        (count, lanes), lambda i: (0, offset + jnp.maximum(i - parts, 0))
    )
    column = pl.BlockSpec((count, width), lambda i: (0, jnp.minimum(i, parts - 1)))
    once = lambda shape: pl.BlockSpec(shape, lambda i: (0, 0), pipeline_mode=pl.Buffered(1))
    heads = jax.ShapeDtypeStruct((count, width), BF16)
    total = jax.ShapeDtypeStruct((2 * r, hidden.shape[1]), F32)
    ns = PER * len(chunks)
    return pl.pallas_call(
        functools.partial(attend_back_deep_kernel, parts, (256, True, hd, hd**-0.5), chunks),
        grid=(parts + pairs,),
        in_specs=[
            once((count, width)),
            once((count, width)),
            column,
            column,
            pair(0),
            pair(pairs),
            pair(2 * pairs),
            pair(0),
            pl.BlockSpec((1, 2, count), lambda i: (jnp.maximum(i - parts, 0), 0, 0)),
            once((1, count)),
            once((count, 128)),
        ],
        out_specs=[pair(0), pair(0), pair(0), once((8, 128))]
        + [pl.BlockSpec(memory_space=pl.ANY)] * 2,
        out_shape=[heads, heads, heads, jax.ShapeDtypeStruct((8, 128), F32), total, total],
        scratch_shapes=[
            pltpu.VMEM((count, lanes), F32),
            pltpu.VMEM((count, lanes), F32),
            pltpu.VMEM((count, count), F32),
            pltpu.VMEM((Z, X, 2, r, hidden.shape[1]), BF16),
            pltpu.VMEM((Z, X, 2, r, hidden.shape[1]), BF16),
            pltpu.VMEM(total.shape, F32),
            pltpu.VMEM(total.shape, F32),
            pltpu.SemaphoreType.DMA((ns,)),
            pltpu.SemaphoreType.DMA((ns,)),
            pltpu.SemaphoreType.DMA((2,)),
        ]
        + [pltpu.VMEM(*b) for (t, lo, w, o) in chunks for b in shapes(r, w, o, BF16)],
        compiler_params=pltpu.CompilerParams(
            collective_id=3, has_side_effects=True, vmem_limit_bytes=60 * 2**20
        ),
    )(mixed, ddown, hidden, dupper, qkv, qkv, qkv, dout, lse, seg_q, aux)


def layer_norm(hidden, gain, shift):
    mean = jnp.mean(hidden, -1, keepdims=True)
    centred = hidden - mean
    var = jnp.mean(centred * centred, -1, keepdims=True)
    rstd = lax.rsqrt(var + NORM_EPS)
    unit = centred * rstd
    return (unit * gain + shift, unit, rstd)


def norm_back(grad, unit, rstd, gain):
    dunit = grad * gain
    dhid = rstd * (
        dunit
        - jnp.mean(dunit, -1, keepdims=True)
        - unit * jnp.mean(dunit * unit, -1, keepdims=True)
    )
    return (dhid, jnp.sum(grad * unit, 0), jnp.sum(grad, 0))


def adamw(weight, first, second, grad, rate, decay):
    new_first = BETA_ONE * first + (1.0 - BETA_ONE) * grad
    new_second = BETA_TWO * second + (1.0 - BETA_TWO) * grad * grad
    first_hat = new_first / (1.0 - BETA_ONE**STEP)
    second_hat = new_second / (1.0 - BETA_TWO**STEP)
    return (
        weight - rate * (first_hat / (jnp.sqrt(second_hat) + ADAM_EPS) + decay * weight),
        new_first,
        new_second,
    )


def norm_rows(hidden):
    mean = jnp.mean(hidden, -1, keepdims=True)
    centred = hidden - mean
    rstd = lax.rsqrt(jnp.mean(centred * centred, -1, keepdims=True) + NORM_EPS)
    return centred * rstd, rstd


def norm_rows_back(grad, unit, rstd, gain):
    dunit = grad * gain
    return rstd * (
        dunit
        - jnp.mean(dunit, -1, keepdims=True)
        - unit * jnp.mean(dunit * unit, -1, keepdims=True)
    )


def add_rows(ref, row, value):
    ref[row : row + 1, :] += jnp.sum(value, 0, keepdims=True)


GELU_A = math.sqrt(2.0 / math.pi)
GELU_B = 0.044715


def mlp_kernel(
    wide, o_ref, h0_ref, aux_ref, ws_ref, wa_far, wu_far, wd_far, wh_ref,
    do_ref, dh1_ref, dat_ref, m_ref, hid_ref, dd_ref, du_ref, ghead_ref, sums_ref, loss_ref,
    slope, gains_all, wa_ref, wu_ref, wd_ref, enter,
):
    step = pl.program_id(0)
    pairs = ((wa_far, wa_ref), (wu_far, wu_ref), (wd_far, wd_ref))
    bring = lambda i: pltpu.make_async_copy(*pairs[i], enter.at[i])

    def arrived(*which):
        @pl.when(step == 0)
        def _():
            for i in which:
                bring(i).wait()

    tile, width = h0_ref.shape
    blocks = [slice(j, j + wide) for j in range(0, wu_ref.shape[1], wide)]

    @pl.when(step == 0)
    def _():
        for i in range(len(pairs)):
            bring(i).start()
        gains_all[...] = gains_of(ws_ref)
        sums_ref[...] = jnp.zeros_like(sums_ref)
        loss_ref[...] = jnp.zeros_like(loss_ref)
        ghead_ref[...] = jnp.zeros_like(ghead_ref)

    gains = gains_all[...]
    o = o_ref[...]
    arrived(0)
    h1 = h0_ref[...] + dot(o, wa_ref[...]) + (gains[7:8] - 1.0)
    unit_two, rstd_two = norm_rows(h1)
    m = (unit_two * gains[2:3] + (gains[3:4] - 1.0)).astype(BF16)
    m_ref[...] = m
    h2 = h1
    arrived(1, 2)
    for b in blocks:
        u = dot(m, wu_ref[:, b])
        square = u * u
        cube = (GELU_A * GELU_B) * square
        one = 1.0 + jnp.tanh(u * (GELU_A + cube))
        half = 0.5 * u
        hid = (half * one).astype(BF16)
        slope[:, b] = one * (0.5 + half * (2.0 - one) * (GELU_A + 3.0 * cube))
        hid_ref[:, b] = hid
        h2 = h2 + dot(hid, wd_ref[:, b], NT)
    unit_fin, rstd_fin = norm_rows(h2)
    final = (unit_fin * gains[4:5] + (gains[5:6] - 1.0)).astype(BF16)
    out = dot(final, wh_ref[...])
    aux = aux_ref[...]
    lane = lax.broadcasted_iota(jnp.int32, out.shape, 1)
    used = lane < PATCH
    pair, first = aux[:, PAIR : PAIR + 1], aux[:, FIRST : FIRST + 1]
    alpha = jnp.where(used, pltpu.roll(out, 128 - PATCH, 1), 0.0)
    plain = jnp.where(used, pltpu.roll(aux, 128 - PATCH, 1), 0.0)
    shrink = jnp.exp(-alpha)
    scaled = jnp.where(used, aux - out, 0.0) * shrink
    term = pair * (0.5 * scaled * scaled + alpha) + first * (0.5 * plain * plain)
    loss_ref[...] += jnp.sum(term.reshape(tile // 8, 8, 128), 0)
    dmu = -pair * scaled * shrink
    dalpha = pltpu.roll(jnp.where(used, pair * (1.0 - scaled * scaled), 0.0), PATCH, 1)
    dout = jnp.where(used, dmu, dalpha).astype(BF16)
    ghead_ref[...] += dot(final, dout, TN)
    dfinal = dot(dout, wh_ref[...], NT)
    add_rows(sums_ref, 4, dfinal * unit_fin)
    add_rows(sums_ref, 5, dfinal)
    dh2 = norm_rows_back(dfinal, unit_fin, rstd_fin, gains[4:5])
    dd = dh2.astype(BF16)
    dd_ref[...] = dd
    dmixed = jnp.zeros((tile, width), F32)
    for b in blocks:
        du = (dot(dd, wd_ref[:, b]) * slope[:, b]).astype(BF16)
        du_ref[:, b] = du
        dmixed = dmixed + dot(du, wu_ref[:, b], NT)
    add_rows(sums_ref, 2, dmixed * unit_two)
    add_rows(sums_ref, 3, dmixed)
    dh1 = dh2 + norm_rows_back(dmixed, unit_two, rstd_two, gains[2:3])
    add_rows(sums_ref, 7, dh1)
    dh1_ref[...] = dh1
    dat = dh1.astype(BF16)
    dat_ref[...] = dat
    do_ref[...] = dot(dat, wa_ref[...], NT).astype(BF16)


def mlp(o, h0, aux, w_small, w_attn, w_up, w_down):
    count, width = h0.shape
    deep = w_up.shape[1]
    tile = min(256, count)
    row = lambda columns: pl.BlockSpec((tile, columns), lambda i: (i, 0))
    once = lambda shape: pl.BlockSpec(shape, lambda i: (0, 0), pipeline_mode=pl.Buffered(1))
    tall = lambda columns, dt: jax.ShapeDtypeStruct((count, columns), dt)
    return pl.pallas_call(
        functools.partial(mlp_kernel, width),
        grid=(count // tile,),
        in_specs=[
            row(width),
            row(width),
            row(128),
            pl.BlockSpec((width, 128), lambda i: (0, 1), pipeline_mode=pl.Buffered(1)),
            *[pl.BlockSpec(memory_space=pl.ANY)] * 3,
            once((width, 128)),
        ],
        out_specs=[
            row(width),
            row(width),
            row(width),
            row(width),
            row(deep),
            row(width),
            row(deep),
            once((width, 128)),
            once((8, width)),
            once((8, 128)),
        ],
        out_shape=[
            tall(width, BF16),
            tall(width, F32),
            tall(width, BF16),
            tall(width, BF16),
            tall(deep, BF16),
            tall(width, BF16),
            tall(deep, BF16),
            jax.ShapeDtypeStruct((width, 128), F32),
            jax.ShapeDtypeStruct((8, width), F32),
            jax.ShapeDtypeStruct((8, 128), F32),
        ],
        scratch_shapes=[
            pltpu.VMEM((tile, deep), F32),
            pltpu.VMEM((8, width), F32),
            *[pltpu.VMEM(v.shape, BF16) for v in (w_attn, w_up, w_down)],
            pltpu.SemaphoreType.DMA((3,)),
        ],
        compiler_params=pltpu.CompilerParams(vmem_limit_bytes=60 * 2**20),
    )(o, h0, aux, w_small, w_attn, w_up, w_down, w_small)


def back_kernel(
    tiles, chunks, h0_ref, dh1_ref, aux_ref, slots_ref, o_far, dat_far, normed_far, dq_far, dk_far,
    dv_far, wq_far, ws_ref, ghead_ref, sums_ref, squares_ref, loss_ref, count_ref, *refs,
):
    final, result, out, g = refs[:4], refs[4], refs[5:9], refs[9:13]
    tot, got, gains_all, vec, high, rest, send, recv, leave, enter = refs[13:23]
    near = refs[23:30]
    o_ref, dat_ref, normed_ref, dq_ref, dk_ref, dv_ref, wq_ref = near
    step = pl.program_id(0)
    R = reducers(chunks, g, out, refs[30:], send, recv)
    far = (o_far, dat_far, normed_far, dq_far, dk_far, dv_far, wq_far)
    bring = lambda i: pltpu.make_async_copy(far[i], near[i], enter.at[i])
    tile, width = h0_ref.shape
    place = lambda value: value.reshape(Z, X, 2, width // (2 * X * Z), value.shape[-1])

    def last(*group):
        for a in group:
            tot[0] += fold(a.stage4())

    def when(index, *stages):
        @pl.when(step == index)
        def _():
            for stage in stages:
                stage()

    def first():
        for i in range(len(far)):
            bring(i).start()
        greet(ALL)
        gains_all[...] = gains_of(ws_ref)
        vec[...] = sums_ref[...]
        tot[0] = squares_ref[...]
        tot[1] = loss_ref[...]
        tot[2] = count_ref[...]

    when(0, first)
    for j, d_ref in enumerate((dat_ref, dq_ref, dk_ref, dv_ref)):

        @pl.when(step == j)
        def _():
            for i in ((0, 1), (2, 3), (4,), (5,))[j]:
                bring(i).wait()
            if j:
                value = dot(normed_ref[...], d_ref[...], TN).astype(BF16)
                g[1][:, :, :, :, (j - 1) * width : j * width] = place(value)
            else:
                g[0][...] = place(dot(o_ref[...], d_ref[...], TN).astype(BF16))
            R[j].begin()
            if j:
                R[j - 1].stage1()

    when(4, R[3].stage1, bring(6).wait)
    when(6, R[0].stage2)
    when(8, R[1].stage2)

    @pl.when((step >= 4) & (step < 4 + tiles))
    def _():
        gains = gains_all[...]
        unit, rstd = norm_rows(h0_ref[...])
        rows = pl.ds(pl.multiple_of(jnp.clip(step - 4, 0, tiles - 1) * tile, tile), tile)
        dnormed = dot(dq_ref[rows, :], wq_ref[:, :width], NT)
        dnormed = dnormed + dot(dk_ref[rows, :], wq_ref[:, width : 2 * width], NT)
        dnormed = dnormed + dot(dv_ref[rows, :], wq_ref[:, 2 * width :], NT)
        add_rows(vec, 0, dnormed * unit)
        add_rows(vec, 1, dnormed)
        dh0 = dh1_ref[...] + norm_rows_back(dnormed, unit, rstd, gains[0:1])
        add_rows(vec, 6, dh0)
        top = dh0.astype(BF16)
        high[rows, :] = top
        rest[rows, :] = (dh0 - top.astype(F32)).astype(BF16)

    @pl.when(step == 4 + tiles)
    def _():
        slots = slots_ref[...]
        lookup = lookup_of(slots, g[2].shape[-1])
        top, low = high[...], rest[...]
        half = lookup.shape[1] // 2
        for j in range(2):
            cols = slice(j * half, (j + 1) * half)
            value = dot(top, lookup[:, cols], TN) + dot(low, lookup[:, cols], TN)
            g[2][:, :, :, :, cols] = place(value.astype(BF16))
            R[4 + j].begin()
        line = jnp.concatenate([vec[...], jnp.zeros((120, width), F32)], axis=0)
        both = dot(top, tokens_of(slots), TN) + line.T
        g[3][...] = place(jnp.concatenate([ghead_ref[...], both], axis=1))
        R[6].begin()
        for a in R[4:]:
            a.stage1()
        R[0].stage3()
        R[2].stage2()
        R[3].stage2()
        R[1].stage3()
        last(R[0], R[1])
        for a in R[4:]:
            a.stage2()
        R[2].stage3()
        R[3].stage3()
        R[0].stage5()
        R[1].stage5()
        for a in R[4:]:
            a.stage3()
        last(R[2], R[3])
        last(*R[4:])
        totals(tot, got, send, recv, PER * len(R))
        result[...] = tot[...]
        for a in R[2:]:
            a.stage5()
        for a in R:
            a.finish()
        copies = [pltpu.make_async_copy(out[i], final[i], leave.at[i]) for i in range(4)]
        for c in copies:
            c.start()
        for c in copies:
            c.wait()


def back(h0, dh1, aux, normed, o, dat, dqkv, w_qkv, w_small, ghead, sums, squares, loss, held, chunks):
    count, width = h0.shape
    length = count
    r = width // (2 * X * Z)
    tile = 256
    tiles = count // tile
    once = lambda shape: pl.BlockSpec(
        shape, lambda i: (0,) * len(shape), pipeline_mode=pl.Buffered(1)
    )
    row = lambda columns: pl.BlockSpec((tile, columns), lambda i: (jnp.clip(i - 4, 0, tiles - 1), 0))
    types = (BF16, BF16, BF16, F32)
    widths = (width, 3 * width, length, 256)
    ns = PER * len(chunks) + 12
    outs = [jax.ShapeDtypeStruct((2 * r, w), F32) for w in widths]
    totals_of = jax.ShapeDtypeStruct((3, 8, 128), F32)
    far = (o, dat, normed, *dqkv, w_qkv)
    return pl.pallas_call(
        functools.partial(back_kernel, tiles, chunks),
        grid=(5 + tiles,),
        in_specs=[
            row(width),
            row(width),
            row(128),
            once((count, 128)),
            *[pl.BlockSpec(memory_space=pl.ANY)] * len(far),
            pl.BlockSpec((width, 128), lambda i: (0, 1), pipeline_mode=pl.Buffered(1)),
            once((width, 128)),
            once((8, width)),
            *[once((8, 128))] * 3,
        ],
        out_specs=[pl.BlockSpec(memory_space=pl.ANY)] * 4 + [once((3, 8, 128))],
        out_shape=[*outs, totals_of],
        scratch_shapes=[pltpu.VMEM(o.shape, F32) for o in outs]
        + [pltpu.VMEM((Z, X, 2, r, w), t) for w, t in zip(widths, types)]
        + [
            pltpu.VMEM((3, 8, 128), F32),
            pltpu.VMEM((12, 3, 8, 128), F32),
            pltpu.VMEM((8, width), F32),
            pltpu.VMEM((8, width), F32),
            pltpu.VMEM((count, width), BF16),
            pltpu.VMEM((count, width), BF16),
            pltpu.SemaphoreType.DMA((ns,)),
            pltpu.SemaphoreType.DMA((ns,)),
            pltpu.SemaphoreType.DMA((4,)),
            pltpu.SemaphoreType.DMA((len(far),)),
            *[pltpu.VMEM(v.shape, v.dtype) for v in far],
        ]
        + [pltpu.VMEM(*b) for (t, lo, w, o) in chunks for b in shapes(r, w, o, types[t])],
        compiler_params=pltpu.CompilerParams(
            collective_id=2, has_side_effects=True, vmem_limit_bytes=60 * 2**20
        ),
    )(h0, dh1, aux, aux, *far, w_small, ghead, sums, squares, loss, held)


def adam_kernel(totals_ref, down, up, attn, wide, table, small_rows, small, *refs):
    sums = [jnp.sum(totals_ref[i], axis=(0, 1), keepdims=True) for i in range(3)]
    squares, total, valid = sums
    norm = jnp.sqrt(squares) / valid
    clip = jnp.minimum(1.0, CLIP_AT / (norm + 1e-06))
    scale = clip / valid
    state, outs, scalars = refs[:24], refs[24:48], refs[48]
    row = lax.broadcasted_iota(jnp.int32, scalars.shape, 0)
    scalars[...] = jnp.where(row == 0, total / math.log(2.0), jnp.where(row == 1, valid, norm))

    def update(index, grad):
        rate, decay = (RATE, DECAY) if index < 7 else (VEC_RATE, 0.0)
        weight, first, second = [state[index + 8 * i][...] for i in range(3)]
        for i, value in enumerate(adamw(weight, first, second, grad * scale, rate, decay)):
            outs[index + 8 * i][...] = value

    @pl.when(pl.program_id(0) == 0)
    def _():
        both = small[:, 128:].T
        update(0, both[PATCH : 2 * PATCH, :])
        update(7, both[:8, :])

    update(1, table[...])
    update(2, wide[...])
    update(3, attn[...])
    update(4, up[...])
    update(5, down[...])
    update(6, small_rows[:, : state[6].shape[1]])


def adam(totals, sums, masters, firsts, seconds):
    down, up, attn, wide, table, small = sums
    cuts = 4
    whole = lambda a: pl.BlockSpec(a.shape, lambda i: (0,) * a.ndim)
    by_row = lambda a: pl.BlockSpec((a.shape[0] // cuts, a.shape[1]), lambda i: (i, 0))
    turn = lambda values: [v.T if i % 8 in (1, 5) else v for i, v in enumerate(values)]
    state = turn((*masters, *firsts, *seconds))
    specs = [whole(a) if i % 8 in (0, 7) else by_row(a) for i, a in enumerate(state)]
    outs = pl.pallas_call(
        adam_kernel,
        grid=(cuts,),
        in_specs=[
            whole(totals),
            by_row(down),
            by_row(up),
            by_row(attn),
            by_row(wide),
            by_row(table),
            by_row(small),
            whole(small),
            *specs,
        ],
        out_specs=[*specs, pl.BlockSpec((8, 128), lambda i: (0, 0))],
        out_shape=[jax.ShapeDtypeStruct(a.shape, F32) for a in state]
        + [jax.ShapeDtypeStruct((8, 128), F32)],
        compiler_params=pltpu.CompilerParams(vmem_limit_bytes=60 * 2**20),
    )(totals, down, up, attn, wide, table, small, small, *state)
    scalars = outs[24]
    return (scalars[0, 0], scalars[1, 0], scalars[2, 0], *turn(outs[:24]))


def body(*args):
    patches, segments = args[:2]
    masters, firsts, seconds = (args[2:10], args[10:18], args[18:26])
    embed_in, pos_table, attn_qkv, attn_out, mlp_up, mlp_down, head_out, vectors = masters
    ways = lines()
    n_seq = lax.axis_size("seq")
    seq_at = lax.axis_index("seq")
    micros, group = segments.shape[0], segments.shape[2]
    length = group * n_seq
    width = attn_qkv.shape[1] // 3

    share = max(1, n_seq // micros)
    count = length // share
    mine = seq_at // share
    patches = patches.reshape(micros, PATCH, group)
    segments = segments.reshape(micros, group)
    low = lambda value: value.astype(BF16)
    outs = head_out.shape[1]
    pad = lambda value, columns: jnp.pad(value, ((0, 0), (0, columns - value.shape[1])))
    small = jnp.concatenate(
        [pad(head_out, 128), pad(vectors.T, PATCH), pad(embed_in.T, 128 - PATCH)], axis=1
    )
    early = [attn_qkv, pos_table.T, small]
    late = [mlp_up, mlp_down.T, attn_out]
    aligned = (lax.axis_size("dp"), n_seq, micros) == (X * Z, 4, 4) and width % (32 * X * Z) == 0
    start = (seq_at % share) * count
    part = lambda value: lax.dynamic_slice_in_dim(value, start, count, 0)
    pos_q = (start + jnp.arange(count))[None, :].astype(jnp.int32)
    if aligned:
        aux, seg_q, count_of, h0, normed, qkv, attended, lse, w_qkv, w_small, w_up, w_down, w_attn = front(
            patches, segments, early, late, EARLY, LATE
        )
        dattended, dh1, dat, mixed, hidden, ddown, dupper, grad_head, grad_sums, total = mlp(
            attended, h0, aux, w_small, w_attn, w_up, w_down
        )
        dq, dk, dv, squares, down, up = attend_back_deep(
            qkv, dattended, lse, seg_q, aux, mixed, ddown, hidden, dupper, DEEP
        )
        attn, wide, table, small, part = back(
            h0, dh1, aux, normed, attended, dat, (dq, dk, dv), w_qkv, w_small, grad_head, grad_sums,
            squares, total, count_of, REST,
        )
        sums = (down, up, attn, wide, table, small)
        return adam(part, sums, masters, firsts, seconds)

    row = lax.all_gather(patches, "seq", axis=2, tiled=True)
    seg = lax.all_gather(segments, "seq", axis=1, tiled=True)
    row = lax.dynamic_index_in_dim(row, mine, 0, keepdims=False)
    seg = lax.dynamic_index_in_dim(seg, mine, 0, keepdims=False)
    w_qkv, w_pos, w_small, w_up, w_down, w_attn = [
        gather_rows(low(v), ways, False) for v in early + late
    ]
    gains = w_small[:, 128:136].astype(F32).T

    at = jnp.arange(length)
    begins = jnp.zeros((length,), jnp.int32)
    for image in range(5):
        before = (seg > 0) & (seg < image) if image else seg > 0
        begins = jnp.where(seg == image, jnp.sum(before.astype(jnp.int32)), begins)
    offset = part(at - begins)
    own = part(seg)
    later = jnp.concatenate([row[:, 1:], jnp.zeros((PATCH, 1), BF16)], axis=1)
    seg_next = part(jnp.concatenate([seg[1:], jnp.zeros((1,), jnp.int32)]))
    pair = (own == seg_next) & (own > 0)
    first = (own > 0) & (offset == 0)
    more = jnp.stack([pair, first, offset, own], axis=1).astype(F32)
    aux = pad(jnp.concatenate([part(later.T).astype(F32), part(row.T).astype(F32), more], axis=1), 128)
    valid = jnp.sum((own > 0).astype(jnp.int32)).astype(F32) * PATCH
    seg_q, seg_k = own[None, :].astype(F32), seg[:, None].astype(F32)
    lookup, tokens = lookup_of(aux, length), tokens_of(aux)

    h0 = dot(lookup, w_pos, NT) + dot(tokens, w_small[:, 128:], NT) + (gains[6] - 1.0)
    normed, unit_one, rstd_one = layer_norm(h0, gains[0], gains[1] - 1.0)
    normed = low(normed)
    qkv = low(dot(normed, w_qkv))
    keys, values, offsets = (qkv, qkv, (HEADS // 2, HEADS))
    if share > 1:
        near = [list(range(g, g + share)) for g in range(0, n_seq, share)]
        keys = lax.all_gather(qkv[:, width:], "seq", axis=0, tiled=True, axis_index_groups=near)
        values, offsets = (keys, (0, HEADS // 2))
    attended, lse = attend(qkv, keys, values, offsets, seg_q, seg_k, pos_q, width)
    dattended, dh1, dat, mixed, hidden, ddown, dupper, grad_head, grad_sums, total = mlp(
        attended, h0, aux, w_small, w_attn, w_up, w_down
    )
    grad_down, grad_up = dot(ddown, hidden, TN), dot(mixed, dupper, TN)
    grad_attn = dot(attended, dat, TN)
    dq, dk, dv = attend_back(
        qkv, keys, values, offsets, dattended, lse, seg_q, seg_k, pos_q, width,
        BF16 if share == 1 else F32,
    )
    if share > 1:
        dk, dv = (
            low(lax.psum_scatter(d, "seq", scatter_dimension=0, tiled=True, axis_index_groups=near))
            for d in (dk, dv)
        )
    dqkv = jnp.concatenate([dq, dk, dv], axis=1)
    grad_qkv = dot(normed, dqkv, TN)
    dnorm, gain_one, shift_one = norm_back(dot(dqkv, w_qkv, NT), unit_one, rstd_one, gains[0])
    dh0 = dh1 + dnorm
    high = low(dh0)
    grad_pos = dot(high, lookup, TN) + dot(low(dh0 - high.astype(F32)), lookup, TN)
    grad_vec = jnp.concatenate(
        [gain_one[None], shift_one[None], grad_sums[2:6], jnp.sum(dh0, 0)[None], grad_sums[7:]]
    )
    small = jnp.concatenate([grad_head, dot(high, tokens, TN) + pad(grad_vec.T, 128)], axis=1)
    grads = [grad_down, grad_up, grad_attn, grad_qkv, grad_pos, small]
    parts = [
        scatter_rows(g.astype(F32), ways, order, F32 if g is small else BF16)
        for g, order in zip(grads, ("xy", "yx") * 3)
    ]
    squares = sum(jnp.sum(p * p) for p in parts)
    squares, total, valid = lax.psum((squares, jnp.sum(total), valid), ("dp", "seq"))
    down, up, attn, wide, table, small = [gather_parts(p, ways) for p in parts]
    pieces = [
        small[:, 128 + PATCH : 128 + 2 * PATCH].T,
        table.T,
        wide,
        attn,
        up,
        down.T,
        small[:, :outs],
        small[:, 128:136].T,
    ]
    norm = jnp.sqrt(squares) / valid
    clip = jnp.minimum(1.0, CLIP_AT / (norm + 1e-06))
    results = [
        adamw(
            masters[i],
            firsts[i],
            seconds[i],
            pieces[i] / valid * clip,
            RATE if i < 7 else VEC_RATE,
            DECAY if i < 7 else 0.0,
        )
        for i in range(8)
    ]
    return (
        total / math.log(2.0),
        valid,
        norm,
        *[r[0] for r in results],
        *[r[1] for r in results],
        *[r[2] for r in results],
    )


def solution(mesh):
    rows, columns = (P("dp", None), P(None, "dp"))
    weights = (columns, columns, rows, rows, rows, columns, rows, columns)
    in_specs = (P(None, "dp", None, "seq"), P(None, "dp", "seq")) + weights * 3
    out_specs = (P(), P(), P()) + weights * 3
    return jax.shard_map(body, mesh=mesh, in_specs=in_specs, out_specs=out_specs, check_vma=False)
```

```python
import functools
import math

import jax
import jax.numpy as jnp
from jax import lax
from jax.experimental import pallas as pl
from jax.experimental.pallas import tpu as pltpu
from jax.sharding import PartitionSpec as P

HEADS = 12
PATCH = 48
STEP = 10
RATE = 0.02
VEC_RATE = 0.15
BETA_ONE = 0.9
BETA_TWO = 0.95
ADAM_EPS = 1e-08
DECAY = 0.1
CLIP_AT = 0.01
NORM_EPS = 1e-05

F32 = jnp.float32
BF16 = jnp.bfloat16
WIRE = jnp.bfloat16
EARLY = [
    (0, 0, 1280, True),
    (0, 1280, 1024, True),
    (1, 0, 1024, False),
    (2, 0, 256, False),
]
LATE = [
    (0, 0, 1536, True),
    (0, 1536, 1536, True),
    (1, 0, 1536, True),
    (2, 0, 768, True),
    (1, 1536, 1536, False),
]
DEEP = [
    (0, 0, 768, "xy"),
    (1, 0, 768, "yx"),
    (0, 768, 768, "xy"),
    (1, 768, 768, "yx"),
    (0, 1536, 768, "xy"),
    (1, 1536, 768, "yx"),
    (0, 2304, 768, "xy"),
    (1, 2304, 768, "yx"),
]
REST = [
    (0, 0, 768, "yx"),
    (1, 0, 768, "xy"),
    (1, 768, 768, "xy"),
    (1, 1536, 768, "yx"),
    (2, 0, 512, "yx"),
    (2, 512, 512, "xy"),
    (3, 0, 256, "xy"),
]
NN = (((1,), (0,)), ((), ()))
NT = (((1,), (1,)), ((), ()))
TN = (((0,), (0,)), ((), ()))


PAIR, FIRST, OFFSET, SLOT_ID = range(2 * PATCH, 2 * PATCH + 4)


def dot(left, right, dims=NN):
    return lax.dot_general(left, right, dims, preferred_element_type=F32)


def lookup_of(aux, length):
    slot = lax.broadcasted_iota(jnp.int32, (aux.shape[0], length), 1).astype(F32)
    return (slot == aux[:, OFFSET : OFFSET + 1]).astype(F32).astype(BF16)


def tokens_of(aux):
    lane = lax.broadcasted_iota(jnp.int32, aux.shape, 1)
    return jnp.where((lane >= PATCH) & (lane < 2 * PATCH), aux, 0.0).astype(BF16)


def gains_of(small):
    return small[...].astype(F32).T[:8]


def line(axis, size, count, stride):
    place = (lax.axis_index(axis) // stride) % count
    swaps = [
        (axis, [(source, source ^ (step * stride)) for source in range(size)])
        for step in range(1, count)
    ]
    return (count, place, swaps)


def lines():
    n_dp, n_seq = lax.axis_size("dp"), lax.axis_size("seq")
    n_x = 1 << ((n_dp.bit_length() - 1) // 2)
    return {
        "z": line("dp", n_dp, n_dp // n_x, n_x),
        "x": line("dp", n_dp, n_x, 1),
        "y": line("seq", n_seq, n_seq // 2, 2),
        "core": line("seq", n_seq, 2, 1),
    }


def gather_line(block, along):
    count, place, swaps = along
    others = [lax.ppermute(block, axis, swap) for axis, swap in swaps]
    if count == 2:
        first = place == 0
        return jnp.stack([jnp.where(first, block, others[0]), jnp.where(first, others[0], block)])
    whole = jnp.zeros((count,) + block.shape, block.dtype)
    for step, piece in enumerate([block] + others):
        whole = lax.dynamic_update_index_in_dim(whole, piece, place ^ step, 0)
    return whole


def scatter_line(blocks, along, dim, wire):
    count, place, swaps = along
    pick = lambda index: lax.dynamic_index_in_dim(blocks, index, dim, keepdims=False)
    arrived = [
        lax.ppermute(pick(place ^ (step + 1)).astype(wire), axis, swap)
        for step, (axis, swap) in enumerate(swaps)
    ]
    total = pick(place)
    for piece in arrived:
        total = total + piece.astype(F32)
    return total


def gather_rows(shard, ways, split_y):
    n_core, core, _ = ways["core"]
    n_y, y_at, _ = ways["y"]
    rows, columns = shard.shape
    if split_y:
        part = lax.dynamic_slice_in_dim(
            shard, (core * n_y + y_at) * (rows // (2 * n_y)), rows // (2 * n_y), 0
        )
    else:
        part = lax.dynamic_slice_in_dim(shard, core * (rows // 2), rows // 2, 0)
    part = gather_line(part, ways["z"])
    part = gather_line(part, ways["x"])
    if split_y:
        part = gather_line(part, ways["y"])
        part = gather_line(part, ways["core"])
        part = jnp.transpose(part, (3, 2, 0, 1, 4, 5))
    else:
        part = gather_line(part, ways["core"])
        part = jnp.transpose(part, (2, 1, 0, 3, 4))
    return part.reshape(-1, columns)


def scatter_rows(grad, ways, order, wire):
    n_z, n_x, n_y = ways["z"][0], ways["x"][0], ways["y"][0]
    columns = grad.shape[1]
    blocks = grad.reshape(n_z, n_x, 2, n_y, -1, columns)
    blocks = scatter_line(blocks, ways["core"], 2, wire)
    if order == "xy":
        blocks = scatter_line(blocks, ways["x"], 1, wire)
        blocks = scatter_line(blocks, ways["y"], 1, wire)
    else:
        blocks = scatter_line(blocks, ways["y"], 2, wire)
        blocks = scatter_line(blocks, ways["x"], 1, wire)
    return scatter_line(blocks, ways["z"], 0, wire)


def gather_parts(part, ways):
    part = gather_line(part, ways["y"])
    part = gather_line(part, ways["core"])
    return part.reshape(-1, part.shape[-1])


MESH=pl.DeviceIdType.MESH
X = 2
Z = 4
def here():
    d=lax.axis_index("dp"); s=lax.axis_index("seq")
    return d//X, d%X, s//2, s%2
def peer(kz,kx,ky,kc):
    z,x,y,c=here()
    return ((z^kz)*X+(x^kx), (y^ky)*2+(c^kc))
class Gather:
    def __init__(s, src, dst, sems, base, split, lo, width):
        s.src,s.dst,s.split,s.lo,s.width=src,dst,split,lo,width
        s.send,s.recv=sems; s.n=base
        s.live=[]; s.rows=src.shape[0]
        s.idx={}
    def region(s,ref,kz,kx,half,ky,local=False):
        z,x,y,c=here(); r=s.rows//2
        row=(c^half)*r
        if not local: row=row+((z^kz)*X+(x^kx))*s.rows
        row=pl.multiple_of(row,16)
        if ky is None: return ref.at[pl.ds(row,r),pl.ds(s.lo,s.width)]
        w=s.width//2
        return ref.at[pl.ds(row,r),pl.ds(pl.multiple_of(s.lo+(y^ky)*w,128),w)]
    def copy(s,key,kz,kx,ky,to,own=False):
        i=s.idx.setdefault(key,s.n)
        if i==s.n: s.n+=1
        col=ky if s.split else None
        return pltpu.make_async_remote_copy(s.region(s.src if own else s.dst,kz,kx,0,col,own),s.region(s.dst,kz,kx,0,col),s.send.at[i],s.recv.at[i],device_id=peer(*to),device_id_type=MESH)
    def start(s,*a,**k):
        s.copy(*a,**k).start(); s.live.append((a,k))
    def begin(s):
        for k in (1,2,3): s.start(("z",k),0,0,0,(k,0,0,0),own=True)
        s.start(("x",0),0,0,0,(0,1,0,0),own=True)
    def after_z(s,k):
        s.recvd(("z",k),k,0,0)
        s.start(("x",k),k,0,0,(0,1,0,0))
        if s.split: s.start(("y",k,0),k,0,0,(0,0,1,0))
        s.start(("c",k,0),k,0,0,(0,0,0,1))
    def after_x(s,k):
        s.recvd(("x",k),k,1,0)
        if s.split: s.start(("y",k,1),k,1,0,(0,0,1,0))
        s.start(("c",k,1),k,1,0,(0,0,0,1))
    def after_y(s,k,kx):
        s.recvd(("y",k,kx),k,kx,1)
        s.start(("d",k,kx),k,kx,1,(0,0,0,1))
    def recvd(s,key,kz,kx,ky):
        s.copy(key,kz,kx,ky,(0,0,0,1)).wait_recv()
    def stage_z(s):
        for k in (1,2,3): s.after_z(k)
    def stage_x(s):
        for k in range(4): s.after_x(k)
    def stage_y(s):
        if s.split:
            for kx in range(2):
                for k in range(4):
                    if k or kx: s.after_y(k,kx)
    def finish(s):
        for k in range(4):
            for kx in range(2):
                if (k or kx):
                    s.core_recv(("c",k,kx),k,kx,0)
                    if s.split: s.core_recv(("d",k,kx),k,kx,1)
        for a,k in s.live: s.copy(*a,**k).wait_send()
    def core_recv(s,key,kz,kx,ky):
        i=s.idx[key]; col=ky if s.split else None
        r=s.region(s.dst,kz,kx,1,col)
        pltpu.make_async_remote_copy(r,r,s.send.at[i],s.recv.at[i],device_id=peer(0,0,0,1),device_id_type=MESH).wait_recv()

def greet(peers):
    bar=pltpu.get_barrier_semaphore()
    for p in peers: pl.semaphore_signal(bar,inc=1,device_id=peer(*p),device_id_type=MESH)
    pl.semaphore_wait(bar,len(peers))
PEERS=[(1,0,0,0),(2,0,0,0),(3,0,0,0),(0,1,0,0),(0,0,1,0),(0,0,0,1)]
class Own:
    def __init__(s,*refs): s.refs=refs
    def copy(s):
        src,dst,sem=s.refs
        z,x,y,c=here(); r=src.shape[0]
        return pltpu.make_async_copy(src,dst.at[pl.ds(pl.multiple_of((z*X+x)*r,16),r),:],sem)
    def start(s): s.copy().start()
    def wait(s): s.copy().wait()
def open_chunks(chunks,src,dst,send,recv,loc):
    mine=[Own(src[i],dst[i],loc.at[i]) for i in range(len(src))]
    g=[]; base=0
    for (t,lo,w,sp) in chunks:
        g.append(Gather(src[t],dst[t],(send,recv),base,sp,lo,w)); base+=28 if sp else 14
    return mine,g
def about_slots(row,seg):
    ids=seg[...]; length=ids.shape[1]
    slot=lax.broadcasted_iota(jnp.int32,ids.shape,1)
    begins=jnp.zeros_like(ids)
    for image in range(5):
        before=(ids>0)&(ids<image) if image else ids>0
        begins=jnp.where(ids==image,jnp.sum(before.astype(F32),axis=1,keepdims=True).astype(jnp.int32),begins)
    offset=slot-begins
    after=jnp.where(slot==length-1,0,pltpu.roll(ids,length-1,1))
    pair=((ids==after)&(ids>0)).astype(F32)
    first=((ids>0)&(offset==0)).astype(F32)
    x=row[...].astype(F32)
    later=jnp.where(lax.broadcasted_iota(jnp.int32,x.shape,1)==length-1,0.0,pltpu.roll(x,length-1,1))
    line=lax.broadcasted_iota(jnp.int32,(128-2*PATCH,length),0)
    more=jnp.zeros(line.shape,F32)
    for i,v in enumerate((pair,first,offset.astype(F32),ids.astype(F32))): more=jnp.where(line==i,v,more)
    return jnp.concatenate([later,x,more],axis=0).T
def semaphores(chunks,n):
    tot=sum(28 if s[3] else 14 for s in chunks)
    return [pltpu.SemaphoreType.DMA((tot,)),pltpu.SemaphoreType.DMA((tot,)),pltpu.SemaphoreType.DMA((n,))]
PER=8
class Reduce:
    def __init__(s,g,out,bufs,sems,base,lo,w,order):
        s.g,s.out,s.lo,s.w,s.order=g,out,lo,w,order
        s.r1,s.p2,s.r2,s.p3,s.r3,s.p4,s.r4=bufs
        s.send,s.recv=sems; s.base=base; s.r=g.shape[3]
    def col(s,ky,lo=0):
        z,x,y,c=here(); h=s.w//2
        return pl.ds(pl.multiple_of(lo+(y^ky)*h,128),h)
    def remote(s,src,dst,i,to):
        return pltpu.make_async_remote_copy(src,dst,s.send.at[s.base+i],s.recv.at[s.base+i],device_id=peer(*to),device_id_type=MESH)
    def c1(s):
        z,x,y,c=here()
        return s.remote(s.g.at[:,:,1-c,:,pl.ds(s.lo,s.w)],s.r1,0,(0,0,0,1))
    def begin(s): s.c1().start()
    def two(s,zz,xx,ky=None):
        z,x,y,c=here()
        cols=slice(None) if ky is None else s.col(ky)
        own=s.g[zz,xx,c,:,pl.ds(s.lo,s.w) if ky is None else s.col(ky,s.lo)]
        return own.astype(F32)+s.r1[zz,xx,:,cols].astype(F32)
    def three(s,zz,xx,ky):
        if s.order=="xy": return s.two(zz,xx,ky)+s.r2[zz,:,s.col(ky)].astype(F32)
        return s.two(zz,xx,ky)+s.r2[zz,xx].astype(F32)
    def four(s,zz):
        z,x,y,c=here()
        return s.three(zz,x,0)+s.r3[zz].astype(F32)
    def c2(s): return s.remote(s.p2,s.r2,1,(0,1,0,0) if s.order=="xy" else (0,0,1,0))
    def c3(s): return s.remote(s.p3,s.r3,2,(0,0,1,0) if s.order=="xy" else (0,1,0,0))
    def c4(s,k): return s.remote(s.p4.at[k-1],s.r4.at[k-1],2+k,(k,0,0,0))
    def c5(s):
        z,x,y,c=here()
        ref=s.out.at[pl.ds(pl.multiple_of(c*s.r,8),s.r),s.col(0,s.lo)]
        return s.remote(ref,ref,6,(0,0,1,0))
    def c6(s):
        z,x,y,c=here()
        ref=s.out.at[pl.ds(pl.multiple_of(c*s.r,8),s.r),pl.ds(s.lo,s.w)]
        return s.remote(ref,ref,7,(0,0,0,1))
    def stage1(s):
        z,x,y,c=here()
        s.c1().wait_recv()
        @pl.loop(0,Z)
        def _(zz):
            if s.order=="xy":
                s.p2[zz]=s.two(zz,1-x).astype(s.p2.dtype)
            else:
                for xx in range(X): s.p2[zz,xx]=s.two(zz,xx,1).astype(s.p2.dtype)
        s.c2().start()
    def stage2(s):
        z,x,y,c=here()
        s.c2().wait_recv()
        @pl.loop(0,Z)
        def _(zz):
            s.p3[zz]=(s.three(zz,x,1) if s.order=="xy" else s.three(zz,1-x,0)).astype(s.p3.dtype)
        s.c3().start()
    def stage3(s):
        z,x,y,c=here()
        s.c3().wait_recv()
        for k in (1,2,3):
            s.p4[k-1]=s.four(z^k).astype(s.p4.dtype)
            s.c4(k).start()
    def stage4(s):
        z,x,y,c=here()
        total=s.four(z)
        for k in (1,2,3):
            s.c4(k).wait_recv()
            total=total+s.r4[k-1].astype(F32)
        s.out[pl.ds(pl.multiple_of(c*s.r,8),s.r),s.col(0,s.lo)]=total
        s.c5().start()
        return total
    def stage5(s):
        s.c5().wait_recv()
        s.c6().start()
    def finish(s):
        s.c6().wait_recv()
        s.c1().wait_send(); s.c2().wait_send(); s.c3().wait_send()
        for k in (1,2,3): s.c4(k).wait_send()
        s.c5().wait_send(); s.c6().wait_send()

def shapes(r,w,order,dt):
    h=w//2
    two=(Z,r,w) if order=="xy" else (Z,X,r,h)
    return [((Z,X,r,w),dt)]+[(two,dt)]*2+[((Z,r,h),dt)]*2+[((3,r,h),dt)]*2
def reducers(chunks,g,out,bufs,send,recv):
    return [Reduce(g[t],out[t],bufs[7*i:7*i+7],(send,recv),PER*i,lo,w,o) for i,(t,lo,w,o) in enumerate(chunks)]

def totals(part,got,send,recv,base,between):
    d=lax.axis_index("dp"); q=lax.axis_index("seq")
    def hop(first,count,mine,peers):
        got[first+mine]=part[...]
        cs=[pltpu.make_async_remote_copy(part,got.at[first+mine],send.at[base+first+i],recv.at[base+first+i],device_id=p,device_id_type=MESH) for i,p in enumerate(peers)]
        for k in cs: k.start()
        for k in cs: k.wait()
        t=got[first]
        for i in range(1,count): t=t+got[first+i]
        part[...]=t
    hop(0,4,q,[peer(0,0,ky,kc) for ky,kc in ((0,1),(1,0),(1,1))])
    between()
    hop(4,8,d,[peer(kz,kx,0,0) for kz,kx in ((0,1),(1,0),(1,1),(2,0),(2,1),(3,0),(3,1))])

ALL=[(0,0,ky,kc) for ky,kc in ((0,1),(1,0),(1,1))]+[(kz,kx,0,0) for kz,kx in ((0,1),(1,0),(1,1),(2,0),(2,1),(3,0),(3,1))]
def fold(v):
    v=v*v
    t=jnp.zeros((8,128),F32)
    for i in range(v.shape[0]//8):
        for j in range(v.shape[1]//128):
            t=t+v[8*i:8*i+8,128*j:128*j+128]
    return t


def hide(bias, tile, skip, sq_ref, sk, qp_ref):
    for step in range(bias.shape[1] // tile):
        rows = slice(step * tile, (step + 1) * tile)
        keys = (step + 1) * tile if skip else bias.shape[0]
        pos_key = lax.broadcasted_iota(jnp.int32, (keys, tile), 0)
        if qp_ref is None:
            pos = lax.broadcasted_iota(jnp.int32, (1, tile), 1) + step * tile
        else:
            pos = qp_ref[:, rows]
        allowed = (sk[:keys, :] == sq_ref[:, rows]) & (pos_key <= pos)
        bias[:keys, rows] = jnp.where(allowed, 0.0, -1e30)


def head_forward(tile, skip, hd, scale, q_ref, k_ref, v_ref, bias, o_ref, lse_ref):
    length = k_ref.shape[0]
    for head in range(q_ref.shape[1] // hd):
        cols = slice(hd * head, hd * head + hd)
        for step in range(q_ref.shape[0] // tile):
            rows = slice(step * tile, (step + 1) * tile)
            keys = (step + 1) * tile if skip else length
            query = (q_ref[rows, cols].astype(F32) * scale).astype(BF16)
            scores = dot(k_ref[:keys, cols], query, NT) + bias[:keys, rows]
            top = jnp.max(scores, 0, keepdims=True)
            weight = jnp.exp(scores - top)
            total = jnp.sum(weight, 0, keepdims=True)
            probs = (weight * (1.0 / total)).astype(BF16)
            o_ref[rows, cols] = dot(probs, v_ref[:keys, cols], TN).astype(BF16)
            lse_ref[0, head : head + 1, rows] = top + jnp.log(total)


def attend_kernel(tile, skip, hd, scale, q_ref, k_ref, v_ref, sq_ref, sk_ref, qp_ref, o_ref, lse_ref, bias):
    @pl.when(pl.program_id(0) == 0)
    def _():
        hide(bias, tile, skip, sq_ref, sk_ref, qp_ref)

    head_forward(tile, skip, hd, scale, q_ref, k_ref, v_ref, bias, o_ref, lse_ref)


def front_kernel(tiles, lanes, shape, early, late, pieces, ids, *refs):
    wide, src = refs[:6], refs[-6:]
    aux, sq_ref, count, h0_ref, normed_ref, qkv_ref, o_ref, lse_ref = refs[6:14]
    wq_out, ws_out, *dst = refs[14:19]
    wq, wp, ws, qkv, bias, gains_all, row, seg = refs[19:27]
    send, recv, loc, late_send, late_recv, late_loc, psend, precv, leave = refs[27:-6]
    step = pl.program_id(0)
    mine, e = open_chunks(early, src[:3], (wq, wp, ws), send, recv, loc)
    mine_late, g = open_chunks(late, src[3:], dst, late_send, late_recv, late_loc)
    group = pieces.shape[2]

    def when(index, *stages):
        @pl.when(step == index)
        def _():
            for stage in stages:
                stage()

    def out(i):
        pair = ((wq, wq_out), (ws, ws_out))[i]
        return pltpu.make_async_copy(*pair, leave.at[i])

    def begin():
        greet(PEERS + [(0, 0, 1, 1)])
        q = lax.axis_index("seq")
        at = pl.ds(pl.multiple_of(q * group, 128), group)
        swaps = []
        for k, to in ((1, (0, 0, 0, 1)), (2, (0, 0, 1, 0)), (3, (0, 0, 1, 1))):
            for j, (a, b) in enumerate(
                ((pieces.at[q ^ k], row.at[:, at]), (ids.at[q ^ k], seg.at[:, at]))
            ):
                i = 2 * (k - 1) + j
                swaps.append(
                    pltpu.make_async_remote_copy(
                        a, b, psend.at[i], precv.at[i], device_id=peer(*to), device_id_type=MESH
                    )
                )
                swaps[-1].start()

        def narrow(*which):
            for i in which:
                src[i][...] = wide[i][...].astype(BF16)

        narrow(0)
        e[0].begin()
        e[1].begin()
        narrow(1, 2)
        for a in mine:
            a.start()
        narrow(3, 4, 5)
        for a in mine_late:
            a.start()
        row[:, at] = pieces[q]
        seg[:, at] = ids[q]
        for a in swaps:
            a.wait()
        aux[...] = about_slots(row, seg)
        sq_ref[...] = seg[...].astype(F32)
        down, across = [lax.broadcasted_iota(jnp.int32, count.shape, i) for i in range(2)]
        held = jnp.sum((seg[...] > 0).astype(F32), axis=1, keepdims=True)
        count[...] = jnp.where((down == 0) & (across == 0), held * PATCH, 0.0)
        e[0].stage_z()
        e[2].begin()
        e[3].begin()
        e[1].stage_z()
        g[0].begin()
        e[0].stage_x()
        e[2].stage_z()
        e[3].stage_z()
        g[1].begin()
        e[1].stage_x()
        e[0].stage_y()
        e[2].stage_x()
        e[3].stage_x()
        e[1].stage_y()
        for a in e:
            a.finish()
        for a in mine:
            a.wait()
        out(0).start()
        out(1).start()
        gains_all[...] = gains_of(ws.at[:, 128:])
        g[0].stage_z()
        g[2].begin()

    when(0, begin)
    when(2, g[1].stage_z, g[3].begin, g[0].stage_x)
    when(4, g[2].stage_z, g[4].begin, g[1].stage_x)
    when(5, g[0].stage_y, g[3].stage_z)
    when(6, g[2].stage_x)
    when(7, g[1].stage_y, g[3].stage_x)
    when(8, g[4].stage_z)
    when(9, g[2].stage_y)

    @pl.when(step < tiles)
    def _():
        tile, length = h0_ref.shape[0], wp.shape[1]
        rows = pl.ds(pl.multiple_of(jnp.minimum(step, tiles - 1) * tile, tile), tile)
        slots = aux[rows, :]
        gains = gains_all[...]
        h0 = dot(lookup_of(slots, length), wp[...], NT) + dot(tokens_of(slots), ws[:, 128:], NT)
        h0 = h0 + (gains[6:7] - 1.0)
        h0_ref[...] = h0
        unit, _ = norm_rows(h0)
        normed = (unit * gains[0:1] + (gains[1:2] - 1.0)).astype(BF16)
        normed_ref[...] = normed
        value = dot(normed, wq[...]).astype(BF16)
        qkv_ref[...] = value
        qkv[rows, :] = value

    @pl.when(step >= tiles)
    def _():
        pair = step - tiles
        width = qkv.shape[1] // 3

        @pl.when(pair == 0)
        def _():
            hide(bias, *shape[:2], sq_ref, aux[:, SLOT_ID : SLOT_ID + 1], None)

        part = lambda i: qkv.at[:, pl.ds(pl.multiple_of(i * width + pair * lanes, lanes), lanes)]
        head_forward(*shape, part(0), part(1), part(2), bias, o_ref, lse_ref)

    def drain():
        g[4].stage_x()
        g[3].stage_y()
        g[4].stage_y()
        for a in g:
            a.finish()
        for a in mine_late:
            a.wait()
        out(0).wait()
        out(1).wait()

    when(pl.num_programs(0) - 1, drain)


def front(pieces, ids, early_shards, late_shards, early, late):
    count, dp = pieces.shape[2] * lax.axis_size("seq"), lax.axis_size("dp")
    shards = [*early_shards, *late_shards]
    full = [jax.ShapeDtypeStruct((v.shape[0] * dp, v.shape[1]), BF16) for v in shards]
    width = full[0].shape[0]
    hd = width // HEADS
    lanes, pairs, tile = 2 * hd, HEADS // 2, 256
    tiles = count // tile
    once = lambda shape: pl.BlockSpec(
        shape, lambda i: (0,) * len(shape), pipeline_mode=pl.Buffered(1)
    )
    row = lambda columns: pl.BlockSpec((tile, columns), lambda i: (jnp.minimum(i, tiles - 1), 0))
    after = lambda i: jnp.maximum(i - tiles, 0)
    anywhere = pl.BlockSpec(memory_space=pl.ANY)
    ids = ids[:, None, :]
    landing = [pltpu.VMEM(v.shape, v.dtype) for v in full[:3]]
    return pl.pallas_call(
        functools.partial(front_kernel, tiles, lanes, (tile, True, hd, hd**-0.5), early, late),
        grid=(tiles + pairs,),
        in_specs=[once(pieces.shape), once(ids.shape)]
        + [once(v.shape) for v in shards],
        out_specs=[
            once((count, 128)),
            once((1, count)),
            once((8, 128)),
            row(width),
            row(width),
            row(3 * width),
            pl.BlockSpec((count, lanes), lambda i: (0, after(i))),
            pl.BlockSpec((1, 2, count), lambda i: (after(i), 0, 0)),
        ]
        + [anywhere] * 5,
        out_shape=[
            jax.ShapeDtypeStruct((count, 128), F32),
            jax.ShapeDtypeStruct((1, count), F32),
            jax.ShapeDtypeStruct((8, 128), F32),
            jax.ShapeDtypeStruct((count, width), F32),
            jax.ShapeDtypeStruct((count, width), BF16),
            jax.ShapeDtypeStruct((count, 3 * width), BF16),
            jax.ShapeDtypeStruct((count, width), BF16),
            jax.ShapeDtypeStruct((pairs, 2, count), F32),
            full[0],
            full[2],
            *full[3:],
        ],
        scratch_shapes=landing
        + [
            pltpu.VMEM((count, 3 * width), BF16),
            pltpu.VMEM((count, count), F32),
            pltpu.VMEM((8, width), F32),
            pltpu.VMEM((pieces.shape[1], count), pieces.dtype),
            pltpu.VMEM((1, count), ids.dtype),
        ]
        + semaphores(early, 3)
        + semaphores(late, 3)
        + [pltpu.SemaphoreType.DMA((6,)), pltpu.SemaphoreType.DMA((6,)), pltpu.SemaphoreType.DMA((2,))]
        + [pltpu.VMEM(v.shape, BF16) for v in shards],
        compiler_params=pltpu.CompilerParams(
            collective_id=4, has_side_effects=True, vmem_limit_bytes=60 * 2**20
        ),
    )(pieces, ids, *shards)


def head_back(
    tile, skip, hd, scale, q_ref, k_ref, v_ref, do_ref, lse_ref, bias, dq_ref, dk_ref, dv_ref,
    dk_sum, dv_sum, before=lambda head: None,
):
    length = k_ref.shape[0]
    dk_sum[...] = jnp.zeros_like(dk_sum)
    dv_sum[...] = jnp.zeros_like(dv_sum)
    for head in range(q_ref.shape[1] // hd):
        cols = slice(hd * head, hd * head + hd)
        before(head)
        for step in range(q_ref.shape[0] // tile):
            rows = slice(step * tile, (step + 1) * tile)
            keys = (step + 1) * tile if skip else length
            query = (q_ref[rows, cols].astype(F32) * scale).astype(BF16)
            key = k_ref[:keys, cols]
            dout = do_ref[rows, cols]
            scores = dot(key, query, NT) + bias[:keys, rows]
            probs = jnp.exp(scores - lse_ref[0, head : head + 1, rows])
            dprobs = dot(v_ref[:keys, cols], dout, NT)
            delta = jnp.sum(dprobs * probs, 0, keepdims=True)
            dscores = (probs * (dprobs - delta)).astype(BF16)
            dv_sum[:keys, cols] += dot(probs.astype(BF16), dout)
            dk_sum[:keys, cols] += dot(dscores, query)
            dq_ref[rows, cols] = (dot(dscores, key, TN) * scale).astype(dq_ref.dtype)
    dk_ref[...] = dk_sum[...].astype(dk_ref.dtype)
    dv_ref[...] = dv_sum[...].astype(dv_ref.dtype)


def attend_back_kernel(
    tile, skip, hd, scale, q_ref, k_ref, v_ref, do_ref, lse_ref, sq_ref, sk_ref, qp_ref,
    dq_ref, dk_ref, dv_ref, dk_sum, dv_sum, bias,
):
    @pl.when(pl.program_id(0) == 0)
    def _():
        hide(bias, tile, skip, sq_ref, sk_ref, qp_ref)

    head_back(
        tile, skip, hd, scale, q_ref, k_ref, v_ref, do_ref, lse_ref, bias, dq_ref, dk_ref, dv_ref,
        dk_sum, dv_sum,
    )


def attend_back_deep_kernel(
    parts, shape, chunks, m_ref, dd_ref, hid_ref, du_ref, q_ref, k_ref, v_ref, do_ref, lse_ref,
    sq_ref, aux_ref, dq_ref, dk_ref, dv_ref, squares, down_ref, up_ref, dk_sum, dv_sum, bias,
    g_down, g_up, down, up, send, recv, leave, *bufs,
):
    step = pl.program_id(0)
    width, wide = m_ref.shape[1], hid_ref.shape[1]
    R = reducers(chunks, (g_down, g_up), (down, up), bufs, send, recv)
    pairs = [R[2 * j : 2 * j + 2] for j in range(parts)]
    every = lambda name, j: lambda: [getattr(a, name)() for a in pairs[j]]

    def last(j):
        def run():
            for a in pairs[j]:
                squares[...] += fold(a.stage4())

        return run

    def when(index, *stages):
        @pl.when(step == index)
        def _():
            for stage in stages:
                stage()

    def first():
        greet(PEERS)
        squares[...] = jnp.zeros_like(squares)

    when(0, first)
    place = lambda value: value.astype(BF16).reshape(Z, X, 2, width // (2 * X * Z), wide)
    for j in range(parts):

        @pl.when(step == j)
        def _():
            cols = slice(j * wide, (j + 1) * wide)
            g_down[:, :, :, :, cols] = place(dot(dd_ref[...], hid_ref[...], TN))
            pairs[j][0].begin()
            g_up[:, :, :, :, cols] = place(dot(m_ref[...], du_ref[...], TN))
            pairs[j][1].begin()
            if j == 1:
                every("stage1", 0)()
            if j == 3:
                every("stage1", 1)()

    when(parts, lambda: hide(bias, *shape[:2], sq_ref, aux_ref[:, SLOT_ID : SLOT_ID + 1], None))
    moves = {
        1: [every("stage2", 0)],
        2: [every("stage1", 2)],
        4: [every("stage2", 1), every("stage3", 0)],
        5: [every("stage1", 3)],
        7: [every("stage2", 2), every("stage3", 1), last(0)],
        9: [every("stage2", 3)],
        10: [every("stage3", 2), last(1), every("stage5", 0)],
        11: [every("stage3", 3)],
    }

    def before(head):
        for half, stages in moves.items():
            if half % 2 == head:
                when(parts + half // 2, *stages)

    @pl.when(step >= parts)
    def _():
        head_back(
            *shape, q_ref, k_ref, v_ref, do_ref, lse_ref, bias, dq_ref, dk_ref, dv_ref, dk_sum,
            dv_sum, before,
        )

    def drain():
        last(2)()
        every("stage5", 1)()
        last(3)()
        every("stage5", 2)()
        every("stage5", 3)()
        for a in R:
            a.finish()
        copies = [
            pltpu.make_async_copy(down, down_ref, leave.at[0]),
            pltpu.make_async_copy(up, up_ref, leave.at[1]),
        ]
        for c in copies:
            c.start()
        for c in copies:
            c.wait()

    when(9, drain)


def blocks_of(rows, width, offset):
    return pl.BlockSpec((rows, width), lambda pair: (0, pair + offset))


def fixed(shape):
    return pl.BlockSpec(shape, lambda pair: (0, 0))


def kernel_params():
    return pltpu.CompilerParams(vmem_limit_bytes=48 * 2**20)


def attend(qkv, keys, values, offsets, seg_q, seg_k, pos_q, width):
    count, length = qkv.shape[0], keys.shape[0]
    hd = width // HEADS
    lanes = 2 * hd
    pairs = HEADS // 2
    return pl.pallas_call(
        functools.partial(attend_kernel, min(256, count), count == length, hd, hd**-0.5),
        grid=(pairs,),
        in_specs=[
            blocks_of(count, lanes, 0),
            blocks_of(length, lanes, offsets[0]),
            blocks_of(length, lanes, offsets[1]),
            fixed((1, count)),
            fixed((length, 1)),
            fixed((1, count)),
        ],
        out_specs=[blocks_of(count, lanes, 0), pl.BlockSpec((1, 2, count), lambda pair: (pair, 0, 0))],
        out_shape=[
            jax.ShapeDtypeStruct((count, width), BF16),
            jax.ShapeDtypeStruct((pairs, 2, count), F32),
        ],
        scratch_shapes=[pltpu.VMEM((length, count), F32)],
        cost_estimate=pl.CostEstimate(
            flops=25_000_000_000, bytes_accessed=8_000_000, transcendentals=8_000_000
        ),
        compiler_params=kernel_params(),
    )(qkv, keys, values, seg_q, seg_k, pos_q)


def attend_back(qkv, keys, values, offsets, dout, lse, seg_q, seg_k, pos_q, width, kv_type):
    count, length = qkv.shape[0], keys.shape[0]
    hd = width // HEADS
    lanes = 2 * hd
    pairs = HEADS // 2
    return pl.pallas_call(
        functools.partial(attend_back_kernel, min(256, count), count == length, hd, hd**-0.5),
        grid=(pairs,),
        in_specs=[
            blocks_of(count, lanes, 0),
            blocks_of(length, lanes, offsets[0]),
            blocks_of(length, lanes, offsets[1]),
            blocks_of(count, lanes, 0),
            pl.BlockSpec((1, 2, count), lambda pair: (pair, 0, 0)),
            fixed((1, count)),
            fixed((length, 1)),
            fixed((1, count)),
        ],
        out_specs=[
            blocks_of(count, lanes, 0),
            blocks_of(length, lanes, 0),
            blocks_of(length, lanes, 0),
        ],
        out_shape=[
            jax.ShapeDtypeStruct((count, width), BF16),
            jax.ShapeDtypeStruct((length, width), kv_type),
            jax.ShapeDtypeStruct((length, width), kv_type),
        ],
        scratch_shapes=[pltpu.VMEM((length, lanes), F32)] * 2 + [pltpu.VMEM((length, count), F32)],
        compiler_params=kernel_params(),
    )(qkv, keys, values, dout, lse, seg_q, seg_k, pos_q)


def attend_back_deep(qkv, dout, lse, seg_q, aux, mixed, ddown, hidden, dupper, chunks):
    count, width = mixed.shape
    hd = width // HEADS
    lanes, pairs, parts = 2 * hd, HEADS // 2, hidden.shape[1] // width
    r = width // (2 * X * Z)
    pair = lambda offset: pl.BlockSpec(
        (count, lanes), lambda i: (0, offset + jnp.maximum(i - parts, 0))
    )
    column = pl.BlockSpec((count, width), lambda i: (0, jnp.minimum(i, parts - 1)))
    once = lambda shape: pl.BlockSpec(shape, lambda i: (0, 0), pipeline_mode=pl.Buffered(1))
    heads = jax.ShapeDtypeStruct((count, width), BF16)
    total = jax.ShapeDtypeStruct((2 * r, hidden.shape[1]), F32)
    ns = PER * len(chunks)
    return pl.pallas_call(
        functools.partial(attend_back_deep_kernel, parts, (256, True, hd, hd**-0.5), chunks),
        grid=(parts + pairs,),
        in_specs=[
            once((count, width)),
            once((count, width)),
            column,
            column,
            pair(0),
            pair(pairs),
            pair(2 * pairs),
            pair(0),
            pl.BlockSpec((1, 2, count), lambda i: (jnp.maximum(i - parts, 0), 0, 0)),
            once((1, count)),
            once((count, 128)),
        ],
        out_specs=[pair(0), pair(0), pair(0), once((8, 128))]
        + [pl.BlockSpec(memory_space=pl.ANY)] * 2,
        out_shape=[heads, heads, heads, jax.ShapeDtypeStruct((8, 128), F32), total, total],
        scratch_shapes=[
            pltpu.VMEM((count, lanes), F32),
            pltpu.VMEM((count, lanes), F32),
            pltpu.VMEM((count, count), F32),
            pltpu.VMEM((Z, X, 2, r, hidden.shape[1]), BF16),
            pltpu.VMEM((Z, X, 2, r, hidden.shape[1]), BF16),
            pltpu.VMEM(total.shape, F32),
            pltpu.VMEM(total.shape, F32),
            pltpu.SemaphoreType.DMA((ns,)),
            pltpu.SemaphoreType.DMA((ns,)),
            pltpu.SemaphoreType.DMA((2,)),
        ]
        + [pltpu.VMEM(*b) for (t, lo, w, o) in chunks for b in shapes(r, w, o, BF16)],
        compiler_params=pltpu.CompilerParams(
            collective_id=3, has_side_effects=True, vmem_limit_bytes=60 * 2**20
        ),
    )(mixed, ddown, hidden, dupper, qkv, qkv, qkv, dout, lse, seg_q, aux)


def layer_norm(hidden, gain, shift):
    mean = jnp.mean(hidden, -1, keepdims=True)
    centred = hidden - mean
    var = jnp.mean(centred * centred, -1, keepdims=True)
    rstd = lax.rsqrt(var + NORM_EPS)
    unit = centred * rstd
    return (unit * gain + shift, unit, rstd)


def norm_back(grad, unit, rstd, gain):
    dunit = grad * gain
    dhid = rstd * (
        dunit
        - jnp.mean(dunit, -1, keepdims=True)
        - unit * jnp.mean(dunit * unit, -1, keepdims=True)
    )
    return (dhid, jnp.sum(grad * unit, 0), jnp.sum(grad, 0))


def adamw(weight, first, second, grad, rate, decay):
    new_first = BETA_ONE * first + (1.0 - BETA_ONE) * grad
    new_second = BETA_TWO * second + (1.0 - BETA_TWO) * grad * grad
    first_hat = new_first / (1.0 - BETA_ONE**STEP)
    second_hat = new_second / (1.0 - BETA_TWO**STEP)
    return (
        weight - rate * (first_hat / (jnp.sqrt(second_hat) + ADAM_EPS) + decay * weight),
        new_first,
        new_second,
    )


def norm_rows(hidden):
    mean = jnp.mean(hidden, -1, keepdims=True)
    centred = hidden - mean
    rstd = lax.rsqrt(jnp.mean(centred * centred, -1, keepdims=True) + NORM_EPS)
    return centred * rstd, rstd


def norm_rows_back(grad, unit, rstd, gain):
    dunit = grad * gain
    return rstd * (
        dunit
        - jnp.mean(dunit, -1, keepdims=True)
        - unit * jnp.mean(dunit * unit, -1, keepdims=True)
    )


def add_rows(ref, row, value):
    ref[row : row + 1, :] += jnp.sum(value, 0, keepdims=True)


GELU_A = math.sqrt(2.0 / math.pi)
GELU_B = 0.044715


def mlp_kernel(
    wide, o_ref, h0_ref, aux_ref, ws_ref, wa_far, wu_far, wd_far, wh_ref,
    do_ref, dh1_ref, dat_ref, m_ref, hid_ref, dd_ref, du_ref, ghead_ref, sums_ref, loss_ref,
    slope, gains_all, wa_ref, wu_ref, wd_ref, enter,
):
    step = pl.program_id(0)
    pairs = ((wa_far, wa_ref), (wu_far, wu_ref), (wd_far, wd_ref))
    bring = lambda i: pltpu.make_async_copy(*pairs[i], enter.at[i])

    def arrived(*which):
        @pl.when(step == 0)
        def _():
            for i in which:
                bring(i).wait()

    tile, width = h0_ref.shape
    blocks = [slice(j, j + wide) for j in range(0, wu_ref.shape[1], wide)]

    @pl.when(step == 0)
    def _():
        for i in range(len(pairs)):
            bring(i).start()
        gains_all[...] = gains_of(ws_ref)
        sums_ref[...] = jnp.zeros_like(sums_ref)
        loss_ref[...] = jnp.zeros_like(loss_ref)
        ghead_ref[...] = jnp.zeros_like(ghead_ref)

    gains = gains_all[...]
    o = o_ref[...]
    arrived(0)
    h1 = h0_ref[...] + dot(o, wa_ref[...]) + (gains[7:8] - 1.0)
    unit_two, rstd_two = norm_rows(h1)
    m = (unit_two * gains[2:3] + (gains[3:4] - 1.0)).astype(BF16)
    m_ref[...] = m
    h2 = h1
    arrived(1, 2)
    for b in blocks:
        u = dot(m, wu_ref[:, b])
        square = u * u
        cube = (GELU_A * GELU_B) * square
        one = 1.0 + jnp.tanh(u * (GELU_A + cube))
        half = 0.5 * u
        hid = (half * one).astype(BF16)
        slope[:, b] = one * (0.5 + half * (2.0 - one) * (GELU_A + 3.0 * cube))
        hid_ref[:, b] = hid
        h2 = h2 + dot(hid, wd_ref[:, b], NT)
    unit_fin, rstd_fin = norm_rows(h2)
    final = (unit_fin * gains[4:5] + (gains[5:6] - 1.0)).astype(BF16)
    out = dot(final, wh_ref[...])
    aux = aux_ref[...]
    lane = lax.broadcasted_iota(jnp.int32, out.shape, 1)
    used = lane < PATCH
    pair, first = aux[:, PAIR : PAIR + 1], aux[:, FIRST : FIRST + 1]
    alpha = jnp.where(used, pltpu.roll(out, 128 - PATCH, 1), 0.0)
    plain = jnp.where(used, pltpu.roll(aux, 128 - PATCH, 1), 0.0)
    shrink = jnp.exp(-alpha)
    scaled = jnp.where(used, aux - out, 0.0) * shrink
    term = pair * (0.5 * scaled * scaled + alpha) + first * (0.5 * plain * plain)
    loss_ref[...] += jnp.sum(term.reshape(tile // 8, 8, 128), 0)
    dmu = -pair * scaled * shrink
    dalpha = pltpu.roll(jnp.where(used, pair * (1.0 - scaled * scaled), 0.0), PATCH, 1)
    dout = jnp.where(used, dmu, dalpha).astype(BF16)
    ghead_ref[...] += dot(final, dout, TN)
    dfinal = dot(dout, wh_ref[...], NT)
    add_rows(sums_ref, 4, dfinal * unit_fin)
    add_rows(sums_ref, 5, dfinal)
    dh2 = norm_rows_back(dfinal, unit_fin, rstd_fin, gains[4:5])
    dd = dh2.astype(BF16)
    dd_ref[...] = dd
    dmixed = jnp.zeros((tile, width), F32)
    for b in blocks:
        du = (dot(dd, wd_ref[:, b]) * slope[:, b]).astype(BF16)
        du_ref[:, b] = du
        dmixed = dmixed + dot(du, wu_ref[:, b], NT)
    add_rows(sums_ref, 2, dmixed * unit_two)
    add_rows(sums_ref, 3, dmixed)
    dh1 = dh2 + norm_rows_back(dmixed, unit_two, rstd_two, gains[2:3])
    add_rows(sums_ref, 7, dh1)
    dh1_ref[...] = dh1
    dat = dh1.astype(BF16)
    dat_ref[...] = dat
    do_ref[...] = dot(dat, wa_ref[...], NT).astype(BF16)


def mlp(o, h0, aux, w_small, w_attn, w_up, w_down):
    count, width = h0.shape
    deep = w_up.shape[1]
    tile = min(256, count)
    row = lambda columns: pl.BlockSpec((tile, columns), lambda i: (i, 0))
    once = lambda shape: pl.BlockSpec(shape, lambda i: (0, 0), pipeline_mode=pl.Buffered(1))
    tall = lambda columns, dt: jax.ShapeDtypeStruct((count, columns), dt)
    return pl.pallas_call(
        functools.partial(mlp_kernel, width),
        grid=(count // tile,),
        in_specs=[
            row(width),
            row(width),
            row(128),
            pl.BlockSpec((width, 128), lambda i: (0, 1), pipeline_mode=pl.Buffered(1)),
            *[pl.BlockSpec(memory_space=pl.ANY)] * 3,
            once((width, 128)),
        ],
        out_specs=[
            row(width),
            row(width),
            row(width),
            row(width),
            row(deep),
            row(width),
            row(deep),
            once((width, 128)),
            once((8, width)),
            once((8, 128)),
        ],
        out_shape=[
            tall(width, BF16),
            tall(width, F32),
            tall(width, BF16),
            tall(width, BF16),
            tall(deep, BF16),
            tall(width, BF16),
            tall(deep, BF16),
            jax.ShapeDtypeStruct((width, 128), F32),
            jax.ShapeDtypeStruct((8, width), F32),
            jax.ShapeDtypeStruct((8, 128), F32),
        ],
        scratch_shapes=[
            pltpu.VMEM((tile, deep), F32),
            pltpu.VMEM((8, width), F32),
            *[pltpu.VMEM(v.shape, BF16) for v in (w_attn, w_up, w_down)],
            pltpu.SemaphoreType.DMA((3,)),
        ],
        compiler_params=pltpu.CompilerParams(vmem_limit_bytes=60 * 2**20),
    )(o, h0, aux, w_small, w_attn, w_up, w_down, w_small)


def back_kernel(
    tiles, chunks, h0_ref, dh1_ref, aux_ref, slots_ref, o_far, dat_far, normed_far, dq_far, dk_far,
    dv_far, wq_far, ws_ref, ghead_ref, sums_ref, squares_ref, loss_ref, count_ref, *refs,
):
    final, result, out, g = refs[:4], refs[4], refs[5:9], refs[9:13]
    tot, got, gains_all, vec, high, rest, send, recv, leave, enter = refs[13:23]
    near = refs[23:30]
    o_ref, dat_ref, normed_ref, dq_ref, dk_ref, dv_ref, wq_ref = near
    step = pl.program_id(0)
    R = reducers(chunks, g, out, refs[30:], send, recv)
    far = (o_far, dat_far, normed_far, dq_far, dk_far, dv_far, wq_far)
    bring = lambda i: pltpu.make_async_copy(far[i], near[i], enter.at[i])
    tile, width = h0_ref.shape
    place = lambda value: value.reshape(Z, X, 2, width // (2 * X * Z), value.shape[-1])

    def last(*group):
        for a in group:
            tot[0] += fold(a.stage4())

    def when(index, *stages):
        @pl.when(step == index)
        def _():
            for stage in stages:
                stage()

    def first():
        for i in range(len(far)):
            bring(i).start()
        greet(ALL)
        gains_all[...] = gains_of(ws_ref)
        vec[...] = sums_ref[...]
        tot[0] = squares_ref[...]
        tot[1] = loss_ref[...]
        tot[2] = count_ref[...]

    when(0, first)
    for j, d_ref in enumerate((dat_ref, dq_ref, dk_ref, dv_ref)):

        @pl.when(step == j)
        def _():
            for i in ((0, 1), (2, 3), (4,), (5,))[j]:
                bring(i).wait()
            if j:
                value = dot(normed_ref[...], d_ref[...], TN).astype(BF16)
                g[1][:, :, :, :, (j - 1) * width : j * width] = place(value)
            else:
                g[0][...] = place(dot(o_ref[...], d_ref[...], TN).astype(BF16))
            R[j].begin()
            if j:
                R[j - 1].stage1()

    when(4, R[3].stage1, bring(6).wait)
    when(6, R[0].stage2)
    when(8, R[1].stage2)

    @pl.when((step >= 4) & (step < 4 + tiles))
    def _():
        gains = gains_all[...]
        unit, rstd = norm_rows(h0_ref[...])
        rows = pl.ds(pl.multiple_of(jnp.clip(step - 4, 0, tiles - 1) * tile, tile), tile)
        dnormed = dot(dq_ref[rows, :], wq_ref[:, :width], NT)
        dnormed = dnormed + dot(dk_ref[rows, :], wq_ref[:, width : 2 * width], NT)
        dnormed = dnormed + dot(dv_ref[rows, :], wq_ref[:, 2 * width :], NT)
        add_rows(vec, 0, dnormed * unit)
        add_rows(vec, 1, dnormed)
        dh0 = dh1_ref[...] + norm_rows_back(dnormed, unit, rstd, gains[0:1])
        add_rows(vec, 6, dh0)
        top = dh0.astype(BF16)
        high[rows, :] = top
        rest[rows, :] = (dh0 - top.astype(F32)).astype(BF16)

    @pl.when(step == 4 + tiles)
    def _():
        slots = slots_ref[...]
        lookup = lookup_of(slots, g[2].shape[-1])
        top, low = high[...], rest[...]
        half = lookup.shape[1] // 2
        for j in range(2):
            cols = slice(j * half, (j + 1) * half)
            value = dot(top, lookup[:, cols], TN) + dot(low, lookup[:, cols], TN)
            g[2][:, :, :, :, cols] = place(value.astype(BF16))
            R[4 + j].begin()
        line = jnp.concatenate([vec[...], jnp.zeros((120, width), F32)], axis=0)
        both = dot(top, tokens_of(slots), TN) + line.T
        g[3][...] = place(jnp.concatenate([ghead_ref[...], both], axis=1))
        R[6].begin()
        for a in R[4:]:
            a.stage1()
        R[0].stage3()
        R[2].stage2()
        R[3].stage2()
        R[1].stage3()
        last(R[0], R[1])
        for a in R[4:]:
            a.stage2()
        R[2].stage3()
        R[3].stage3()
        R[0].stage5()
        R[1].stage5()
        for a in R[4:]:
            a.stage3()
        last(R[2], R[3])
        last(*R[4:])
        R[2].stage5()
        R[3].stage5()
        copies = [pltpu.make_async_copy(out[i], final[i], leave.at[i]) for i in range(4)]

        def between():
            for a in R[4:]:
                a.stage5()
            for a in R[:4]:
                a.finish()
            copies[0].start()
            copies[1].start()

        totals(tot, got, send, recv, PER * len(R), between)
        result[...] = tot[...]
        for a in R[4:]:
            a.finish()
        copies[2].start()
        copies[3].start()
        for c in copies:
            c.wait()


def back(h0, dh1, aux, normed, o, dat, dqkv, w_qkv, w_small, ghead, sums, squares, loss, held, chunks):
    count, width = h0.shape
    length = count
    r = width // (2 * X * Z)
    tile = 256
    tiles = count // tile
    once = lambda shape: pl.BlockSpec(
        shape, lambda i: (0,) * len(shape), pipeline_mode=pl.Buffered(1)
    )
    row = lambda columns: pl.BlockSpec((tile, columns), lambda i: (jnp.clip(i - 4, 0, tiles - 1), 0))
    types = (BF16, BF16, BF16, F32)
    widths = (width, 3 * width, length, 256)
    ns = PER * len(chunks) + 12
    outs = [jax.ShapeDtypeStruct((2 * r, w), F32) for w in widths]
    totals_of = jax.ShapeDtypeStruct((3, 8, 128), F32)
    far = (o, dat, normed, *dqkv, w_qkv)
    return pl.pallas_call(
        functools.partial(back_kernel, tiles, chunks),
        grid=(5 + tiles,),
        in_specs=[
            row(width),
            row(width),
            row(128),
            once((count, 128)),
            *[pl.BlockSpec(memory_space=pl.ANY)] * len(far),
            pl.BlockSpec((width, 128), lambda i: (0, 1), pipeline_mode=pl.Buffered(1)),
            once((width, 128)),
            once((8, width)),
            *[once((8, 128))] * 3,
        ],
        out_specs=[pl.BlockSpec(memory_space=pl.ANY)] * 4 + [once((3, 8, 128))],
        out_shape=[*outs, totals_of],
        scratch_shapes=[pltpu.VMEM(o.shape, F32) for o in outs]
        + [pltpu.VMEM((Z, X, 2, r, w), t) for w, t in zip(widths, types)]
        + [
            pltpu.VMEM((3, 8, 128), F32),
            pltpu.VMEM((12, 3, 8, 128), F32),
            pltpu.VMEM((8, width), F32),
            pltpu.VMEM((8, width), F32),
            pltpu.VMEM((count, width), BF16),
            pltpu.VMEM((count, width), BF16),
            pltpu.SemaphoreType.DMA((ns,)),
            pltpu.SemaphoreType.DMA((ns,)),
            pltpu.SemaphoreType.DMA((4,)),
            pltpu.SemaphoreType.DMA((len(far),)),
            *[pltpu.VMEM(v.shape, v.dtype) for v in far],
        ]
        + [pltpu.VMEM(*b) for (t, lo, w, o) in chunks for b in shapes(r, w, o, types[t])],
        compiler_params=pltpu.CompilerParams(
            collective_id=2, has_side_effects=True, vmem_limit_bytes=60 * 2**20
        ),
    )(h0, dh1, aux, aux, *far, w_small, ghead, sums, squares, loss, held)


def adam_kernel(totals_ref, down, up, attn, wide, table, small_rows, small, *refs):
    sums = [jnp.sum(totals_ref[i], axis=(0, 1), keepdims=True) for i in range(3)]
    squares, total, valid = sums
    norm = jnp.sqrt(squares) / valid
    clip = jnp.minimum(1.0, CLIP_AT / (norm + 1e-06))
    scale = clip / valid
    state, outs = refs[:24], refs[24:48]
    for ref, value in zip(refs[48:], (total / math.log(2.0), valid, norm)):
        ref[...] = value

    def update(index, grad):
        rate, decay = (RATE, DECAY) if index < 7 else (VEC_RATE, 0.0)
        weight, first, second = [state[index + 8 * i][...] for i in range(3)]
        for i, value in enumerate(adamw(weight, first, second, grad * scale, rate, decay)):
            outs[index + 8 * i][...] = value

    @pl.when(pl.program_id(0) == 0)
    def _():
        both = small[:, 128:].T
        update(0, both[PATCH : 2 * PATCH, :])
        update(7, both[:8, :])

    update(1, table[...])
    update(2, wide[...])
    update(3, attn[...])
    update(4, up[...])
    update(5, down[...])
    update(6, small_rows[:, : state[6].shape[1]])


def adam(totals, sums, masters, firsts, seconds):
    down, up, attn, wide, table, small = sums
    cuts = 4
    whole = lambda a: pl.BlockSpec(a.shape, lambda i: (0,) * a.ndim)
    by_row = lambda a: pl.BlockSpec((a.shape[0] // cuts, a.shape[1]), lambda i: (i, 0))
    turn = lambda values: [v.T if i % 8 in (1, 5) else v for i, v in enumerate(values)]
    state = turn((*masters, *firsts, *seconds))
    specs = [whole(a) if i % 8 in (0, 7) else by_row(a) for i, a in enumerate(state)]
    outs = pl.pallas_call(
        adam_kernel,
        grid=(cuts,),
        in_specs=[
            whole(totals),
            by_row(down),
            by_row(up),
            by_row(attn),
            by_row(wide),
            by_row(table),
            by_row(small),
            whole(small),
            *specs,
        ],
        out_specs=[*specs, *[pl.BlockSpec((1, 1), lambda i: (0, 0))] * 3],
        out_shape=[jax.ShapeDtypeStruct(a.shape, F32) for a in state]
        + [jax.ShapeDtypeStruct((1, 1), F32)] * 3,
        compiler_params=pltpu.CompilerParams(vmem_limit_bytes=60 * 2**20),
    )(totals, down, up, attn, wide, table, small, small, *state)
    return (*[v.reshape(()) for v in outs[24:]], *turn(outs[:24]))


def body(*args):
    patches, segments = args[:2]
    masters, firsts, seconds = (args[2:10], args[10:18], args[18:26])
    embed_in, pos_table, attn_qkv, attn_out, mlp_up, mlp_down, head_out, vectors = masters
    ways = lines()
    n_seq = lax.axis_size("seq")
    seq_at = lax.axis_index("seq")
    micros, group = segments.shape[0], segments.shape[2]
    length = group * n_seq
    width = attn_qkv.shape[1] // 3

    share = max(1, n_seq // micros)
    count = length // share
    mine = seq_at // share
    patches = patches.reshape(micros, PATCH, group)
    segments = segments.reshape(micros, group)
    low = lambda value: value.astype(BF16)
    outs = head_out.shape[1]
    pad = lambda value, columns: jnp.pad(value, ((0, 0), (0, columns - value.shape[1])))
    small = jnp.concatenate(
        [pad(head_out, 128), pad(vectors.T, PATCH), pad(embed_in.T, 128 - PATCH)], axis=1
    )
    early = [attn_qkv, pos_table.T, small]
    late = [mlp_up, mlp_down.T, attn_out]
    aligned = (lax.axis_size("dp"), n_seq, micros) == (X * Z, 4, 4) and width % (32 * X * Z) == 0
    start = (seq_at % share) * count
    part = lambda value: lax.dynamic_slice_in_dim(value, start, count, 0)
    pos_q = (start + jnp.arange(count))[None, :].astype(jnp.int32)
    if aligned:
        aux, seg_q, count_of, h0, normed, qkv, attended, lse, w_qkv, w_small, w_up, w_down, w_attn = front(
            patches, segments, early, late, EARLY, LATE
        )
        dattended, dh1, dat, mixed, hidden, ddown, dupper, grad_head, grad_sums, total = mlp(
            attended, h0, aux, w_small, w_attn, w_up, w_down
        )
        dq, dk, dv, squares, down, up = attend_back_deep(
            qkv, dattended, lse, seg_q, aux, mixed, ddown, hidden, dupper, DEEP
        )
        attn, wide, table, small, part = back(
            h0, dh1, aux, normed, attended, dat, (dq, dk, dv), w_qkv, w_small, grad_head, grad_sums,
            squares, total, count_of, REST,
        )
        sums = (down, up, attn, wide, table, small)
        return adam(part, sums, masters, firsts, seconds)

    row = lax.all_gather(patches, "seq", axis=2, tiled=True)
    seg = lax.all_gather(segments, "seq", axis=1, tiled=True)
    row = lax.dynamic_index_in_dim(row, mine, 0, keepdims=False)
    seg = lax.dynamic_index_in_dim(seg, mine, 0, keepdims=False)
    w_qkv, w_pos, w_small, w_up, w_down, w_attn = [
        gather_rows(low(v), ways, False) for v in early + late
    ]
    gains = w_small[:, 128:136].astype(F32).T

    at = jnp.arange(length)
    begins = jnp.zeros((length,), jnp.int32)
    for image in range(5):
        before = (seg > 0) & (seg < image) if image else seg > 0
        begins = jnp.where(seg == image, jnp.sum(before.astype(jnp.int32)), begins)
    offset = part(at - begins)
    own = part(seg)
    later = jnp.concatenate([row[:, 1:], jnp.zeros((PATCH, 1), BF16)], axis=1)
    seg_next = part(jnp.concatenate([seg[1:], jnp.zeros((1,), jnp.int32)]))
    pair = (own == seg_next) & (own > 0)
    first = (own > 0) & (offset == 0)
    more = jnp.stack([pair, first, offset, own], axis=1).astype(F32)
    aux = pad(jnp.concatenate([part(later.T).astype(F32), part(row.T).astype(F32), more], axis=1), 128)
    valid = jnp.sum((own > 0).astype(jnp.int32)).astype(F32) * PATCH
    seg_q, seg_k = own[None, :].astype(F32), seg[:, None].astype(F32)
    lookup, tokens = lookup_of(aux, length), tokens_of(aux)

    h0 = dot(lookup, w_pos, NT) + dot(tokens, w_small[:, 128:], NT) + (gains[6] - 1.0)
    normed, unit_one, rstd_one = layer_norm(h0, gains[0], gains[1] - 1.0)
    normed = low(normed)
    qkv = low(dot(normed, w_qkv))
    keys, values, offsets = (qkv, qkv, (HEADS // 2, HEADS))
    if share > 1:
        near = [list(range(g, g + share)) for g in range(0, n_seq, share)]
        keys = lax.all_gather(qkv[:, width:], "seq", axis=0, tiled=True, axis_index_groups=near)
        values, offsets = (keys, (0, HEADS // 2))
    attended, lse = attend(qkv, keys, values, offsets, seg_q, seg_k, pos_q, width)
    dattended, dh1, dat, mixed, hidden, ddown, dupper, grad_head, grad_sums, total = mlp(
        attended, h0, aux, w_small, w_attn, w_up, w_down
    )
    grad_down, grad_up = dot(ddown, hidden, TN), dot(mixed, dupper, TN)
    grad_attn = dot(attended, dat, TN)
    dq, dk, dv = attend_back(
        qkv, keys, values, offsets, dattended, lse, seg_q, seg_k, pos_q, width,
        BF16 if share == 1 else F32,
    )
    if share > 1:
        dk, dv = (
            low(lax.psum_scatter(d, "seq", scatter_dimension=0, tiled=True, axis_index_groups=near))
            for d in (dk, dv)
        )
    dqkv = jnp.concatenate([dq, dk, dv], axis=1)
    grad_qkv = dot(normed, dqkv, TN)
    dnorm, gain_one, shift_one = norm_back(dot(dqkv, w_qkv, NT), unit_one, rstd_one, gains[0])
    dh0 = dh1 + dnorm
    high = low(dh0)
    grad_pos = dot(high, lookup, TN) + dot(low(dh0 - high.astype(F32)), lookup, TN)
    grad_vec = jnp.concatenate(
        [gain_one[None], shift_one[None], grad_sums[2:6], jnp.sum(dh0, 0)[None], grad_sums[7:]]
    )
    small = jnp.concatenate([grad_head, dot(high, tokens, TN) + pad(grad_vec.T, 128)], axis=1)
    grads = [grad_down, grad_up, grad_attn, grad_qkv, grad_pos, small]
    parts = [
        scatter_rows(g.astype(F32), ways, order, F32 if g is small else BF16)
        for g, order in zip(grads, ("xy", "yx") * 3)
    ]
    squares = sum(jnp.sum(p * p) for p in parts)
    squares, total, valid = lax.psum((squares, jnp.sum(total), valid), ("dp", "seq"))
    down, up, attn, wide, table, small = [gather_parts(p, ways) for p in parts]
    pieces = [
        small[:, 128 + PATCH : 128 + 2 * PATCH].T,
        table.T,
        wide,
        attn,
        up,
        down.T,
        small[:, :outs],
        small[:, 128:136].T,
    ]
    norm = jnp.sqrt(squares) / valid
    clip = jnp.minimum(1.0, CLIP_AT / (norm + 1e-06))
    results = [
        adamw(
            masters[i],
            firsts[i],
            seconds[i],
            pieces[i] / valid * clip,
            RATE if i < 7 else VEC_RATE,
            DECAY if i < 7 else 0.0,
        )
        for i in range(8)
    ]
    return (
        total / math.log(2.0),
        valid,
        norm,
        *[r[0] for r in results],
        *[r[1] for r in results],
        *[r[2] for r in results],
    )


def solution(mesh):
    rows, columns = (P("dp", None), P(None, "dp"))
    weights = (columns, columns, rows, rows, rows, columns, rows, columns)
    in_specs = (P(None, "dp", None, "seq"), P(None, "dp", "seq")) + weights * 3
    out_specs = (P(), P(), P()) + weights * 3
    return jax.shard_map(body, mesh=mesh, in_specs=in_specs, out_specs=out_specs, check_vma=False)
```
